32 devices in a mesh: wide: 8 (over z, core), blk: 4 (over y, x).
Axes of the slice: x: 2, y: 2, z: 4, core: 2. Of those that a mesh axis runs over, the one named last changes fastest.
Arguments:
- query_emb: bfloat16 [128, 4096], P(('wide', 'blk')), may hold values from -0.1875 to 0.1875
- passage_emb: bfloat16 [128, 4096], P(('wide', 'blk')), may hold values from -0.1875 to 0.1875
- row_lse: float32 [128], P('wide'), may hold values from 2.5 to 4.5
- positive: int32 [128], P('wide'), may hold values from 0 to 15
- token_lengths: int32 [8, 16], P('wide'), may hold values from 1 to 16, 192 in all within a row
- destination: int32 [1536, 1], P('wide'), may hold values from 0 to 7; in each aligned block of 192 rows (0 to 191, 192 to 383, ...) at most 36 rows name the same one
- mlp_act: bfloat16 [1536, 12288], P('wide', 'blk'), may hold values from -6 to 6
- resid: bfloat16 [1536, 4096], P('wide', 'blk'), may hold values from -6 to 6
- w_down: bfloat16 [12288, 4096], P('blk'), may hold values from -0.054126588 to 0.054126588
- gain: float32 [4096], P('blk'), may hold values from 0.1 to 1.9
Outputs:
- query_grad: bfloat16 [128, 4096], P(('wide', 'blk'))
- resid_grad: bfloat16 [2304, 4096], P('wide', 'blk')
- act_grad: bfloat16 [2304, 12288], P('wide', 'blk')
- normed_out: bfloat16 [2304, 4096], P('wide', 'blk')
The draws below stay inside these ranges and needn't reach their ends.
Inputs may be any that keep to these rules, and one draw needn't show every extreme that they name: `token_lengths`: each row lists the token counts of the group's 16 passages in order and sums to 192. Among the token rows of one group, at most 36 name the same destination.
All inputs are finite; a program needn't handle non-finite values.
Results may differ from the reference program's by a relative error of at most 0.02.
Values may be sent and summed in bfloat16 or wider, within the bound.
No kernel may reach another device: no remote copies, remote signals or barrier semaphores. Data moves between devices by JAX's collectives and lax.ppermute only.
A program may use at most 64 MiB of HBM per device.

```python
import math
import jax
import jax.numpy as jnp
import numpy as np
from jax import lax

D = 4096
FF = 12288
TOK_DEV = 192
LMAX = 16
NPG = 16
HB = 1024
FB = 3072
SLOT = 36
RECV = 288
ROWS = 128
TOKENS = 1536
OUTROWS = 2304
N_WIDE = 8
N_BLK = 4


def shared_direction(key):
    return jnp.clip(jax.random.normal(jax.random.fold_in(key, 7001), (D,), jnp.float32), -3.0, 3.0)


def unit_signs(key, count):
    picks = jax.random.randint(key, (count,), 0, 2)
    return (2 * picks - 1).astype(jnp.float32)


def hidden_signs(key):
    return unit_signs(jax.random.fold_in(key, 7002), FF)


def draw_w_down(key, part):
    limit = 6.0 * FF ** (-0.5)
    base_key = jax.random.fold_in(key, 7003)
    base = jax.random.normal(base_key, (FF, D), jnp.float32)
    common = 2.5 / FF * hidden_signs(key)[:, None] * shared_direction(key)[None, :]
    values = base * FF ** (-0.5) + common
    return jnp.clip(values, -limit, limit).astype(jnp.bfloat16)


def draw_mlp_act(key, part):
    noise_key = jax.random.fold_in(key, 7004)
    size_key = jax.random.fold_in(key, 7005)
    sign_key = jax.random.fold_in(key, 7006)
    noise = jax.random.normal(noise_key, (TOKENS, FF), jnp.float32)
    magnitude = jax.random.uniform(size_key, (TOKENS,), jnp.float32, 0.6, 1.4)
    token_level = magnitude * unit_signs(sign_key, TOKENS)
    values = 0.8 * noise + 0.6 * token_level[:, None] * hidden_signs(key)[None, :]
    return jnp.clip(values, -6.0, 6.0).astype(jnp.bfloat16)


def draw_query_emb(key, part):
    noise_key = jax.random.fold_in(key, 7007)
    size_key = jax.random.fold_in(key, 7008)
    sign_key = jax.random.fold_in(key, 7009)
    noise = jax.random.normal(noise_key, (ROWS, D), jnp.float32)
    magnitude = jax.random.uniform(size_key, (ROWS,), jnp.float32, 0.6, 1.4)
    row_level = magnitude * unit_signs(sign_key, ROWS)
    values = 0.8 * noise + 0.6 * row_level[:, None] * shared_direction(key)[None, :]
    return (0.03125 * jnp.clip(values, -6.0, 6.0)).astype(jnp.bfloat16)


def with_ends(entries, own_key, low, top_value):
    place = [jax.random.randint(jax.random.fold_in(own_key, axis), (), 0, length) for axis, length in enumerate(entries.shape)]
    longest = entries.shape.index(max(entries.shape))
    neighbour = place[:longest] + [(place[longest] + 1) % entries.shape[longest]] + place[longest + 1:]
    return entries.at[tuple(place)].set(low).at[tuple(neighbour)].set(top_value)


def shard_levels(stream_key, shape, pieces, smallest, high):
    def one(axis_at, blocks):
        heights = jax.random.uniform(jax.random.fold_in(jax.random.fold_in(stream_key, 6), axis_at), (blocks,), jnp.float32, smallest / len(pieces), high / len(pieces))
        return jnp.repeat(jnp.exp(heights), shape[axis_at] // blocks).reshape((-1,) + (1,) * (len(shape) - axis_at - 1))

    level = one(*pieces[0])
    for cut in pieces[1:]:
        level = level * one(*cut)
    return level


def split_up(count, total, most, skew):
    portions = [(1 << 20) // math.isqrt(rank ** skew) + 1 for rank in range(2, count + 1)]
    surplus, given = total - most - (count - 1), [1] * (count - 1)
    while surplus > 0:
        movable = [i for i in range(count - 1) if given[i] < most]
        pool, left = sum([portions[i] for i in movable]), surplus
        for i in movable:
            more = min(most - given[i], max(1, left * portions[i] // pool), surplus)
            given[i] = given[i] + more
            surplus = surplus - more
    return np.array([most] + given)


def ragged_sizes(stream_key, number_of, total, most, slope):
    if number_of == 2:
        one = jax.random.randint(stream_key, (), max(1, total - most), min(most, total - 1) + 1)
        return jnp.stack([one, total - one])
    tallies = jnp.asarray(split_up(number_of, total, most, slope), jnp.int32)
    twos = (number_of - 1) // 2
    donor, sink = tallies[1:1 + 2 * twos:2], tallies[2:2 + 2 * twos:2]
    room = jnp.minimum(donor - 1, most - sink)
    moved = jax.random.randint(jax.random.fold_in(stream_key, 1), (twos,), 0, 1 << 20) % (room + 1)
    tallies = tallies.at[1:1 + 2 * twos:2].set(donor - moved).at[2:2 + 2 * twos:2].set(sink + moved)
    return tallies[jax.random.permutation(jax.random.fold_in(stream_key, 2), number_of)]


def routed_block(own_key, own, number, rows, number_of, top, bound, slope):
    ranking = jax.random.permutation(own_key, number_of)
    packed, usual = portions_of(number_of, rows * top, bound, slope, True), portions_of(number_of, rows * top, bound, slope, False)
    places = jnp.arange(number_of)

    def named(sizes, rotation):
        used = int((sizes > 0).sum())
        fixed = max(1, used // 4)
        moved = fixed + (places - fixed + rotation * (used - fixed)) % max(1, number_of - fixed)
        return jnp.zeros((number_of,), jnp.int32).at[ranking[jnp.where(places < fixed, places, moved)]].set(jnp.asarray(sizes, jnp.int32))

    sizes = jnp.where(number % 4 == 0, named(packed, number // 4), named(usual, number - number // 4 - 1))
    mixed = jax.random.permutation(jax.random.fold_in(own, 3), number_of)
    donor, receiver = mixed[0:number_of // 2 * 2:2], mixed[1:number_of // 2 * 2:2]
    room = jnp.minimum(sizes[donor] - 1, bound - sizes[receiver]) // 2
    room = jnp.where((donor == ranking[0]) | (receiver == ranking[0]) | (sizes[receiver] == 0), 0, jnp.maximum(room, 0))
    moved = jax.random.randint(jax.random.fold_in(own, 4), (number_of // 2,), 0, 1 << 20) % (room + 1)
    sizes = sizes.at[donor].add(-moved).at[receiver].add(moved)
    members = jnp.searchsorted(jnp.cumsum(sizes), jnp.arange(rows * top), side="right").astype(jnp.int32)
    grid = members.reshape(top, rows).T
    grid = grid[jax.random.permutation(jax.random.fold_in(own, 1), rows)]
    rotation = jax.random.randint(jax.random.fold_in(own, 2), (rows, 1), 0, top)
    return jnp.take_along_axis(grid, (jnp.arange(top)[None, :] + rotation) % top, axis=1)


def portions_of(number_of, total, reach, slope, full):
    portions = [(1 << 20) // math.isqrt(rank ** slope) + 1 for rank in range(1, number_of + 1)]
    largest = reach if full else min(reach, max(-(-total // number_of), total * portions[0] // sum(portions)))
    least = 1 if total - largest >= number_of - 1 else 0
    counts, rest = [largest] + [least] * (number_of - 1), total - largest - least * (number_of - 1)
    while rest > 0:
        candidates = [i for i in range(1, number_of) if counts[i] < largest] or [i for i in range(1, number_of) if counts[i] < reach]
        mass, remaining = sum([portions[i] for i in candidates]), rest
        for i in candidates:
            extra = min(reach - counts[i], max(1, remaining * portions[i] // mass), rest)
            counts[i] = counts[i] + extra
            rest = rest - extra
    return np.array(counts)


def normal_values(stream_key, extent, spread, most, split=(), kind=jnp.bfloat16):
    entries = spread * jax.random.normal(stream_key, extent, jnp.float32)
    if split:
        entries = entries * shard_levels(stream_key, extent, split, -0.22, 0.18)
    return jnp.clip(entries, -most, most).astype(kind)


def setup_inputs(seed: int = 0) -> dict:
    streams_of = jax.random.split(jax.random.key(seed), 11)
    query_emb = draw_query_emb(jax.random.fold_in(streams_of[10], 71), 0)
    passage_emb = normal_values(streams_of[1], (ROWS, D), 0.03125, 0.1875, ((0, 32),))
    row_lse = jnp.clip(2.5 + 2.0 * jax.random.uniform(streams_of[2], (ROWS,), jnp.float32) ** shard_levels(streams_of[2], (ROWS,), ((0, 8),), -0.2, 0.2), 2.5, 4.5)
    positive = with_ends(jax.random.randint(streams_of[3], (ROWS,), 0, NPG), jax.random.fold_in(streams_of[3], 1), 0, NPG - 1).astype(jnp.int32)
    token_lengths = jax.vmap(lambda own: ragged_sizes(own, NPG, TOK_DEV, LMAX, 2))(jax.random.split(streams_of[4], N_WIDE)).reshape((N_WIDE, NPG)).astype(jnp.int32)
    destination_keys = jax.random.split(jax.random.fold_in(streams_of[5], 1), TOKENS // TOK_DEV)
    destination_turns = jax.random.permutation(jax.random.fold_in(streams_of[5], 3), TOKENS // TOK_DEV)
    destination = jax.vmap(lambda own, number: routed_block(jax.random.fold_in(streams_of[5], 2), own, number, TOK_DEV, N_WIDE, 1, SLOT, 2))(destination_keys, destination_turns).reshape((TOKENS, 1))
    mlp_act = draw_mlp_act(jax.random.fold_in(streams_of[10], 71), 0)
    resid = normal_values(streams_of[7], (TOKENS, D), 1.0, 6.0, ((0, 8), (1, 4)))
    w_down = draw_w_down(jax.random.fold_in(streams_of[10], 71), 0)
    gain = jnp.clip(1.0 + 0.18 * jax.random.normal(streams_of[9], (D,), jnp.float32), 0.1, 1.9)
    return {"query_emb": query_emb, "passage_emb": passage_emb, "row_lse": row_lse, "positive": positive, "token_lengths": token_lengths, "destination": destination, "mlp_act": mlp_act, "resid": resid, "w_down": w_down, "gain": gain}


logit_scale = 24.0
norm_eps = 1e-06

def reference(query_emb, passage_emb, row_lse, positive, token_lengths, destination, mlp_act, resid, w_down, gain):
    queries = query_emb.reshape(N_WIDE, NPG, D).astype(jnp.float32)
    passages = passage_emb.reshape(N_WIDE, NPG, D).astype(jnp.float32)
    scores = logit_scale * jnp.einsum('gid,gjd->gij', queries, passages)
    lse_rows = row_lse.reshape(N_WIDE, NPG)
    pos_rows = positive.reshape(N_WIDE, NPG)
    columns = jnp.arange(NPG, dtype=jnp.int32)
    target = (pos_rows[:, :, None] == columns[None, None, :]).astype(jnp.float32)
    coef_half = lax.optimization_barrier((jnp.exp(scores - lse_rows[:, :, None]) - target).astype(jnp.bfloat16))
    coef_wide = coef_half.astype(jnp.float32)
    query_grad = (logit_scale * jnp.einsum('gij,gjd->gid', coef_wide, passages)).astype(jnp.bfloat16).reshape(ROWS, D)
    pass_grad = logit_scale * jnp.einsum('gij,gid->gjd', coef_wide, queries)
    lengths = token_lengths.astype(jnp.int32)
    starts = jnp.cumsum(lengths, axis=1) - lengths
    positions = jnp.arange(TOK_DEV, dtype=jnp.int32)
    member = (positions[None, :, None] >= starts[:, None, :]) & (positions[None, :, None] < (starts + lengths)[:, None, :])
    weights = member.astype(jnp.float32) * (1.0 / lengths.astype(jnp.float32))[:, None, :]
    tok_grad = jnp.einsum('gtj,gjd->gtd', weights, pass_grad, precision=lax.Precision.HIGHEST).astype(jnp.bfloat16)
    targets = destination.reshape(N_WIDE, TOK_DEV).astype(jnp.int32)
    dest_hot = (targets[:, :, None] == jnp.arange(N_WIDE, dtype=jnp.int32)[None, None, :]).astype(jnp.int32)
    rank_of = jnp.cumsum(dest_hot, axis=1) - dest_hot
    slot_of = lax.optimization_barrier(jnp.sum(rank_of * dest_hot, axis=2))
    groups = jnp.arange(N_WIDE, dtype=jnp.int32)[:, None]
    out_index = (targets * RECV + groups * SLOT + slot_of).reshape(-1)
    blocks = w_down.reshape(N_BLK, FB, D).astype(jnp.float32)
    picker = jnp.eye(N_BLK, dtype=jnp.float32)

    def layer(inputs):
        act_rows, resid_rows, grad_rows = inputs
        partial_terms = jnp.einsum('tcf,cfd->tcd', act_rows.reshape(TOK_DEV, N_BLK, FB).astype(jnp.float32), blocks)
        placed = jnp.einsum('tch,ce->tceh', resid_rows.reshape(TOK_DEV, N_BLK, HB).astype(jnp.float32), picker).reshape(TOK_DEV, N_BLK, D)
        rounded = lax.optimization_barrier((partial_terms + placed).astype(jnp.bfloat16))
        hidden = lax.optimization_barrier(jnp.sum(rounded.astype(jnp.float32), axis=1))
        inv_rms = lax.rsqrt(lax.optimization_barrier(jnp.mean(hidden * hidden, axis=1, keepdims=True)) + norm_eps)
        normed = (gain.astype(jnp.float32)[None, :] * hidden * inv_rms).astype(jnp.bfloat16)
        gained = gain.astype(jnp.float32)[None, :] * grad_rows.astype(jnp.float32)
        inner_sum = lax.optimization_barrier(jnp.sum(gained * hidden, axis=1, keepdims=True))
        resid_back = (inv_rms * gained - hidden * (inv_rms * inv_rms * inv_rms) * inner_sum / D).astype(jnp.bfloat16)
        act_back = jnp.dot(resid_back, w_down.T, preferred_element_type=jnp.float32).astype(jnp.bfloat16)
        return (resid_back, act_back, normed)
    resid_back, act_back, normed = lax.map(layer, (mlp_act.reshape(N_WIDE, TOK_DEV, FF), resid.reshape(N_WIDE, TOK_DEV, D), tok_grad))
    resid_grad = jnp.zeros((OUTROWS, D), jnp.bfloat16).at[out_index].set(resid_back.reshape(-1, D))
    act_grad = jnp.zeros((OUTROWS, FF), jnp.bfloat16).at[out_index].set(act_back.reshape(-1, FF))
    normed_out = jnp.zeros((OUTROWS, D), jnp.bfloat16).at[out_index].set(normed.reshape(-1, D))
    return (query_grad, resid_grad, act_grad, normed_out)
```

```python
import jax
import jax.numpy as jnp
from jax import lax
from jax.experimental import pallas as pl
from jax.experimental.pallas import tpu as pltpu
from jax.sharding import PartitionSpec as P

logit_scale = 24.0
norm_eps = 1e-06
f32 = jnp.float32
bf16 = jnp.bfloat16
kernel_vmem = 24 * 1024 * 1024


def tile_of(extent, most):
    tile = most
    while extent % tile:
        tile //= 2
    return tile


def swap(rows, axis, count, k):
    return lax.ppermute(rows, axis, [(i, i ^ k) for i in range(count)])


def project_body(group_ref, act_ref, w_ref, out_ref):
    out_ref[...] = jnp.dot(act_ref[...], w_ref[...], preferred_element_type=f32).astype(
        out_ref.dtype
    )


def project_own_body(group_ref, act_ref, w_ref, resid_ref, out_ref):
    out_ref[...] = jnp.dot(act_ref[...], w_ref[...], preferred_element_type=f32) + resid_ref[
        ...
    ].astype(f32)


def project(group, act, w_down, width, resid=None):
    rows, depth = act.shape
    tile = tile_of(width, 256)
    per_group = width // tile
    column_spec = pl.BlockSpec((rows, tile), lambda j, g: (0, j))
    in_specs = [
        pl.BlockSpec((rows, depth), lambda j, g: (0, 0)),
        pl.BlockSpec((depth, tile), lambda j, g: (0, g[0] * per_group + j)),
    ]
    operands = [act, w_down]
    if resid is not None:
        in_specs.append(column_spec)
        operands.append(resid)
    return pl.pallas_call(
        project_body if resid is None else project_own_body,
        grid_spec=pltpu.PrefetchScalarGridSpec(
            num_scalar_prefetch=1, grid=(per_group,), in_specs=in_specs, out_specs=column_spec
        ),
        out_shape=jax.ShapeDtypeStruct((rows, width), bf16 if resid is None else f32),
        compiler_params=pltpu.CompilerParams(vmem_limit_bytes=kernel_vmem),
        cost_estimate=pl.CostEstimate(
            flops=2 * rows * depth * width,
            bytes_accessed=2 * depth * width + 2 * rows * (depth + width),
            transcendentals=0,
        ),
    )(group, *operands)


def dot_t(left, right):
    return lax.dot_general(left, right, (((1,), (1,)), ((), ())), preferred_element_type=f32)


def back_first_body(group_ref, hid_ref, w_ref, out_ref):
    out_ref[...] = dot_t(hid_ref[...], w_ref[...])


def back_next_body(group_ref, hid_ref, w_ref, acc_ref, out_ref):
    out_ref[...] = acc_ref[...] + dot_t(hid_ref[...], w_ref[...])


def back(group, hid, w_down, acc=None):
    rows, width = hid.shape
    depth = w_down.shape[0]
    tile = tile_of(depth, 512)
    unit_spec = pl.BlockSpec((rows, tile), lambda j, g: (0, j))
    in_specs = [
        pl.BlockSpec((rows, width), lambda j, g: (0, 0)),
        pl.BlockSpec((tile, width), lambda j, g: (j, g[0])),
    ]
    operands = [hid, w_down]
    if acc is not None:
        in_specs.append(unit_spec)
        operands.append(acc)
    return pl.pallas_call(
        back_first_body if acc is None else back_next_body,
        grid_spec=pltpu.PrefetchScalarGridSpec(
            num_scalar_prefetch=1, grid=(depth // tile,), in_specs=in_specs, out_specs=unit_spec
        ),
        out_shape=jax.ShapeDtypeStruct((rows, depth), f32),
        compiler_params=pltpu.CompilerParams(vmem_limit_bytes=kernel_vmem),
        cost_estimate=pl.CostEstimate(
            flops=2 * rows * depth * width,
            bytes_accessed=2 * depth * width + 2 * rows * width + 8 * rows * depth,
            transcendentals=0,
        ),
    )(group, *operands)


def finish_body(features, *refs):
    (
        group_ref,
        hid_ref,
        w_ref,
        acc_ref,
        cross_ref,
        square_ref,
        hot_ref,
        share_ref,
        low_ref,
        low_act_ref,
        own_hid_ref,
        own_low_ref,
        gain_ref,
        act_out,
        resid_out,
        normed_out,
        lead,
        back_off,
    ) = refs

    @pl.when(pl.program_id(0) == 0)
    def _():
        hid = hid_ref[...]
        wide_hid = hid.astype(f32)
        squares = square_ref[...] + jnp.sum(wide_hid * wide_hid, axis=1, keepdims=True)
        cross = cross_ref[...] + dot_t(hid, low_ref[...])
        weights = hot_ref[...].astype(f32) * share_ref[...]
        inner = jnp.sum(cross * weights, axis=1, keepdims=True)
        inv_rms = lax.rsqrt(squares / features + norm_eps)
        lead[...] = inv_rms * jnp.sum(weights, axis=1, keepdims=True)
        back_off[...] = inv_rms * inv_rms * inv_rms * inner / features
        own = own_hid_ref[...].astype(f32)
        own_low = jnp.dot(hot_ref[...], own_low_ref[...], preferred_element_type=f32)
        resid_out[...] = (lead[...] * own_low - own * back_off[...]).astype(bf16)
        normed_out[...] = (gain_ref[...] * own * inv_rms).astype(bf16)

    low_act = jnp.dot(hot_ref[...], low_act_ref[...], preferred_element_type=f32)
    hid_act = acc_ref[...] + dot_t(hid_ref[...], w_ref[...])
    act_out[...] = (lead[...] * low_act - back_off[...] * hid_act).astype(bf16)


def finish(groups, hid, w_down, acc, cross, squares, hot, share, low, low_act, own_hid, gain):
    rows, width = hid.shape
    depth, features = w_down.shape
    pairs = hot.shape[1]
    tile = tile_of(depth, 512)

    def whole(shape):
        return pl.BlockSpec(shape, lambda j, g: (0, 0))

    def body(*refs):
        finish_body(features, *refs)

    return pl.pallas_call(
        body,
        grid_spec=pltpu.PrefetchScalarGridSpec(
            num_scalar_prefetch=1,
            grid=(depth // tile,),
            in_specs=[
                whole((rows, width)),
                pl.BlockSpec((tile, width), lambda j, g: (j, g[0])),
                pl.BlockSpec((rows, tile), lambda j, g: (0, j)),
                whole((rows, pairs)),
                whole((rows, 1)),
                whole((rows, pairs)),
                whole((1, pairs)),
                pl.BlockSpec((pairs, width), lambda j, g: (0, g[0])),
                pl.BlockSpec((pairs, tile), lambda j, g: (0, j)),
                whole((rows, width)),
                pl.BlockSpec((pairs, width), lambda j, g: (0, g[1])),
                whole((1, width)),
            ],
            out_specs=[
                pl.BlockSpec((rows, tile), lambda j, g: (0, j)),
                whole((rows, width)),
                whole((rows, width)),
            ],
            scratch_shapes=[pltpu.VMEM((rows, 1), f32), pltpu.VMEM((rows, 1), f32)],
        ),
        out_shape=[
            jax.ShapeDtypeStruct((rows, depth), bf16),
            jax.ShapeDtypeStruct((rows, width), bf16),
            jax.ShapeDtypeStruct((rows, width), bf16),
        ],
        compiler_params=pltpu.CompilerParams(vmem_limit_bytes=kernel_vmem),
        cost_estimate=pl.CostEstimate(
            flops=2 * rows * depth * width,
            bytes_accessed=2 * depth * width + 8 * rows * width + 6 * rows * depth,
            transcendentals=0,
        ),
    )(groups, hid, w_down, acc, cross, squares, hot, share, low, low_act, own_hid, low, gain)


def group_gradients(query_emb, passage_emb, row_lse, positive, gain, blk, blk_count):
    pair_rows = query_emb.shape[0]
    pairs = row_lse.shape[0]
    width = gain.shape[0]
    both = jnp.concatenate([query_emb, passage_emb], axis=0)
    parts = [both] + [swap(both, "blk", blk_count, k) for k in range(1, blk_count)]
    gains = [gain[None]] + [swap(gain[None], "blk", blk_count, k) for k in range(1, blk_count)]
    queries = jnp.concatenate([part[:pair_rows] for part in parts], axis=0)
    passages = jnp.concatenate([part[pair_rows:] for part in parts], axis=0)
    place = lax.iota(jnp.int32, pairs)
    named = (blk ^ (place // pair_rows)) * pair_rows + place % pair_rows
    reorder = named[:, None] == place[None, :]
    lse = jnp.sum(jnp.where(reorder, row_lse[None, :], 0.0), axis=1)
    target = jnp.sum(jnp.where(reorder, positive[None, :], 0), axis=1)
    scores = logit_scale * dot_t(queries, passages)
    hit = (target[:, None] == named[None, :]).astype(f32)
    coef = (jnp.exp(scores - lse[:, None]) - hit).astype(bf16)
    query_grad = (
        logit_scale * jnp.dot(coef[:pair_rows], passages, preferred_element_type=f32)
    ).astype(bf16)
    coef_named = jnp.dot(coef, reorder.astype(bf16), preferred_element_type=f32).astype(bf16)
    pass_grad = logit_scale * lax.dot_general(
        coef_named, queries, (((0,), (0,)), ((), ())), preferred_element_type=f32
    )
    stacked = jnp.concatenate(gains, axis=0)
    index = lax.iota(jnp.int32, blk_count)
    pick = (blk ^ index)[:, None, None] == index[None, :, None]
    whole_gain = jnp.sum(jnp.where(pick, stacked[None], 0.0), axis=1).reshape(1, blk_count * width)
    return query_grad, (whole_gain * pass_grad).astype(bf16)


def place_rows(destination, wide_count, slot_count):
    tok_count = destination.shape[0]
    dest_hot = (destination == lax.broadcasted_iota(jnp.int32, (tok_count, wide_count), 1)).astype(
        bf16
    )
    token = lax.iota(jnp.int32, tok_count)
    earlier = (token[None, :] < token[:, None]).astype(bf16)
    rank_of = jnp.dot(earlier, dest_hot, preferred_element_type=f32)
    slot_of = jnp.sum(rank_of * dest_hot.astype(f32), axis=1).astype(jnp.int32)
    slot_of = slot_of + destination[:, 0] * slot_count
    return (
        lax.broadcasted_iota(jnp.int32, (wide_count * slot_count, tok_count), 0) == slot_of[None, :]
    ).astype(bf16)


def slot_passages(dest_all, len_all, wide, slot_count):
    groups, tok_count = dest_all.shape
    per_group = len_all.shape[1]
    token = lax.iota(jnp.int32, tok_count)
    hit = dest_all == wide
    earlier = (token[:, None] < token[None, :]).astype(bf16)
    rank = jnp.dot(hit.astype(bf16), earlier, preferred_element_type=f32).astype(jnp.int32)
    order = lax.iota(jnp.int32, per_group)
    upto = (order[:, None] <= order[None, :]).astype(jnp.int32)
    ends = jnp.sum(len_all[:, :, None] * upto[None], axis=1)
    passage = jnp.sum((token[None, None, :] >= ends[:, :, None]).astype(jnp.int32), axis=1)
    code = jnp.where(hit, passage + 1, 0)
    slot = lax.iota(jnp.int32, slot_count)
    taken = jnp.sum(
        jnp.where(rank[:, None, :] == slot[None, :, None], code[:, None, :], 0), axis=2
    )
    column = lax.iota(jnp.int32, groups * per_group)
    group = lax.iota(jnp.int32, groups)
    hot = (column[None, None, :] // per_group == group[:, None, None]) & (
        column[None, None, :] % per_group + 1 == taken[:, :, None]
    )
    return hot.astype(bf16).reshape(groups * slot_count, groups * per_group)


def low_rank_shards(
    query_emb,
    passage_emb,
    row_lse,
    positive,
    token_lengths,
    destination,
    mlp_act,
    resid,
    w_down,
    gain,
):
    blk_count, wide_count = lax.axis_size("blk"), lax.axis_size("wide")
    blk, wide = lax.axis_index("blk"), lax.axis_index("wide")
    tok_count, width = resid.shape
    pairs = row_lse.shape[0]
    slot_count = 3 * tok_count // (2 * wide_count)

    query_grad, low_own = group_gradients(
        query_emb, passage_emb, row_lse, positive, gain, blk, blk_count
    )
    tables = jnp.concatenate([destination[:, 0], token_lengths[0]])
    tables = lax.all_gather(tables, "wide", axis=0)
    dest_all, len_all = tables[:, :tok_count], tables[:, tok_count:]
    low = lax.all_gather(low_own, "wide", axis=0, tiled=True)

    def group_index(k):
        return (blk ^ k)[None]

    far_first = [k for k in range(blk_count - 1, 0, -1)]
    arrived = {}
    for k in far_first:
        term = project(group_index(k), mlp_act, w_down, width)
        arrived[k] = swap(term, "blk", blk_count, k)
    hidden = project(group_index(0), mlp_act, w_down, width, resid)
    for k in far_first:
        hidden = hidden + arrived[k].astype(f32)

    placer = place_rows(destination, wide_count, slot_count)
    packed = jnp.dot(placer, hidden.astype(bf16), preferred_element_type=f32).astype(bf16)
    packed = packed.reshape(wide_count, slot_count, width)
    own_hid = lax.all_to_all(packed, "wide", split_axis=0, concat_axis=0, tiled=True).reshape(
        wide_count * slot_count, width
    )
    hids = [own_hid] + [swap(own_hid, "blk", blk_count, k) for k in range(1, blk_count)]

    low_act = dot_t(low, w_down).astype(bf16)
    hot = slot_passages(dest_all, len_all, wide, slot_count)
    share = (1.0 / len_all.astype(f32)).reshape(1, wide_count * pairs)

    acc, cross, squares = None, 0.0, 0.0
    for k in range(blk_count - 1):
        acc = back(group_index(k), hids[k], w_down, acc)
        low_part = lax.dynamic_slice_in_dim(low, (blk ^ k) * width, width, 1)
        cross = cross + dot_t(hids[k], low_part)
        wide_hid = hids[k].astype(f32)
        squares = squares + jnp.sum(wide_hid * wide_hid, axis=1, keepdims=True)
    last = blk_count - 1
    act_grad, resid_grad, normed_out = finish(
        jnp.stack([blk ^ last, blk]),
        hids[last],
        w_down,
        acc,
        cross,
        squares,
        hot,
        share,
        low,
        low_act,
        own_hid,
        gain[None],
    )
    return (query_grad, resid_grad, act_grad, normed_out)


def coefficients(scores, lse_part, pos_part):
    columns = lax.broadcasted_iota(jnp.int32, scores.shape, 1)
    target = (pos_part[:, None] == columns).astype(jnp.float32)
    return (jnp.exp(scores - lse_part[:, None]) - target).astype(jnp.bfloat16)


def row_shards(
    query_emb,
    passage_emb,
    row_lse,
    positive,
    token_lengths,
    destination,
    mlp_act,
    resid,
    w_down,
    gain,
):
    pair_rows = query_emb.shape[0]
    tok_count, feat_width = resid.shape
    features = w_down.shape[1]
    blk_index = lax.axis_index("blk")
    wide_count = lax.axis_size("wide")
    slot_count = 3 * tok_count // (2 * wide_count)
    offset = blk_index * feat_width
    query_all = lax.all_gather(query_emb, "blk", axis=0, tiled=True)
    passage_all = lax.all_gather(passage_emb, "blk", axis=0, tiled=True)
    scores = logit_scale * jnp.dot(query_all, passage_all.T, preferred_element_type=f32)
    coef_full = coefficients(scores, row_lse, positive)
    own_coef = lax.dynamic_slice_in_dim(coef_full, blk_index * pair_rows, pair_rows, 0)
    query_grad = (
        logit_scale * jnp.dot(own_coef, passage_all, preferred_element_type=f32)
    ).astype(bf16)
    query_cols = lax.dynamic_slice_in_dim(query_all, offset, feat_width, 1)
    grad_cols = logit_scale * lax.dot_general(
        query_cols, coef_full, (((0,), (0,)), ((), ())), preferred_element_type=f32
    )
    lengths_row = token_lengths[0]
    starts = jnp.cumsum(lengths_row) - lengths_row
    positions = lax.broadcasted_iota(jnp.int32, (tok_count, lengths_row.shape[0]), 0)
    member = (positions >= starts[None, :]) & (positions < (starts + lengths_row)[None, :])
    weights = member.astype(f32) * (1.0 / lengths_row.astype(f32))[None, :]
    tok_grad = lax.dot_general(
        weights,
        grad_cols,
        (((1,), (1,)), ((), ())),
        precision=lax.Precision.HIGHEST,
        preferred_element_type=f32,
    ).astype(bf16)
    terms = jnp.dot(mlp_act, w_down, preferred_element_type=f32)
    own = lax.dynamic_slice_in_dim(terms, offset, feat_width, 1) + resid.astype(f32)
    terms = lax.dynamic_update_slice_in_dim(terms, own, offset, 1)
    hidden = lax.psum_scatter(terms.astype(bf16), "blk", scatter_dimension=1, tiled=True)
    placer = place_rows(destination, wide_count, slot_count)
    payload = jnp.concatenate([hidden, tok_grad], axis=1)
    packed = jnp.dot(placer, payload, preferred_element_type=f32).astype(bf16)
    packed = packed.reshape(wide_count, slot_count, 2 * feat_width)
    rows = lax.all_to_all(packed, "wide", split_axis=0, concat_axis=0, tiled=True).reshape(
        wide_count * slot_count, 2 * feat_width
    )
    hidden = rows[:, :feat_width].astype(f32)
    gained = gain[None, :] * rows[:, feat_width:].astype(f32)
    squares, inner_sum = lax.psum(
        (jnp.sum(hidden * hidden, axis=1), jnp.sum(gained * hidden, axis=1)), "blk"
    )
    inv_rms = lax.rsqrt(squares / features + norm_eps)[:, None]
    normed = (gain[None, :] * hidden * inv_rms).astype(bf16)
    resid_back = (
        inv_rms * gained - hidden * (inv_rms * inv_rms * inv_rms) * inner_sum[:, None] / features
    ).astype(bf16)
    act_back = dot_t(lax.all_gather(resid_back, "blk", axis=1, tiled=True), w_down)
    return (query_grad, resid_back, act_back.astype(bf16), normed)


def solution(mesh):
    blk_count, wide_count = mesh.shape["blk"], mesh.shape["wide"]

    def shards(*operands):
        pairs, tok_count = operands[2].shape[0], operands[7].shape[0]
        low_rank = 2 * wide_count * pairs <= 3 * tok_count
        if low_rank and blk_count > 1 and blk_count & (blk_count - 1) == 0:
            return low_rank_shards(*operands)
        return row_shards(*operands)

    return jax.shard_map(
        shards,
        mesh=mesh,
        in_specs=(
            P(("wide", "blk"), None),
            P(("wide", "blk"), None),
            P("wide"),
            P("wide"),
            P("wide", None),
            P("wide", None),
            P("wide", "blk"),
            P("wide", "blk"),
            P("blk", None),
            P("blk"),
        ),
        out_specs=(P(("wide", "blk"), None), P("wide", "blk"), P("wide", "blk"), P("wide", "blk")),
        check_vma=False,
    )
```

```python
import jax
import jax.numpy as jnp
from jax import lax
from jax.experimental import pallas as pl
from jax.experimental.pallas import tpu as pltpu
from jax.sharding import PartitionSpec as P

logit_scale = 24.0
norm_eps = 1e-06
f32 = jnp.float32
bf16 = jnp.bfloat16
i32 = jnp.int32
lane = 128
kernel_vmem = 46 * 1024 * 1024


def params():
    return pltpu.CompilerParams(vmem_limit_bytes=kernel_vmem)


def cost(flops, nbytes):
    return pl.CostEstimate(flops=flops, bytes_accessed=nbytes, transcendentals=0)


def tile_of(extent, most):
    tile = most
    while extent % tile:
        tile //= 2
    return tile


def iota(shape, dim):
    return lax.broadcasted_iota(i32, shape, dim)


def dot(left, right):
    return jnp.dot(left, right, preferred_element_type=f32)


def dot_t(left, right):
    return lax.dot_general(left, right, (((1,), (1,)), ((), ())), preferred_element_type=f32)


def swap(rows, k):
    return lax.ppermute(rows, "blk", [(i, i ^ k) for i in range(lax.axis_size("blk"))])


def project_body(group_ref, act_ref, w_ref, out_ref):
    out_ref[...] = dot(act_ref[...], w_ref[...]).astype(bf16)


def project_own_body(group_ref, act_ref, w_ref, resid_ref, out_ref):
    out_ref[...] = dot(act_ref[...], w_ref[...]) + resid_ref[...].astype(f32)


def project(group, act, w_down, width, resid=None):
    rows, depth = act.shape
    tile = tile_of(width, 256)
    per_group = width // tile
    column_spec = pl.BlockSpec((rows, tile), lambda j, g: (0, j))
    in_specs = [
        pl.BlockSpec((rows, depth), lambda j, g: (0, 0)),
        pl.BlockSpec((depth, tile), lambda j, g: (0, g[0] * per_group + j)),
    ]
    operands = [act, w_down]
    if resid is not None:
        in_specs.append(column_spec)
        operands.append(resid)
    return pl.pallas_call(
        project_body if resid is None else project_own_body,
        grid_spec=pltpu.PrefetchScalarGridSpec(
            num_scalar_prefetch=1, grid=(per_group,), in_specs=in_specs, out_specs=column_spec
        ),
        out_shape=jax.ShapeDtypeStruct((rows, width), bf16 if resid is None else f32),
        compiler_params=params(),
        cost_estimate=cost(2 * rows * depth * width, 2 * depth * width + 2 * rows * depth),
    )(group, *operands)


def group_body(blk_ref, parts_ref, lse_row_ref, lse_ref, pos_row_ref, pos_ref, table_ref, *rest):
    query_grad_ref, low_ref, gain_ref = rest
    own, features = query_grad_ref.shape
    pairs = parts_ref.shape[0]
    blk = blk_ref[0]
    queries = parts_ref[:, :features]
    passages = parts_ref[:, features : 2 * features]

    def named(dim):
        place = iota((pairs, pairs), dim)
        return (blk ^ (place // own)) * own + place % own

    here_rows, here_cols = named(0), named(1)
    at_rows = here_rows == iota((pairs, pairs), 1)
    at_cols = here_cols == iota((pairs, pairs), 0)
    lse = jnp.sum(jnp.where(at_rows, lse_row_ref[...], 0.0), axis=1, keepdims=True)
    pos = jnp.sum(jnp.where(at_rows, pos_row_ref[...], 0), axis=1, keepdims=True)
    hit = (pos == here_cols).astype(f32)
    coef = (jnp.exp(logit_scale * dot_t(queries, passages) - lse) - hit).astype(bf16)
    query_grad_ref[...] = (logit_scale * dot(coef, passages))[:own].astype(bf16)
    lse = jnp.sum(jnp.where(at_cols, lse_ref[...], 0.0), axis=0, keepdims=True)
    pos = jnp.sum(jnp.where(at_cols, pos_ref[...], 0), axis=0, keepdims=True)
    hit = (pos == here_rows).astype(f32)
    turned = (jnp.exp(logit_scale * dot_t(passages, queries) - lse) - hit).astype(bf16)
    turned = dot(at_cols.astype(bf16), turned).astype(bf16)
    pass_grad = logit_scale * dot(turned, queries)
    piece = (parts_ref.shape[1] - 2 * features) // 2
    gains = (
        parts_ref[:, 2 * features : 2 * features + piece].astype(f32)
        + parts_ref[:, 2 * features + piece :].astype(f32)
    )
    for row in range(pairs):
        first = ((blk ^ (row // own)) * own + row % own) * piece
        gain_ref[:, pl.ds(pl.multiple_of(first, lane), piece)] = gains[row : row + 1]
    low_ref[:, :features] = (gain_ref[...] * pass_grad).astype(bf16)
    low_ref[:, features:] = table_ref[...]


def group_part(query_emb, passage_emb, row_lse, positive, token_lengths, destination, gain, blk):
    own, features = query_emb.shape
    pairs = row_lse.shape[0]
    high = gain.astype(bf16)
    rest = (gain - high.astype(f32)).astype(bf16)
    both = jnp.concatenate(
        [query_emb, passage_emb, high.reshape(own, -1), rest.reshape(own, -1)], axis=1
    )
    parts = jnp.concatenate([both] + [swap(both, k) for k in range(1, pairs // own)], axis=0)
    table = jnp.concatenate([destination.reshape(pairs, -1), token_lengths.reshape(pairs, 1)], 1)
    table = jnp.pad(table, ((0, 0), (0, lane - table.shape[1]))).astype(bf16)
    return pl.pallas_call(
        group_body,
        in_specs=[pl.BlockSpec(memory_space=pltpu.SMEM)]
        + [pl.BlockSpec(memory_space=pltpu.VMEM)] * 6,
        out_specs=[pl.BlockSpec(memory_space=pltpu.VMEM)] * 2,
        out_shape=[
            jax.ShapeDtypeStruct((own, features), bf16),
            jax.ShapeDtypeStruct((pairs, features + lane), bf16),
        ],
        scratch_shapes=[pltpu.VMEM((1, features), f32)],
        compiler_params=params(),
        cost_estimate=cost(8 * pairs * pairs * features, 8 * pairs * features),
    )(
        blk[None],
        parts,
        row_lse[None],
        row_lse[:, None],
        positive[None],
        positive[:, None],
        table,
    )


def earlier_of(tokens):
    return (iota((tokens, tokens), 0) < iota((tokens, tokens), 1)).astype(bf16)


def pack_body(dest_ref, own_ref, *rest):
    terms, out_ref = rest[:-1], rest[-1]
    groups, slots, _ = out_ref.shape
    tokens = dest_ref.shape[1]
    stride = -(-slots // 16) * 16
    hidden = own_ref[...]
    for term in terms:
        hidden = hidden + term[...].astype(f32)
    dest = dest_ref[...]
    hit = (dest == iota((groups, tokens), 0)).astype(f32)
    rank = dot(hit.astype(bf16), earlier_of(tokens))
    rank = jnp.sum(rank * hit, axis=0, keepdims=True).astype(i32)
    place = (iota((groups * stride, tokens), 0) == dest * stride + rank).astype(bf16)
    packed = dot(place, hidden.astype(bf16)).astype(bf16)
    for group in range(groups):
        out_ref[group] = packed[group * stride : group * stride + slots]


def pack(destination, own, terms, groups, slots):
    tokens, width = own.shape
    tile = tile_of(width, 512)
    column_spec = pl.BlockSpec((tokens, tile), lambda j: (0, j))
    return pl.pallas_call(
        pack_body,
        grid=(width // tile,),
        in_specs=[pl.BlockSpec((1, tokens), lambda j: (0, 0))] + [column_spec] * (1 + len(terms)),
        out_specs=pl.BlockSpec((groups, slots, tile), lambda j: (0, 0, j)),
        out_shape=jax.ShapeDtypeStruct((groups, slots, width), bf16),
        compiler_params=params(),
        cost_estimate=cost(4 * groups * slots * tokens * width, 10 * tokens * width),
    )(destination.reshape(1, tokens), own, *terms)


def slots_body(wide_ref, dest_ref, len_ref, hot_ref):
    groups, tokens = dest_ref.shape
    pairs = len_ref.shape[1]
    rows = hot_ref.shape[0]
    slots = rows // groups
    hit = dest_ref[...].astype(i32) == wide_ref[0]
    rank = dot(hit.astype(f32).astype(bf16), earlier_of(tokens))
    upto = (iota((pairs, pairs), 0) <= iota((pairs, pairs), 1)).astype(bf16)
    ends = dot(len_ref[...], upto)
    token = iota((groups, tokens), 1).astype(f32)
    passage = jnp.ones((groups, tokens), f32)
    for pair in range(pairs):
        passage = passage + (token >= ends[:, pair : pair + 1]).astype(f32)
    code = jnp.where(hit, passage, 0.0)
    spread = (iota((rows, groups), 0) // slots == iota((rows, groups), 1)).astype(bf16)
    rank_rows = dot(spread, rank.astype(bf16)).astype(i32)
    code_rows = dot(spread, code.astype(bf16))
    here = rank_rows == iota((rows, tokens), 0) % slots
    taken = jnp.sum(jnp.where(here, code_rows, 0.0), axis=1, keepdims=True).astype(i32)
    column = iota((rows, groups * pairs), 1)
    first = iota((rows, groups * pairs), 0) // slots * pairs
    hot = (taken > 0) & (column == first + taken - 1)
    hot_ref[...] = hot.astype(f32).astype(bf16)


def slot_passages(wide, dest_all, len_all, rows):
    groups, pairs = len_all.shape
    return pl.pallas_call(
        slots_body,
        in_specs=[pl.BlockSpec(memory_space=pltpu.SMEM)]
        + [pl.BlockSpec(memory_space=pltpu.VMEM)] * 2,
        out_specs=pl.BlockSpec(memory_space=pltpu.VMEM),
        out_shape=jax.ShapeDtypeStruct((rows, groups * pairs), bf16),
        compiler_params=params(),
        cost_estimate=cost(4 * rows * groups * dest_all.shape[1], 2 * rows * groups * pairs),
    )(wide[None], dest_all, len_all)


def low_act_body(low_ref, w_ref, out_ref):
    out_ref[...] = dot_t(low_ref[...], w_ref[...]).astype(bf16)


def low_activations(low, w_down):
    pairs = low.shape[0]
    depth, features = w_down.shape
    tile = tile_of(depth, 256)
    return pl.pallas_call(
        low_act_body,
        grid=(depth // tile,),
        in_specs=[
            pl.BlockSpec((pairs, features), lambda j: (0, 0)),
            pl.BlockSpec((tile, features), lambda j: (j, 0)),
        ],
        out_specs=pl.BlockSpec((pairs, tile), lambda j: (0, j)),
        out_shape=jax.ShapeDtypeStruct((pairs, depth), bf16),
        compiler_params=params(),
        cost_estimate=cost(2 * pairs * depth * features, 2 * depth * features),
    )(low, w_down)


def statistics(hids, lows):
    squares, cross = 0.0, 0.0
    for hid_ref, low_ref in zip(hids, lows):
        hid = hid_ref[...].astype(f32)
        squares = squares + jnp.sum(hid * hid, axis=1, keepdims=True)
        cross = cross + dot_t(hid_ref[...], low_ref[...])
    return squares, cross


def product(hids, weights):
    total = 0.0
    for hid_ref, w_ref in zip(hids, weights):
        total = total + dot_t(hid_ref[...], w_ref[...])
    return total


def piece_specs(pieces, low, tile):
    hid_specs, w_specs, low_specs = [], [], []
    for n, piece in enumerate(pieces):
        hid_specs.append(pl.BlockSpec(piece.shape, lambda j, g: (0, 0)))
        w_specs.append(pl.BlockSpec((tile, piece.shape[1]), lambda j, g, n=n: (j, g[n])))
        low_specs.append(
            pl.BlockSpec((low.shape[0], piece.shape[1]), lambda j, g, n=n: (0, g[n]))
        )
    return hid_specs + w_specs + low_specs


def back_body(count, *refs):
    hids, weights, lows = refs[1 : 1 + count], refs[1 + count : 1 + 2 * count], refs[1 + 2 * count :]
    lows, (acc_ref, squares_ref, cross_ref) = lows[:count], lows[count:]

    @pl.when(pl.program_id(0) == 0)
    def _():
        squares_ref[...], cross_ref[...] = statistics(hids, lows)

    acc_ref[...] = product(hids, weights)


def back(places, pieces, w_down, low):
    count = len(pieces)
    rows, width = pieces[0].shape
    depth = w_down.shape[0]
    pairs = low.shape[0]
    tile = tile_of(depth, 512)
    return pl.pallas_call(
        lambda *refs: back_body(count, *refs),
        grid_spec=pltpu.PrefetchScalarGridSpec(
            num_scalar_prefetch=1,
            grid=(depth // tile,),
            in_specs=piece_specs(pieces, low, tile),
            out_specs=[
                pl.BlockSpec((rows, tile), lambda j, g: (0, j)),
                pl.BlockSpec((rows, 1), lambda j, g: (0, 0)),
                pl.BlockSpec((rows, pairs), lambda j, g: (0, 0)),
            ],
        ),
        out_shape=[
            jax.ShapeDtypeStruct((rows, depth), f32),
            jax.ShapeDtypeStruct((rows, 1), f32),
            jax.ShapeDtypeStruct((rows, pairs), f32),
        ],
        compiler_params=params(),
        cost_estimate=cost(2 * rows * depth * width * count, 2 * depth * width * count),
    )(places, *pieces, *[w_down] * count, *[low] * count)


def finish_body(features, count, *refs):
    hids, weights, lows = refs[1 : 1 + count], refs[1 + count : 1 + 2 * count], refs[1 + 2 * count :]
    lows, rest = lows[:count], lows[count:]
    acc_ref, squares_ref, cross_ref, hot_ref, share_ref, low_act_ref, own_ref, own_low_ref = rest[:8]
    gain_ref, act_out, resid_out, normed_out, lead, pull = rest[8:]

    @pl.when(pl.program_id(0) == 0)
    def _():
        squares, cross = statistics(hids, lows)
        weight = hot_ref[...].astype(f32) * share_ref[...]
        inner = jnp.sum((cross_ref[...] + cross) * weight, axis=1, keepdims=True)
        inv_rms = lax.rsqrt((squares_ref[...] + squares) / features + norm_eps)
        lead[...] = inv_rms * jnp.sum(weight, axis=1, keepdims=True)
        pull[...] = inv_rms * inv_rms * inv_rms * inner / features
        own = own_ref[...].astype(f32)
        own_low = dot(hot_ref[...], own_low_ref[...])
        resid_out[...] = (lead[...] * own_low - own * pull[...]).astype(bf16)
        normed_out[...] = (gain_ref[...] * own * inv_rms).astype(bf16)

    low_act = dot(hot_ref[...], low_act_ref[...])
    hid_act = acc_ref[...] + product(hids, weights)
    act_out[...] = (lead[...] * low_act - pull[...] * hid_act).astype(bf16)


def finish(places, pieces, w_down, low, acc, squares, cross, hot, share, low_act, own, gain):
    count = len(pieces)
    rows, width = own.shape
    depth, features = w_down.shape
    pairs = hot.shape[1]
    tile = tile_of(depth, 512)

    def whole(shape):
        return pl.BlockSpec(shape, lambda j, g: (0, 0))

    return pl.pallas_call(
        lambda *refs: finish_body(features, count, *refs),
        grid_spec=pltpu.PrefetchScalarGridSpec(
            num_scalar_prefetch=1,
            grid=(depth // tile,),
            in_specs=piece_specs(pieces, low, tile)
            + [
                pl.BlockSpec((rows, tile), lambda j, g: (0, j)),
                whole((rows, 1)),
                whole((rows, pairs)),
                whole((rows, pairs)),
                whole((1, pairs)),
                pl.BlockSpec((pairs, tile), lambda j, g: (0, j)),
                whole((rows, width)),
                pl.BlockSpec((pairs, width), lambda j, g: (0, g[count])),
                whole((1, width)),
            ],
            out_specs=[
                pl.BlockSpec((rows, tile), lambda j, g: (0, j)),
                whole((rows, width)),
                whole((rows, width)),
            ],
            scratch_shapes=[pltpu.VMEM((rows, 1), f32), pltpu.VMEM((rows, 1), f32)],
        ),
        out_shape=[
            jax.ShapeDtypeStruct((rows, depth), bf16),
            jax.ShapeDtypeStruct((rows, width), bf16),
            jax.ShapeDtypeStruct((rows, width), bf16),
        ],
        compiler_params=params(),
        cost_estimate=cost(2 * rows * depth * width, 2 * depth * width + 6 * rows * depth),
    )(
        places,
        *pieces,
        *[w_down] * count,
        *[low] * count,
        acc,
        squares,
        cross,
        hot,
        share,
        low_act,
        own,
        low,
        gain,
    )


def low_rank_shards(
    query_emb,
    passage_emb,
    row_lse,
    positive,
    token_lengths,
    destination,
    mlp_act,
    resid,
    w_down,
    gain,
):
    wide_count = lax.axis_size("wide")
    blk, wide = lax.axis_index("blk"), lax.axis_index("wide")
    tok_count, width = resid.shape
    features = w_down.shape[1]
    pairs = row_lse.shape[0]
    slot_count = 3 * tok_count // (2 * wide_count)
    rows = wide_count * slot_count

    query_grad, low_own = group_part(
        query_emb, passage_emb, row_lse, positive, token_lengths, destination, gain, blk
    )
    arrived = []
    for k in (3, 1, 2):
        arrived.append(swap(project((blk ^ k)[None], mlp_act, w_down, width), k))
    own_term = project(blk[None], mlp_act, w_down, width, resid)

    low = lax.all_gather(low_own, "wide", axis=0, tiled=True)
    tables = low[:, features:]
    per_pair = tok_count // pairs
    dest_all = tables[:, :per_pair].reshape(wide_count, tok_count)
    len_all = tables[:, per_pair].reshape(wide_count, pairs)
    low = low[:, :features]

    packed = pack(destination, own_term, arrived, wide_count, slot_count)
    own_hid = lax.all_to_all(packed, "wide", split_axis=0, concat_axis=0, tiled=True)
    own_hid = own_hid.reshape(rows, width)

    low_act = low_activations(low, w_down)
    hot = slot_passages(wide, dest_all, len_all, rows)
    share = (1.0 / len_all.astype(f32)).reshape(1, wide_count * pairs)

    half = width // 2
    left, right = own_hid[:, :half], own_hid[:, half:]
    left_1, right_2 = swap(left, 1), swap(right, 2)
    right_1, left_2 = swap(right, 1), swap(left, 2)
    left_3, right_3 = swap(left_1, 2), swap(right_2, 1)

    def places(*pieces):
        return jnp.stack([(blk ^ k) * 2 + side for k, side in pieces])

    acc, squares, cross = back(
        places((0, 0), (0, 1), (1, 0), (1, 1), (2, 0), (2, 1)),
        [left, right, left_1, right_1, left_2, right_2],
        w_down,
        low,
    )
    act_grad, resid_grad, normed_out = finish(
        jnp.concatenate([places((3, 0), (3, 1)), blk[None]]),
        [left_3, right_3],
        w_down,
        low,
        acc,
        squares,
        cross,
        hot,
        share,
        low_act,
        own_hid,
        gain[None],
    )
    return (query_grad, resid_grad, act_grad, normed_out)


def coefficients(scores, lse_part, pos_part):
    columns = lax.broadcasted_iota(jnp.int32, scores.shape, 1)
    target = (pos_part[:, None] == columns).astype(jnp.float32)
    return (jnp.exp(scores - lse_part[:, None]) - target).astype(jnp.bfloat16)


def place_rows(destination, wide_count, slot_count):
    tok_count = destination.shape[0]
    dest_hot = (destination == lax.broadcasted_iota(jnp.int32, (tok_count, wide_count), 1)).astype(
        bf16
    )
    token = lax.iota(jnp.int32, tok_count)
    earlier = (token[None, :] < token[:, None]).astype(bf16)
    rank_of = jnp.dot(earlier, dest_hot, preferred_element_type=f32)
    slot_of = jnp.sum(rank_of * dest_hot.astype(f32), axis=1).astype(jnp.int32)
    slot_of = slot_of + destination[:, 0] * slot_count
    return (
        lax.broadcasted_iota(jnp.int32, (wide_count * slot_count, tok_count), 0) == slot_of[None, :]
    ).astype(bf16)


def row_shards(
    query_emb,
    passage_emb,
    row_lse,
    positive,
    token_lengths,
    destination,
    mlp_act,
    resid,
    w_down,
    gain,
):
    pair_rows = query_emb.shape[0]
    tok_count, feat_width = resid.shape
    features = w_down.shape[1]
    blk_index = lax.axis_index("blk")
    wide_count = lax.axis_size("wide")
    slot_count = 3 * tok_count // (2 * wide_count)
    offset = blk_index * feat_width
    query_all = lax.all_gather(query_emb, "blk", axis=0, tiled=True)
    passage_all = lax.all_gather(passage_emb, "blk", axis=0, tiled=True)
    scores = logit_scale * jnp.dot(query_all, passage_all.T, preferred_element_type=f32)
    coef_full = coefficients(scores, row_lse, positive)
    own_coef = lax.dynamic_slice_in_dim(coef_full, blk_index * pair_rows, pair_rows, 0)
    query_grad = (
        logit_scale * jnp.dot(own_coef, passage_all, preferred_element_type=f32)
    ).astype(bf16)
    query_cols = lax.dynamic_slice_in_dim(query_all, offset, feat_width, 1)
    grad_cols = logit_scale * lax.dot_general(
        query_cols, coef_full, (((0,), (0,)), ((), ())), preferred_element_type=f32
    )
    lengths_row = token_lengths[0]
    starts = jnp.cumsum(lengths_row) - lengths_row
    positions = lax.broadcasted_iota(jnp.int32, (tok_count, lengths_row.shape[0]), 0)
    member = (positions >= starts[None, :]) & (positions < (starts + lengths_row)[None, :])
    weights = member.astype(f32) * (1.0 / lengths_row.astype(f32))[None, :]
    tok_grad = lax.dot_general(
        weights,
        grad_cols,
        (((1,), (1,)), ((), ())),
        precision=lax.Precision.HIGHEST,
        preferred_element_type=f32,
    ).astype(bf16)
    terms = jnp.dot(mlp_act, w_down, preferred_element_type=f32)
    own = lax.dynamic_slice_in_dim(terms, offset, feat_width, 1) + resid.astype(f32)
    terms = lax.dynamic_update_slice_in_dim(terms, own, offset, 1)
    hidden = lax.psum_scatter(terms.astype(bf16), "blk", scatter_dimension=1, tiled=True)
    placer = place_rows(destination, wide_count, slot_count)
    payload = jnp.concatenate([hidden, tok_grad], axis=1)
    packed = jnp.dot(placer, payload, preferred_element_type=f32).astype(bf16)
    packed = packed.reshape(wide_count, slot_count, 2 * feat_width)
    rows = lax.all_to_all(packed, "wide", split_axis=0, concat_axis=0, tiled=True).reshape(
        wide_count * slot_count, 2 * feat_width
    )
    hidden = rows[:, :feat_width].astype(f32)
    gained = gain[None, :] * rows[:, feat_width:].astype(f32)
    squares, inner_sum = lax.psum(
        (jnp.sum(hidden * hidden, axis=1), jnp.sum(gained * hidden, axis=1)), "blk"
    )
    inv_rms = lax.rsqrt(squares / features + norm_eps)[:, None]
    normed = (gain[None, :] * hidden * inv_rms).astype(bf16)
    resid_back = (
        inv_rms * gained - hidden * (inv_rms * inv_rms * inv_rms) * inner_sum[:, None] / features
    ).astype(bf16)
    act_back = dot_t(lax.all_gather(resid_back, "blk", axis=1, tiled=True), w_down)
    return (query_grad, resid_back, act_back.astype(bf16), normed)


def solution(mesh):
    blk_count, wide_count = mesh.shape["blk"], mesh.shape["wide"]

    def shards(*operands):
        pairs, tok_count = operands[2].shape[0], operands[7].shape[0]
        low_rank = 2 * wide_count * pairs <= 3 * tok_count
        per_pair = tok_count // pairs
        aligned = operands[9].shape[0] % (lane * operands[0].shape[0]) == 0
        if low_rank and blk_count == 4 and aligned and per_pair * pairs == tok_count:
            return low_rank_shards(*operands)
        return row_shards(*operands)

    return jax.shard_map(
        shards,
        mesh=mesh,
        in_specs=(
            P(("wide", "blk"), None),
            P(("wide", "blk"), None),
            P("wide"),
            P("wide"),
            P("wide", None),
            P("wide", None),
            P("wide", "blk"),
            P("wide", "blk"),
            P("blk", None),
            P("blk"),
        ),
        out_specs=(P(("wide", "blk"), None), P("wide", "blk"), P("wide", "blk"), P("wide", "blk")),
        check_vma=False,
    )
```

```python
import jax
import jax.numpy as jnp
from jax import lax
from jax.experimental import pallas as pl
from jax.experimental.pallas import tpu as pltpu
from jax.sharding import PartitionSpec as P

logit_scale = 24.0
norm_eps = 1e-06
f32 = jnp.float32
bf16 = jnp.bfloat16
i32 = jnp.int32
lane = 128
kernel_vmem = 46 * 1024 * 1024


def params():
    return pltpu.CompilerParams(vmem_limit_bytes=kernel_vmem)


def cost(flops, nbytes):
    return pl.CostEstimate(flops=flops, bytes_accessed=nbytes, transcendentals=0)


def tile_of(extent, most):
    tile = most
    while extent % tile:
        tile //= 2
    return tile


def iota(shape, dim):
    return lax.broadcasted_iota(i32, shape, dim)


def dot(left, right):
    return jnp.dot(left, right, preferred_element_type=f32)


def dot_t(left, right):
    return lax.dot_general(left, right, (((1,), (1,)), ((), ())), preferred_element_type=f32)


def swap(rows, k, axis="blk"):
    return lax.ppermute(rows, axis, [(i, i ^ k) for i in range(lax.axis_size(axis))])


def after(first, *later):
    return lax.optimization_barrier((first, *later))


def project_step(act_ref, w_ref, total):
    @pl.when(pl.program_id(0) == 0)
    def _():
        total[...] = dot(act_ref[...], w_ref[...])

    @pl.when(pl.program_id(0) > 0)
    def _():
        total[...] += dot(act_ref[...], w_ref[...])


def project_body(group_ref, act_ref, w_ref, out_ref, total):
    project_step(act_ref, w_ref, total)

    @pl.when(pl.program_id(0) == pl.num_programs(0) - 1)
    def _():
        out_ref[...] = total[...].astype(bf16)


def project_own_body(group_ref, act_ref, w_ref, resid_ref, out_ref, total):
    project_step(act_ref, w_ref, total)

    @pl.when(pl.program_id(0) == pl.num_programs(0) - 1)
    def _():
        out_ref[...] = total[...] + resid_ref[...].astype(f32)


def project(group, act, w_down, width, resid=None):
    rows, depth = act.shape
    tile = tile_of(depth, 512)
    whole = pl.BlockSpec((rows, width), lambda j, g: (0, 0))
    in_specs = [
        pl.BlockSpec((rows, tile), lambda j, g: (0, j)),
        pl.BlockSpec((tile, width), lambda j, g: (j, g[0])),
    ]
    operands = [act, w_down]
    if resid is not None:
        in_specs.append(whole)
        operands.append(resid)
    return pl.pallas_call(
        project_body if resid is None else project_own_body,
        grid_spec=pltpu.PrefetchScalarGridSpec(
            num_scalar_prefetch=1,
            grid=(depth // tile,),
            in_specs=in_specs,
            out_specs=whole,
            scratch_shapes=[pltpu.VMEM((rows, width), f32)],
        ),
        out_shape=jax.ShapeDtypeStruct((rows, width), bf16 if resid is None else f32),
        compiler_params=params(),
        cost_estimate=cost(2 * rows * depth * width, 2 * depth * width + 2 * rows * depth),
    )(group, *operands)


def group_body(count, blk_ref, *refs):
    query_parts, passage_parts = refs[:count], refs[count : 2 * count]
    gain_parts, refs = refs[2 * count : 3 * count], refs[3 * count :]
    lse_row_ref, lse_ref, pos_row_ref, pos_ref, table_ref = refs[:5]
    query_grad_ref, low_ref, query_all, passage_all, gain_all = refs[5:]
    own, features = query_grad_ref.shape
    pairs = own * count
    width = features // count
    blk = blk_ref[0]
    for k in range(count):
        query_all[k * own : (k + 1) * own] = query_parts[k][...].astype(f32)
        passage_all[k * own : (k + 1) * own] = passage_parts[k][...].astype(f32)
        gain_all[:, pl.ds(pl.multiple_of((blk ^ k) * width, lane), width)] = gain_parts[k][...]
    queries = query_all[...].astype(bf16)
    passages = passage_all[...].astype(bf16)

    def named(dim):
        place = iota((pairs, pairs), dim)
        return (blk ^ (place // own)) * own + place % own

    here_rows, here_cols = named(0), named(1)
    at_rows = here_rows == iota((pairs, pairs), 1)
    at_cols = here_cols == iota((pairs, pairs), 0)
    lse = jnp.sum(jnp.where(at_rows, lse_row_ref[...], 0.0), axis=1, keepdims=True)
    pos = jnp.sum(jnp.where(at_rows, pos_row_ref[...], 0), axis=1, keepdims=True)
    hit = (pos == here_cols).astype(f32)
    coef = (jnp.exp(logit_scale * dot_t(queries, passages) - lse) - hit).astype(bf16)
    query_grad_ref[...] = (logit_scale * dot(coef, passages))[:own].astype(bf16)
    lse = jnp.sum(jnp.where(at_cols, lse_ref[...], 0.0), axis=0, keepdims=True)
    pos = jnp.sum(jnp.where(at_cols, pos_ref[...], 0), axis=0, keepdims=True)
    hit = (pos == here_rows).astype(f32)
    turned = (jnp.exp(logit_scale * dot_t(passages, queries) - lse) - hit).astype(bf16)
    turned = dot(at_cols.astype(bf16), turned).astype(bf16)
    pass_grad = logit_scale * dot(turned, queries)
    low_ref[:, :features] = (gain_all[...] * pass_grad).astype(bf16)
    low_ref[:, features:] = table_ref[...]


def group_part(parts, row_lse, positive, token_lengths, destination, blk):
    own, features = parts[0].shape
    pairs = row_lse.shape[0]
    table = jnp.concatenate([destination.reshape(pairs, -1), token_lengths.reshape(pairs, 1)], 1)
    table = jnp.pad(table, ((0, 0), (0, lane - table.shape[1]))).astype(bf16)
    return pl.pallas_call(
        lambda *refs: group_body(pairs // own, *refs),
        in_specs=[pl.BlockSpec(memory_space=pltpu.SMEM)]
        + [pl.BlockSpec(memory_space=pltpu.VMEM)] * (len(parts) + 5),
        out_specs=[pl.BlockSpec(memory_space=pltpu.VMEM)] * 2,
        out_shape=[
            jax.ShapeDtypeStruct((own, features), bf16),
            jax.ShapeDtypeStruct((pairs, features + lane), bf16),
        ],
        scratch_shapes=[
            pltpu.VMEM((pairs, features), f32),
            pltpu.VMEM((pairs, features), f32),
            pltpu.VMEM((1, features), f32),
        ],
        compiler_params=params(),
        cost_estimate=cost(8 * pairs * pairs * features, 8 * pairs * features),
    )(
        blk[None],
        *parts,
        row_lse[None],
        row_lse[:, None],
        positive[None],
        positive[:, None],
        table,
    )


def earlier_of(tokens):
    return (iota((tokens, tokens), 0) < iota((tokens, tokens), 1)).astype(bf16)


def pack_body(terms, wide_ref, dest_ref, own_ref, *rest):
    outs = rest[terms:]
    groups, slots = len(outs), outs[0].shape[0]
    tokens = dest_ref.shape[1]
    stride = -(-slots // 16) * 16
    hidden = own_ref[...]
    for term in rest[:terms]:
        hidden = hidden + term[...].astype(f32)
    partner = dest_ref[...] ^ wide_ref[0]
    hit = (partner == iota((groups, tokens), 0)).astype(f32)
    rank = dot(hit.astype(bf16), earlier_of(tokens))
    rank = jnp.sum(rank * hit, axis=0, keepdims=True).astype(i32)
    place = iota((groups * stride, tokens), 0) == partner * stride + rank
    packed = dot(place.astype(f32).astype(bf16), hidden.astype(bf16)).astype(bf16)
    for k in range(groups):
        outs[k][...] = packed[k * stride : k * stride + slots]


def pack(wide, destination, own, terms, groups, slots):
    tokens, width = own.shape
    tile = tile_of(width, 512)
    column_spec = pl.BlockSpec((tokens, tile), lambda j, g: (0, j))
    return pl.pallas_call(
        lambda *refs: pack_body(len(terms), *refs),
        grid_spec=pltpu.PrefetchScalarGridSpec(
            num_scalar_prefetch=1,
            grid=(width // tile,),
            in_specs=[pl.BlockSpec((1, tokens), lambda j, g: (0, 0))]
            + [column_spec] * (1 + len(terms)),
            out_specs=[pl.BlockSpec((slots, tile), lambda j, g: (0, j))] * groups,
        ),
        out_shape=[jax.ShapeDtypeStruct((slots, width), bf16)] * groups,
        compiler_params=params(),
        cost_estimate=cost(4 * groups * slots * tokens * width, 10 * tokens * width),
    )(wide[None], destination.reshape(1, tokens), own, *terms)


def assemble_body(wide_ref, *refs):
    parts, (left_ref, right_ref) = refs[:-2], refs[-2:]
    slots = parts[0].shape[0]
    rows, half = left_ref.shape
    row, column = iota((rows, slots), 0), iota((rows, slots), 1)
    total = 0.0
    for k, part in enumerate(parts):
        group = wide_ref[0] ^ k
        place = (row == group * slots + column).astype(f32).astype(bf16)
        total = total + dot(place, part[...])
    left_ref[...] = total[:, :half].astype(bf16)
    right_ref[...] = total[:, half:].astype(bf16)


def assemble(wide, parts):
    slots, width = parts[0].shape
    rows = slots * len(parts)
    return pl.pallas_call(
        assemble_body,
        in_specs=[pl.BlockSpec(memory_space=pltpu.SMEM)]
        + [pl.BlockSpec(memory_space=pltpu.VMEM)] * len(parts),
        out_specs=[pl.BlockSpec(memory_space=pltpu.VMEM)] * 2,
        out_shape=[jax.ShapeDtypeStruct((rows, width // 2), bf16)] * 2,
        compiler_params=params(),
        cost_estimate=cost(2 * rows * rows * width, 4 * rows * width),
    )(wide[None], *parts)


def slots_body(wide_ref, dest_ref, len_ref, hot_ref):
    groups, tokens = dest_ref.shape
    pairs = len_ref.shape[1]
    rows = hot_ref.shape[0]
    slots = rows // groups
    hit = dest_ref[...].astype(i32) == wide_ref[0]
    rank = dot(hit.astype(f32).astype(bf16), earlier_of(tokens))
    upto = (iota((pairs, pairs), 0) <= iota((pairs, pairs), 1)).astype(bf16)
    ends = dot(len_ref[...], upto)
    token = iota((groups, tokens), 1).astype(f32)
    passage = jnp.ones((groups, tokens), f32)
    for pair in range(pairs):
        passage = passage + (token >= ends[:, pair : pair + 1]).astype(f32)
    code = jnp.where(hit, passage, 0.0)
    spread = (iota((rows, groups), 0) // slots == iota((rows, groups), 1)).astype(bf16)
    rank_rows = dot(spread, rank.astype(bf16)).astype(i32)
    code_rows = dot(spread, code.astype(bf16))
    here = rank_rows == iota((rows, tokens), 0) % slots
    taken = jnp.sum(jnp.where(here, code_rows, 0.0), axis=1, keepdims=True).astype(i32)
    column = iota((rows, groups * pairs), 1)
    first = iota((rows, groups * pairs), 0) // slots * pairs
    hot = (taken > 0) & (column == first + taken - 1)
    hot_ref[...] = hot.astype(f32).astype(bf16)


def slot_passages(wide, dest_all, len_all, rows):
    groups, pairs = len_all.shape
    return pl.pallas_call(
        slots_body,
        in_specs=[pl.BlockSpec(memory_space=pltpu.SMEM)]
        + [pl.BlockSpec(memory_space=pltpu.VMEM)] * 2,
        out_specs=pl.BlockSpec(memory_space=pltpu.VMEM),
        out_shape=jax.ShapeDtypeStruct((rows, groups * pairs), bf16),
        compiler_params=params(),
        cost_estimate=cost(4 * rows * groups * dest_all.shape[1], 2 * rows * groups * pairs),
    )(wide[None], dest_all, len_all)


def low_act_body(low_ref, w_ref, out_ref):
    out_ref[...] = dot_t(w_ref[...], low_ref[...]).astype(bf16)


def low_activations(low, features, w_down):
    pairs = low.shape[0]
    depth = w_down.shape[0]
    tile = tile_of(depth, 256)
    return pl.pallas_call(
        low_act_body,
        grid=(depth // tile,),
        in_specs=[
            pl.BlockSpec((pairs, features), lambda j: (0, 0)),
            pl.BlockSpec((tile, features), lambda j: (j, 0)),
        ],
        out_specs=pl.BlockSpec((tile, pairs), lambda j: (j, 0)),
        out_shape=jax.ShapeDtypeStruct((depth, pairs), bf16),
        compiler_params=params(),
        cost_estimate=cost(2 * pairs * depth * features, 2 * depth * features),
    )(low, w_down)


def statistics(hids, lows):
    squares, cross = 0.0, 0.0
    for hid_ref, low_ref in zip(hids, lows):
        hid = hid_ref[...].astype(f32)
        squares = squares + jnp.sum(hid * hid, axis=1, keepdims=True)
        cross = cross + dot_t(hid_ref[...], low_ref[...])
    return squares, cross


def product(hids, weights):
    total = 0.0
    for hid_ref, w_ref in zip(hids, weights):
        total = total + dot_t(hid_ref[...], w_ref[...])
    return total


def piece_specs(pieces, low, tile):
    hid_specs, w_specs, low_specs = [], [], []
    for n, piece in enumerate(pieces):
        hid_specs.append(pl.BlockSpec(piece.shape, lambda j, g: (0, 0)))
        w_specs.append(pl.BlockSpec((tile, piece.shape[1]), lambda j, g, n=n: (j, g[n])))
        low_specs.append(
            pl.BlockSpec((low.shape[0], piece.shape[1]), lambda j, g, n=n: (0, g[n]))
        )
    return hid_specs + w_specs + low_specs


def back_body(count, carried, *refs):
    hids, weights, lows = refs[1 : 1 + count], refs[1 + count : 1 + 2 * count], refs[1 + 2 * count :]
    lows, refs = lows[:count], lows[count:]
    before, (acc_ref, squares_ref, cross_ref) = refs[:carried], refs[carried:]

    @pl.when(pl.program_id(0) == 0)
    def _():
        squares, cross = statistics(hids, lows)
        if carried:
            squares, cross = before[1][...] + squares, before[2][...] + cross
        squares_ref[...], cross_ref[...] = squares, cross

    total = product(hids, weights)
    acc_ref[...] = before[0][...] + total if carried else total


def carried_specs(rows, pairs, tile):
    return [
        pl.BlockSpec((rows, tile), lambda j, g: (0, j)),
        pl.BlockSpec((rows, 1), lambda j, g: (0, 0)),
        pl.BlockSpec((rows, pairs), lambda j, g: (0, 0)),
    ]


def back(places, pieces, w_down, low, before=()):
    count = len(pieces)
    rows, width = pieces[0].shape
    depth = w_down.shape[0]
    pairs = low.shape[0]
    tile = tile_of(depth, 512)
    totals = carried_specs(rows, pairs, tile)
    return pl.pallas_call(
        lambda *refs: back_body(count, len(before), *refs),
        grid_spec=pltpu.PrefetchScalarGridSpec(
            num_scalar_prefetch=1,
            grid=(depth // tile,),
            in_specs=piece_specs(pieces, low, tile) + totals[: len(before)],
            out_specs=totals,
        ),
        out_shape=[
            jax.ShapeDtypeStruct((rows, depth), f32),
            jax.ShapeDtypeStruct((rows, 1), f32),
            jax.ShapeDtypeStruct((rows, pairs), f32),
        ],
        compiler_params=params(),
        cost_estimate=cost(2 * rows * depth * width * count, 2 * depth * width * count),
    )(places, *pieces, *[w_down] * count, *[low] * count, *before)


def finish_body(features, count, *refs):
    hids, weights, lows = refs[1 : 1 + count], refs[1 + count : 1 + 2 * count], refs[1 + 2 * count :]
    lows, rest = lows[:count], lows[count:]
    acc_ref, squares_ref, cross_ref, hot_ref, share_ref, low_act_ref, left_ref, right_ref = rest[:8]
    own_low_ref, gain_ref, act_out, resid_out, normed_out, lead, pull = rest[8:]

    @pl.when(pl.program_id(0) == 0)
    def _():
        squares, cross = statistics(hids, lows)
        weight = hot_ref[...].astype(f32) * share_ref[...]
        inner = jnp.sum((cross_ref[...] + cross) * weight, axis=1, keepdims=True)
        inv_rms = lax.rsqrt((squares_ref[...] + squares) / features + norm_eps)
        lead[...] = inv_rms * jnp.sum(weight, axis=1, keepdims=True)
        pull[...] = inv_rms * inv_rms * inv_rms * inner / features
        own_low = dot(hot_ref[...], own_low_ref[...])
        half = left_ref.shape[1]
        for own_ref, at in ((left_ref, slice(0, half)), (right_ref, slice(half, 2 * half))):
            own = own_ref[...].astype(f32)
            resid_out[:, at] = (lead[...] * own_low[:, at] - own * pull[...]).astype(bf16)
            normed_out[:, at] = (gain_ref[:, at] * own * inv_rms).astype(bf16)

    low_act = dot_t(hot_ref[...], low_act_ref[...])
    hid_act = acc_ref[...] + product(hids, weights)
    act_out[...] = (lead[...] * low_act - pull[...] * hid_act).astype(bf16)


def finish(places, pieces, w_down, low, before, hot, share, low_act, own, gain):
    count = len(pieces)
    rows, half = own[0].shape
    width = 2 * half
    depth, features = w_down.shape
    pairs = hot.shape[1]
    tile = tile_of(depth, 512)

    def whole(shape):
        return pl.BlockSpec(shape, lambda j, g: (0, 0))

    return pl.pallas_call(
        lambda *refs: finish_body(features, count, *refs),
        grid_spec=pltpu.PrefetchScalarGridSpec(
            num_scalar_prefetch=1,
            grid=(depth // tile,),
            in_specs=piece_specs(pieces, low, tile)
            + carried_specs(rows, pairs, tile)
            + [
                whole((rows, pairs)),
                whole((1, pairs)),
                pl.BlockSpec((tile, pairs), lambda j, g: (j, 0)),
                whole((rows, half)),
                whole((rows, half)),
                pl.BlockSpec((pairs, width), lambda j, g: (0, g[count])),
                whole((1, width)),
            ],
            out_specs=[
                pl.BlockSpec((rows, tile), lambda j, g: (0, j)),
                whole((rows, width)),
                whole((rows, width)),
            ],
            scratch_shapes=[pltpu.VMEM((rows, 1), f32), pltpu.VMEM((rows, 1), f32)],
        ),
        out_shape=[
            jax.ShapeDtypeStruct((rows, depth), bf16),
            jax.ShapeDtypeStruct((rows, width), bf16),
            jax.ShapeDtypeStruct((rows, width), bf16),
        ],
        compiler_params=params(),
        cost_estimate=cost(2 * rows * depth * width, 2 * depth * width + 6 * rows * depth),
    )(
        places,
        *pieces,
        *[w_down] * count,
        *[low] * count,
        *before,
        hot,
        share,
        low_act,
        *own,
        low,
        gain,
    )


def low_rank_shards(
    query_emb,
    passage_emb,
    row_lse,
    positive,
    token_lengths,
    destination,
    mlp_act,
    resid,
    w_down,
    gain,
):
    wide_count = lax.axis_size("wide")
    blk, wide = lax.axis_index("blk"), lax.axis_index("wide")
    tok_count, width = resid.shape
    features = w_down.shape[1]
    pairs = row_lse.shape[0]
    slot_count = 3 * tok_count // (2 * wide_count)
    rows = wide_count * slot_count

    steps = range(1, lax.axis_size("blk"))
    parts = [query_emb, *[swap(query_emb, k) for k in steps]]
    parts += [passage_emb, *[swap(passage_emb, k) for k in steps]]
    parts += [gain[None], *[swap(gain[None], k) for k in steps]]
    first_term = project((blk ^ 3)[None], mlp_act, w_down, width)
    arrived = [swap(first_term, 3)]
    parts = after(first_term, *parts)[1:]
    query_grad, low_own = group_part(parts, row_lse, positive, token_lengths, destination, blk)
    mlp_act = after(low_own, mlp_act)[1]
    for k in (1, 2):
        arrived.append(swap(project((blk ^ k)[None], mlp_act, w_down, width), k))
    own_term = project(blk[None], mlp_act, w_down, width, resid)

    low = lax.all_gather(low_own, "wide", axis=0, tiled=True)
    tables = low[:, features:]
    per_pair = tok_count // pairs
    dest_all = tables[:, :per_pair].reshape(wide_count, tok_count)
    len_all = tables[:, per_pair].reshape(wide_count, pairs)

    packed = pack(wide, destination, own_term, arrived, wide_count, slot_count)
    routed = [packed[k] if k == 0 else swap(packed[k], k, "wide") for k in range(wide_count)]

    low_act = low_activations(low, features, w_down)
    hot = slot_passages(wide, dest_all, len_all, rows)
    share = (1.0 / len_all.astype(f32)).reshape(1, wide_count * pairs)

    left, right = assemble(wide, routed)
    left_1, right_2 = swap(left, 1), swap(right, 2)
    right_1, left_2 = swap(right, 1), swap(left, 2)
    left_3, right_3 = swap(left_1, 2), swap(right_2, 1)

    def places(*pieces):
        return jnp.stack([(blk ^ k) * 2 + side for k, side in pieces])

    totals = back(places((0, 0), (0, 1)), [left, right], w_down, low)
    totals = back(places((1, 0), (2, 1)), [left_1, right_2], w_down, low, totals)
    totals = back(places((1, 1), (2, 0)), [right_1, left_2], w_down, low, totals)
    act_grad, resid_grad, normed_out = finish(
        jnp.concatenate([places((3, 0), (3, 1)), blk[None]]),
        [left_3, right_3],
        w_down,
        low,
        totals,
        hot,
        share,
        low_act,
        [left, right],
        gain[None],
    )
    return (query_grad, resid_grad, act_grad, normed_out)


def coefficients(scores, lse_part, pos_part):
    columns = lax.broadcasted_iota(jnp.int32, scores.shape, 1)
    target = (pos_part[:, None] == columns).astype(jnp.float32)
    return (jnp.exp(scores - lse_part[:, None]) - target).astype(jnp.bfloat16)


def place_rows(destination, wide_count, slot_count):
    tok_count = destination.shape[0]
    dest_hot = (destination == lax.broadcasted_iota(jnp.int32, (tok_count, wide_count), 1)).astype(
        bf16
    )
    token = lax.iota(jnp.int32, tok_count)
    earlier = (token[None, :] < token[:, None]).astype(bf16)
    rank_of = jnp.dot(earlier, dest_hot, preferred_element_type=f32)
    slot_of = jnp.sum(rank_of * dest_hot.astype(f32), axis=1).astype(jnp.int32)
    slot_of = slot_of + destination[:, 0] * slot_count
    return (
        lax.broadcasted_iota(jnp.int32, (wide_count * slot_count, tok_count), 0) == slot_of[None, :]
    ).astype(bf16)


def row_shards(
    query_emb,
    passage_emb,
    row_lse,
    positive,
    token_lengths,
    destination,
    mlp_act,
    resid,
    w_down,
    gain,
):
    pair_rows = query_emb.shape[0]
    tok_count, feat_width = resid.shape
    features = w_down.shape[1]
    blk_index = lax.axis_index("blk")
    wide_count = lax.axis_size("wide")
    slot_count = 3 * tok_count // (2 * wide_count)
    offset = blk_index * feat_width
    query_all = lax.all_gather(query_emb, "blk", axis=0, tiled=True)
    passage_all = lax.all_gather(passage_emb, "blk", axis=0, tiled=True)
    scores = logit_scale * jnp.dot(query_all, passage_all.T, preferred_element_type=f32)
    coef_full = coefficients(scores, row_lse, positive)
    own_coef = lax.dynamic_slice_in_dim(coef_full, blk_index * pair_rows, pair_rows, 0)
    query_grad = (
        logit_scale * jnp.dot(own_coef, passage_all, preferred_element_type=f32)
    ).astype(bf16)
    query_cols = lax.dynamic_slice_in_dim(query_all, offset, feat_width, 1)
    grad_cols = logit_scale * lax.dot_general(
        query_cols, coef_full, (((0,), (0,)), ((), ())), preferred_element_type=f32
    )
    lengths_row = token_lengths[0]
    starts = jnp.cumsum(lengths_row) - lengths_row
    positions = lax.broadcasted_iota(jnp.int32, (tok_count, lengths_row.shape[0]), 0)
    member = (positions >= starts[None, :]) & (positions < (starts + lengths_row)[None, :])
    weights = member.astype(f32) * (1.0 / lengths_row.astype(f32))[None, :]
    tok_grad = lax.dot_general(
        weights,
        grad_cols,
        (((1,), (1,)), ((), ())),
        precision=lax.Precision.HIGHEST,
        preferred_element_type=f32,
    ).astype(bf16)
    terms = jnp.dot(mlp_act, w_down, preferred_element_type=f32)
    own = lax.dynamic_slice_in_dim(terms, offset, feat_width, 1) + resid.astype(f32)
    terms = lax.dynamic_update_slice_in_dim(terms, own, offset, 1)
    hidden = lax.psum_scatter(terms.astype(bf16), "blk", scatter_dimension=1, tiled=True)
    placer = place_rows(destination, wide_count, slot_count)
    payload = jnp.concatenate([hidden, tok_grad], axis=1)
    packed = jnp.dot(placer, payload, preferred_element_type=f32).astype(bf16)
    packed = packed.reshape(wide_count, slot_count, 2 * feat_width)
    rows = lax.all_to_all(packed, "wide", split_axis=0, concat_axis=0, tiled=True).reshape(
        wide_count * slot_count, 2 * feat_width
    )
    hidden = rows[:, :feat_width].astype(f32)
    gained = gain[None, :] * rows[:, feat_width:].astype(f32)
    squares, inner_sum = lax.psum(
        (jnp.sum(hidden * hidden, axis=1), jnp.sum(gained * hidden, axis=1)), "blk"
    )
    inv_rms = lax.rsqrt(squares / features + norm_eps)[:, None]
    normed = (gain[None, :] * hidden * inv_rms).astype(bf16)
    resid_back = (
        inv_rms * gained - hidden * (inv_rms * inv_rms * inv_rms) * inner_sum[:, None] / features
    ).astype(bf16)
    act_back = dot_t(lax.all_gather(resid_back, "blk", axis=1, tiled=True), w_down)
    return (query_grad, resid_back, act_back.astype(bf16), normed)


def solution(mesh):
    blk_count, wide_count = mesh.shape["blk"], mesh.shape["wide"]

    def shards(*operands):
        pairs, tok_count = operands[2].shape[0], operands[7].shape[0]
        low_rank = 2 * wide_count * pairs <= 3 * tok_count
        per_pair = tok_count // pairs
        aligned = operands[9].shape[0] % (lane * operands[0].shape[0]) == 0
        if low_rank and blk_count == 4 and aligned and per_pair * pairs == tok_count and wide_count & (wide_count - 1) == 0:
            return low_rank_shards(*operands)
        return row_shards(*operands)

    return jax.shard_map(
        shards,
        mesh=mesh,
        in_specs=(
            P(("wide", "blk"), None),
            P(("wide", "blk"), None),
            P("wide"),
            P("wide"),
            P("wide", None),
            P("wide", None),
            P("wide", "blk"),
            P("wide", "blk"),
            P("blk", None),
            P("blk"),
        ),
        out_specs=(P(("wide", "blk"), None), P("wide", "blk"), P("wide", "blk"), P("wide", "blk")),
        check_vma=False,
    )
```

```python
import jax
import jax.numpy as jnp
from jax import lax
from jax.experimental import pallas as pl
from jax.experimental.pallas import tpu as pltpu
from jax.sharding import PartitionSpec as P

logit_scale = 24.0
norm_eps = 1e-06
f32 = jnp.float32
bf16 = jnp.bfloat16
i32 = jnp.int32
lane = 128
kernel_vmem = 46 * 1024 * 1024


def params():
    return pltpu.CompilerParams(vmem_limit_bytes=kernel_vmem)


def cost(flops, nbytes):
    return pl.CostEstimate(flops=flops, bytes_accessed=nbytes, transcendentals=0)


def tile_of(extent, most):
    tile = most
    while extent % tile:
        tile //= 2
    return tile


def iota(shape, dim):
    return lax.broadcasted_iota(i32, shape, dim)


def dot(left, right):
    return jnp.dot(left, right, preferred_element_type=f32)


def dot_t(left, right):
    return lax.dot_general(left, right, (((1,), (1,)), ((), ())), preferred_element_type=f32)


def swap(rows, k, axis="blk"):
    return lax.ppermute(rows, axis, [(i, i ^ k) for i in range(lax.axis_size(axis))])


def after(first, *later):
    return lax.optimization_barrier((first, *later))


def project_body(has_resid, group_ref, act_hbm, w_hbm, *refs):
    out_ref, act, weights, act_sem, sems = refs[has_resid:]
    width = out_ref.shape[1]
    count, _, tile = weights.shape
    first = group_ref[0] * width

    def weight_copy(i):
        columns = pl.ds(pl.multiple_of(first + i * tile, lane), tile)
        return pltpu.make_async_copy(w_hbm.at[:, columns], weights.at[i], sems.at[i])

    act_copy = pltpu.make_async_copy(act_hbm, act, act_sem)
    act_copy.start()
    for i in range(count):
        weight_copy(i).start()
    act_copy.wait()

    @pl.loop(0, count)
    def _(i):
        weight_copy(i).wait()
        columns = pl.ds(pl.multiple_of(i * tile, lane), tile)
        term = dot(act[...], weights[i])
        if has_resid:
            term = term + refs[0][:, columns].astype(f32)
        out_ref[:, columns] = term.astype(out_ref.dtype)


def project(group, act, w_down, width, resid=None):
    rows, depth = act.shape
    tile = tile_of(width, 256)
    count = width // tile
    own = [] if resid is None else [resid]
    return pl.pallas_call(
        lambda *refs: project_body(len(own), *refs),
        in_specs=[pl.BlockSpec(memory_space=pltpu.SMEM)]
        + [pl.BlockSpec(memory_space=pl.ANY)] * 2
        + [pl.BlockSpec(memory_space=pltpu.VMEM)] * len(own),
        out_specs=pl.BlockSpec(memory_space=pltpu.VMEM),
        out_shape=jax.ShapeDtypeStruct((rows, width), f32 if own else bf16),
        scratch_shapes=[
            pltpu.VMEM((rows, depth), bf16),
            pltpu.VMEM((count, depth, tile), bf16),
            pltpu.SemaphoreType.DMA,
            pltpu.SemaphoreType.DMA((count,)),
        ],
        compiler_params=params(),
        cost_estimate=cost(2 * rows * depth * width, 2 * depth * width + 2 * rows * depth),
    )(group, act, w_down, *own)


def payload_body(query_ref, passage_ref, gain_ref, out_ref):
    features = query_ref.shape[1]
    piece = gain_ref.shape[1]
    gain = gain_ref[...]
    high = gain.astype(bf16)
    out_ref[:, :features] = query_ref[...]
    out_ref[:, features : 2 * features] = passage_ref[...]
    out_ref[:, 2 * features : 2 * features + piece] = high
    out_ref[:, 2 * features + piece :] = (gain - high.astype(f32)).astype(bf16)


def payload(query_emb, passage_emb, gain):
    own, features = query_emb.shape
    gain = gain.reshape(own, -1)
    return pl.pallas_call(
        payload_body,
        out_shape=jax.ShapeDtypeStruct((own, 2 * features + 2 * gain.shape[1]), bf16),
        compiler_params=params(),
        cost_estimate=cost(own * features, 8 * own * features),
    )(query_emb, passage_emb, gain)


def group_body(count, blk_ref, *refs):
    parts, refs = refs[:count], refs[count:]
    lse_row_ref, lse_ref, pos_row_ref, pos_ref, table_ref = refs[:5]
    query_grad_ref, low_ref, query_all, passage_all, gain_all = refs[5:]
    own, features = query_grad_ref.shape
    pairs = own * count
    piece = features // pairs
    blk = blk_ref[0]
    for k in range(count):
        query_all[k * own : (k + 1) * own] = parts[k][:, :features].astype(f32)
        passage_all[k * own : (k + 1) * own] = parts[k][:, features : 2 * features].astype(f32)
        gains = parts[k][:, 2 * features : 2 * features + piece].astype(f32)
        gains = gains + parts[k][:, 2 * features + piece :].astype(f32)
        for row in range(own):
            first = pl.multiple_of(((blk ^ k) * own + row) * piece, lane)
            gain_all[:, pl.ds(first, piece)] = gains[row : row + 1]
    queries = query_all[...].astype(bf16)
    passages = passage_all[...].astype(bf16)

    def named(dim):
        place = iota((pairs, pairs), dim)
        return (blk ^ (place // own)) * own + place % own

    here_rows, here_cols = named(0), named(1)
    at_rows = here_rows == iota((pairs, pairs), 1)
    at_cols = here_cols == iota((pairs, pairs), 0)
    lse = jnp.sum(jnp.where(at_rows, lse_row_ref[...], 0.0), axis=1, keepdims=True)
    pos = jnp.sum(jnp.where(at_rows, pos_row_ref[...], 0), axis=1, keepdims=True)
    hit = (pos == here_cols).astype(f32)
    coef = (jnp.exp(logit_scale * dot_t(queries, passages) - lse) - hit).astype(bf16)
    query_grad_ref[...] = (logit_scale * dot(coef, passages))[:own].astype(bf16)
    lse = jnp.sum(jnp.where(at_cols, lse_ref[...], 0.0), axis=0, keepdims=True)
    pos = jnp.sum(jnp.where(at_cols, pos_ref[...], 0), axis=0, keepdims=True)
    hit = (pos == here_rows).astype(f32)
    turned = (jnp.exp(logit_scale * dot_t(passages, queries) - lse) - hit).astype(bf16)
    turned = dot(at_cols.astype(bf16), turned).astype(bf16)
    pass_grad = logit_scale * dot(turned, queries)
    low_ref[:, :features] = (gain_all[...] * pass_grad).astype(bf16)
    low_ref[:, features:] = table_ref[...]


def group_part(parts, row_lse, positive, token_lengths, destination, features, blk):
    own = parts[0].shape[0]
    pairs = row_lse.shape[0]
    table = jnp.concatenate([destination.reshape(pairs, -1), token_lengths.reshape(pairs, 1)], 1)
    table = jnp.pad(table, ((0, 0), (0, lane - table.shape[1]))).astype(bf16)
    return pl.pallas_call(
        lambda *refs: group_body(pairs // own, *refs),
        in_specs=[pl.BlockSpec(memory_space=pltpu.SMEM)]
        + [pl.BlockSpec(memory_space=pltpu.VMEM)] * (len(parts) + 5),
        out_specs=[pl.BlockSpec(memory_space=pltpu.VMEM)] * 2,
        out_shape=[
            jax.ShapeDtypeStruct((own, features), bf16),
            jax.ShapeDtypeStruct((pairs, features + lane), bf16),
        ],
        scratch_shapes=[
            pltpu.VMEM((pairs, features), f32),
            pltpu.VMEM((pairs, features), f32),
            pltpu.VMEM((1, features), f32),
        ],
        compiler_params=params(),
        cost_estimate=cost(8 * pairs * pairs * features, 8 * pairs * features),
    )(
        blk[None],
        *parts,
        row_lse[None],
        row_lse[:, None],
        positive[None],
        positive[:, None],
        table,
    )


def earlier_of(tokens):
    return (iota((tokens, tokens), 0) < iota((tokens, tokens), 1)).astype(bf16)


def pack_body(groups, dest_ref, own_ref, *rest):
    terms, out_ref = rest[:-1], rest[-1]
    rows = out_ref.shape[0]
    tokens = dest_ref.shape[1]
    hidden = own_ref[...]
    for term in terms:
        hidden = hidden + term[...].astype(f32)
    dest = dest_ref[...]
    hit = (dest == iota((groups, tokens), 0)).astype(f32)
    rank = dot(hit.astype(bf16), earlier_of(tokens))
    rank = jnp.sum(rank * hit, axis=0, keepdims=True).astype(i32)
    place = iota((rows, tokens), 0) == dest * (rows // groups) + rank
    out_ref[...] = dot(place.astype(f32).astype(bf16), hidden.astype(bf16)).astype(bf16)


def pack(destination, own, terms, groups, slots):
    tokens, width = own.shape
    tile = tile_of(width, 512)
    rows = groups * slots
    column_spec = pl.BlockSpec((tokens, tile), lambda j: (0, j))
    return pl.pallas_call(
        lambda *refs: pack_body(groups, *refs),
        grid=(width // tile,),
        in_specs=[pl.BlockSpec((1, tokens), lambda j: (0, 0))] + [column_spec] * (1 + len(terms)),
        out_specs=pl.BlockSpec((rows, tile), lambda j: (0, j)),
        out_shape=jax.ShapeDtypeStruct((rows, width), bf16),
        compiler_params=params(),
        cost_estimate=cost(2 * rows * tokens * width, 10 * tokens * width),
    )(destination.reshape(1, tokens), own, *terms)


def slots_body(wide_ref, dest_ref, len_ref, hot_ref):
    groups, tokens = dest_ref.shape
    pairs = len_ref.shape[1]
    rows = hot_ref.shape[0]
    slots = rows // groups
    hit = dest_ref[...].astype(i32) == wide_ref[0]
    rank = dot(hit.astype(f32).astype(bf16), earlier_of(tokens))
    upto = (iota((pairs, pairs), 0) <= iota((pairs, pairs), 1)).astype(bf16)
    ends = dot(len_ref[...], upto)
    token = iota((groups, tokens), 1).astype(f32)
    passage = jnp.ones((groups, tokens), f32)
    for pair in range(pairs):
        passage = passage + (token >= ends[:, pair : pair + 1]).astype(f32)
    code = jnp.where(hit, passage, 0.0)
    spread = (iota((rows, groups), 0) // slots == iota((rows, groups), 1)).astype(bf16)
    rank_rows = dot(spread, rank.astype(bf16)).astype(i32)
    code_rows = dot(spread, code.astype(bf16))
    here = rank_rows == iota((rows, tokens), 0) % slots
    taken = jnp.sum(jnp.where(here, code_rows, 0.0), axis=1, keepdims=True).astype(i32)
    column = iota((rows, groups * pairs), 1)
    first = iota((rows, groups * pairs), 0) // slots * pairs
    hot = (taken > 0) & (column == first + taken - 1)
    hot_ref[...] = hot.astype(f32).astype(bf16)


def slot_passages(wide, dest_all, len_all, rows):
    groups, pairs = len_all.shape
    return pl.pallas_call(
        slots_body,
        in_specs=[pl.BlockSpec(memory_space=pltpu.SMEM)]
        + [pl.BlockSpec(memory_space=pltpu.VMEM)] * 2,
        out_specs=pl.BlockSpec(memory_space=pltpu.VMEM),
        out_shape=jax.ShapeDtypeStruct((rows, groups * pairs), bf16),
        compiler_params=params(),
        cost_estimate=cost(4 * rows * groups * dest_all.shape[1], 2 * rows * groups * pairs),
    )(wide[None], dest_all, len_all)


def low_act_body(low_ref, w_hbm, out_ref, weights, sems):
    count, tile, _ = weights.shape

    def weight_copy(t):
        rows = pl.ds(pl.multiple_of(t * tile, tile), tile)
        return pltpu.make_async_copy(w_hbm.at[rows], weights.at[t], sems.at[t])

    for t in range(count):
        weight_copy(t).start()

    @pl.loop(0, count)
    def _(t):
        weight_copy(t).wait()
        rows = pl.ds(pl.multiple_of(t * tile, tile), tile)
        out_ref[rows] = dot_t(weights[t], low_ref[...]).astype(bf16)


def low_activations(low, features, w_down):
    pairs = low.shape[0]
    depth = w_down.shape[0]
    tile = tile_of(depth, 512)
    count = depth // tile
    return pl.pallas_call(
        low_act_body,
        grid=(1,),
        in_specs=[
            pl.BlockSpec((pairs, features), lambda j: (0, 0)),
            pl.BlockSpec(memory_space=pl.ANY),
        ],
        out_specs=pl.BlockSpec((depth, pairs), lambda j: (0, 0)),
        out_shape=jax.ShapeDtypeStruct((depth, pairs), bf16),
        scratch_shapes=[
            pltpu.VMEM((count, tile, features), bf16),
            pltpu.SemaphoreType.DMA((count,)),
        ],
        compiler_params=params(),
        cost_estimate=cost(2 * pairs * depth * features, 2 * depth * features),
    )(low, w_down)


def statistics(hids, lows):
    squares, cross = 0.0, 0.0
    for hid_ref, low_ref in zip(hids, lows):
        hid = hid_ref[...].astype(f32)
        squares = squares + jnp.sum(hid * hid, axis=1, keepdims=True)
        cross = cross + dot_t(hid_ref[...], low_ref[...])
    return squares, cross


def weight_copies(places_ref, w_hbm, weights, sems):
    count, tile, across = weights.shape
    pieces = sems.shape[1]
    width = across // pieces

    def copies(t):
        rows = pl.ds(pl.multiple_of(t * tile, tile), tile)
        return [
            pltpu.make_async_copy(
                w_hbm.at[rows, pl.ds(pl.multiple_of(places_ref[n] * width, lane), width)],
                weights.at[t, :, n * width : (n + 1) * width],
                sems.at[t, n],
            )
            for n in range(pieces)
        ]

    return copies


def back_body(count, carried, places_ref, *refs):
    hids, lows, w_hbm, refs = refs[:count], refs[count : 2 * count], refs[2 * count], refs[2 * count + 1 :]
    before, refs = refs[:carried], refs[carried:]
    acc_hbm, squares_ref, cross_ref, hid, weights, acc, sems, in_sems, out_sems = refs
    copies = weight_copies(places_ref, w_hbm, weights, sems)

    def acc_in(t):
        return pltpu.make_async_copy(before[0].at[t], acc.at[t], in_sems.at[t])

    def acc_out(t):
        return pltpu.make_async_copy(acc.at[t], acc_hbm.at[t], out_sems.at[t])

    for t in range(weights.shape[0]):
        for copy in copies(t):
            copy.start()
        if carried:
            acc_in(t).start()
    squares, cross = statistics(hids, lows)
    if carried:
        squares, cross = before[1][...] + squares, before[2][...] + cross
    squares_ref[...], cross_ref[...] = squares, cross
    width = hids[0].shape[1]
    for n in range(count):
        hid[:, n * width : (n + 1) * width] = hids[n][...]

    @pl.loop(0, weights.shape[0])
    def _(t):
        for copy in copies(t):
            copy.wait()
        total = dot_t(hid[...], weights[t])
        if carried:
            acc_in(t).wait()
            total = total + acc[t]
        acc[t] = total
        acc_out(t).start()

    @pl.loop(0, weights.shape[0])
    def _(t):
        acc_out(t).wait()


def back(places, pieces, w_down, low, before=()):
    count = len(pieces)
    rows, width = pieces[0].shape
    depth = w_down.shape[0]
    pairs = low.shape[0]
    tile = tile_of(depth, 512)
    tiles = depth // tile
    small = [
        pl.BlockSpec((rows, 1), lambda j, g: (0, 0)),
        pl.BlockSpec((rows, pairs), lambda j, g: (0, 0)),
    ]
    anywhere = pl.BlockSpec(memory_space=pl.ANY)
    return pl.pallas_call(
        lambda *refs: back_body(count, len(before), *refs),
        grid_spec=pltpu.PrefetchScalarGridSpec(
            num_scalar_prefetch=1,
            grid=(1,),
            in_specs=[pl.BlockSpec((rows, width), lambda j, g: (0, 0))] * count
            + [pl.BlockSpec((pairs, width), lambda j, g, n=n: (0, g[n])) for n in range(count)]
            + [anywhere]
            + [anywhere, *small][: len(before)],
            out_specs=[anywhere, *small],
            scratch_shapes=[
                pltpu.VMEM((rows, count * width), bf16),
                pltpu.VMEM((tiles, tile, count * width), bf16),
                pltpu.VMEM((tiles, rows, tile), f32),
                pltpu.SemaphoreType.DMA((tiles, count)),
                pltpu.SemaphoreType.DMA((tiles,)),
                pltpu.SemaphoreType.DMA((tiles,)),
            ],
        ),
        out_shape=[
            jax.ShapeDtypeStruct((tiles, rows, tile), f32),
            jax.ShapeDtypeStruct((rows, 1), f32),
            jax.ShapeDtypeStruct((rows, pairs), f32),
        ],
        compiler_params=params(),
        cost_estimate=cost(2 * rows * depth * width * count, 2 * depth * width * count),
    )(places, *pieces, *[low] * count, w_down, *before)


def finish_body(features, count, places_ref, *refs):
    hids, lows, w_hbm, refs = refs[:count], refs[count : 2 * count], refs[2 * count], refs[2 * count + 1 :]
    acc_hbm, squares_ref, cross_ref, hot_ref, share_ref, low_act_ref, left_ref, right_ref = refs[:8]
    own_low_ref, gain_ref, act_hbm, resid_out, normed_out = refs[8:13]
    hid, weights, acc, act, sems, in_sems, out_sems = refs[13:]
    tiles, tile, _ = weights.shape
    copies = weight_copies(places_ref, w_hbm, weights, sems)

    def acc_in(t):
        return pltpu.make_async_copy(acc_hbm.at[t], acc.at[t], in_sems.at[t])

    def act_out(t):
        columns = pl.ds(pl.multiple_of(t * tile, lane), tile)
        return pltpu.make_async_copy(act.at[t], act_hbm.at[:, columns], out_sems.at[t])

    for t in range(tiles):
        for copy in copies(t):
            copy.start()
        acc_in(t).start()
    squares, cross = statistics(hids, lows)
    weight = hot_ref[...].astype(f32) * share_ref[...]
    inner = jnp.sum((cross_ref[...] + cross) * weight, axis=1, keepdims=True)
    inv_rms = lax.rsqrt((squares_ref[...] + squares) / features + norm_eps)
    lead = inv_rms * jnp.sum(weight, axis=1, keepdims=True)
    pull = inv_rms * inv_rms * inv_rms * inner / features
    own_low = dot(hot_ref[...], own_low_ref[...])
    half = left_ref.shape[1]
    for own_ref, at in ((left_ref, slice(0, half)), (right_ref, slice(half, 2 * half))):
        own = own_ref[...].astype(f32)
        resid_out[:, at] = (lead * own_low[:, at] - own * pull).astype(bf16)
        normed_out[:, at] = (gain_ref[:, at] * own * inv_rms).astype(bf16)
    width = hids[0].shape[1]
    for n in range(count):
        hid[:, n * width : (n + 1) * width] = hids[n][...]

    @pl.loop(0, tiles)
    def _(t):
        for copy in copies(t):
            copy.wait()
        total = dot_t(hid[...], weights[t])
        rows = pl.ds(pl.multiple_of(t * tile, tile), tile)
        low_act = dot_t(hot_ref[...], low_act_ref[rows])
        acc_in(t).wait()
        act[t] = (lead * low_act - pull * (total + acc[t])).astype(bf16)
        act_out(t).start()

    @pl.loop(0, tiles)
    def _(t):
        act_out(t).wait()


def finish(places, pieces, w_down, low, before, hot, share, low_act, own, gain):
    count = len(pieces)
    rows, half = own[0].shape
    width = 2 * half
    depth, features = w_down.shape
    pairs = hot.shape[1]
    tile = tile_of(depth, 512)
    tiles = depth // tile
    anywhere = pl.BlockSpec(memory_space=pl.ANY)

    def whole(shape):
        return pl.BlockSpec(shape, lambda j, g: (0, 0))

    return pl.pallas_call(
        lambda *refs: finish_body(features, count, *refs),
        grid_spec=pltpu.PrefetchScalarGridSpec(
            num_scalar_prefetch=1,
            grid=(1,),
            in_specs=[whole((rows, half))] * count
            + [pl.BlockSpec((pairs, half), lambda j, g, n=n: (0, g[n])) for n in range(count)]
            + [
                anywhere,
                anywhere,
                whole((rows, 1)),
                whole((rows, pairs)),
                whole((rows, pairs)),
                whole((1, pairs)),
                whole((depth, pairs)),
                whole((rows, half)),
                whole((rows, half)),
                pl.BlockSpec((pairs, width), lambda j, g: (0, g[count])),
                whole((1, width)),
            ],
            out_specs=[anywhere, whole((rows, width)), whole((rows, width))],
            scratch_shapes=[
                pltpu.VMEM((rows, count * half), bf16),
                pltpu.VMEM((tiles, tile, count * half), bf16),
                pltpu.VMEM((tiles, rows, tile), f32),
                pltpu.VMEM((tiles, rows, tile), bf16),
                pltpu.SemaphoreType.DMA((tiles, count)),
                pltpu.SemaphoreType.DMA((tiles,)),
                pltpu.SemaphoreType.DMA((tiles,)),
            ],
        ),
        out_shape=[
            jax.ShapeDtypeStruct((rows, depth), bf16),
            jax.ShapeDtypeStruct((rows, width), bf16),
            jax.ShapeDtypeStruct((rows, width), bf16),
        ],
        compiler_params=params(),
        cost_estimate=cost(2 * rows * depth * width, 2 * depth * width + 6 * rows * depth),
    )(
        places,
        *pieces,
        *[low] * count,
        w_down,
        *before,
        hot,
        share,
        low_act,
        *own,
        low,
        gain,
    )


def low_rank_shards(
    query_emb,
    passage_emb,
    row_lse,
    positive,
    token_lengths,
    destination,
    mlp_act,
    resid,
    w_down,
    gain,
):
    wide_count = lax.axis_size("wide")
    blk, wide = lax.axis_index("blk"), lax.axis_index("wide")
    tok_count, width = resid.shape
    features = w_down.shape[1]
    pairs = row_lse.shape[0]
    slot_count = 3 * tok_count // (2 * wide_count)
    rows = wide_count * slot_count

    both = payload(query_emb, passage_emb, gain)
    parts = [both] + [swap(both, k) for k in (1, 2, 3)]
    first_term = project((blk ^ 3)[None], mlp_act, w_down, width)
    arrived = [swap(first_term, 3)]
    parts = after(first_term, *parts)[1:]
    query_grad, low_own = group_part(
        parts, row_lse, positive, token_lengths, destination, features, blk
    )
    mlp_act = after(low_own, mlp_act)[1]
    for k in (1, 2):
        arrived.append(swap(project((blk ^ k)[None], mlp_act, w_down, width), k))
    own_term = project(blk[None], mlp_act, w_down, width, resid)

    low = lax.all_gather(low_own, "wide", axis=0, tiled=True)
    tables = low[:, features:]
    per_pair = tok_count // pairs
    dest_all = tables[:, :per_pair].reshape(wide_count, tok_count)
    len_all = tables[:, per_pair].reshape(wide_count, pairs)

    packed = pack(destination, own_term, arrived, wide_count, slot_count)
    packed = packed.reshape(wide_count, slot_count, width)
    own_hid = lax.all_to_all(packed, "wide", split_axis=0, concat_axis=0, tiled=True)

    low_act = low_activations(low, features, w_down)
    hot = slot_passages(wide, dest_all, len_all, rows)
    share = (1.0 / len_all.astype(f32)).reshape(1, wide_count * pairs)

    low_act, hot, share, own_hid = lax.optimization_barrier((low_act, hot, share, own_hid))
    own_hid = own_hid.reshape(rows, width)
    left, right = own_hid[:, : width // 2], own_hid[:, width // 2 :]
    left_1, right_2 = swap(left, 1), swap(right, 2)
    right_1, left_2 = swap(right, 1), swap(left, 2)
    left_3, right_3 = swap(left_1, 2), swap(right_2, 1)

    def places(*pieces):
        return jnp.stack([(blk ^ k) * 2 + side for k, side in pieces])

    totals = back(places((0, 0), (0, 1)), [left, right], w_down, low)
    totals = back(
        places((1, 0), (2, 1), (1, 1), (2, 0)),
        [left_1, right_2, right_1, left_2],
        w_down,
        low,
        totals,
    )
    act_grad, resid_grad, normed_out = finish(
        jnp.concatenate([places((3, 0), (3, 1)), blk[None]]),
        [left_3, right_3],
        w_down,
        low,
        totals,
        hot,
        share,
        low_act,
        [left, right],
        gain[None],
    )
    return (query_grad, resid_grad, act_grad, normed_out)


def coefficients(scores, lse_part, pos_part):
    columns = lax.broadcasted_iota(jnp.int32, scores.shape, 1)
    target = (pos_part[:, None] == columns).astype(jnp.float32)
    return (jnp.exp(scores - lse_part[:, None]) - target).astype(jnp.bfloat16)


def place_rows(destination, wide_count, slot_count):
    tok_count = destination.shape[0]
    dest_hot = (destination == lax.broadcasted_iota(jnp.int32, (tok_count, wide_count), 1)).astype(
        bf16
    )
    token = lax.iota(jnp.int32, tok_count)
    earlier = (token[None, :] < token[:, None]).astype(bf16)
    rank_of = jnp.dot(earlier, dest_hot, preferred_element_type=f32)
    slot_of = jnp.sum(rank_of * dest_hot.astype(f32), axis=1).astype(jnp.int32)
    slot_of = slot_of + destination[:, 0] * slot_count
    return (
        lax.broadcasted_iota(jnp.int32, (wide_count * slot_count, tok_count), 0) == slot_of[None, :]
    ).astype(bf16)


def row_shards(
    query_emb,
    passage_emb,
    row_lse,
    positive,
    token_lengths,
    destination,
    mlp_act,
    resid,
    w_down,
    gain,
):
    pair_rows = query_emb.shape[0]
    tok_count, feat_width = resid.shape
    features = w_down.shape[1]
    blk_index = lax.axis_index("blk")
    wide_count = lax.axis_size("wide")
    slot_count = 3 * tok_count // (2 * wide_count)
    offset = blk_index * feat_width
    query_all = lax.all_gather(query_emb, "blk", axis=0, tiled=True)
    passage_all = lax.all_gather(passage_emb, "blk", axis=0, tiled=True)
    scores = logit_scale * jnp.dot(query_all, passage_all.T, preferred_element_type=f32)
    coef_full = coefficients(scores, row_lse, positive)
    own_coef = lax.dynamic_slice_in_dim(coef_full, blk_index * pair_rows, pair_rows, 0)
    query_grad = (
        logit_scale * jnp.dot(own_coef, passage_all, preferred_element_type=f32)
    ).astype(bf16)
    query_cols = lax.dynamic_slice_in_dim(query_all, offset, feat_width, 1)
    grad_cols = logit_scale * lax.dot_general(
        query_cols, coef_full, (((0,), (0,)), ((), ())), preferred_element_type=f32
    )
    lengths_row = token_lengths[0]
    starts = jnp.cumsum(lengths_row) - lengths_row
    positions = lax.broadcasted_iota(jnp.int32, (tok_count, lengths_row.shape[0]), 0)
    member = (positions >= starts[None, :]) & (positions < (starts + lengths_row)[None, :])
    weights = member.astype(f32) * (1.0 / lengths_row.astype(f32))[None, :]
    tok_grad = lax.dot_general(
        weights,
        grad_cols,
        (((1,), (1,)), ((), ())),
        precision=lax.Precision.HIGHEST,
        preferred_element_type=f32,
    ).astype(bf16)
    terms = jnp.dot(mlp_act, w_down, preferred_element_type=f32)
    own = lax.dynamic_slice_in_dim(terms, offset, feat_width, 1) + resid.astype(f32)
    terms = lax.dynamic_update_slice_in_dim(terms, own, offset, 1)
    hidden = lax.psum_scatter(terms.astype(bf16), "blk", scatter_dimension=1, tiled=True)
    placer = place_rows(destination, wide_count, slot_count)
    payload = jnp.concatenate([hidden, tok_grad], axis=1)
    packed = jnp.dot(placer, payload, preferred_element_type=f32).astype(bf16)
    packed = packed.reshape(wide_count, slot_count, 2 * feat_width)
    rows = lax.all_to_all(packed, "wide", split_axis=0, concat_axis=0, tiled=True).reshape(
        wide_count * slot_count, 2 * feat_width
    )
    hidden = rows[:, :feat_width].astype(f32)
    gained = gain[None, :] * rows[:, feat_width:].astype(f32)
    squares, inner_sum = lax.psum(
        (jnp.sum(hidden * hidden, axis=1), jnp.sum(gained * hidden, axis=1)), "blk"
    )
    inv_rms = lax.rsqrt(squares / features + norm_eps)[:, None]
    normed = (gain[None, :] * hidden * inv_rms).astype(bf16)
    resid_back = (
        inv_rms * gained - hidden * (inv_rms * inv_rms * inv_rms) * inner_sum[:, None] / features
    ).astype(bf16)
    act_back = dot_t(lax.all_gather(resid_back, "blk", axis=1, tiled=True), w_down)
    return (query_grad, resid_back, act_back.astype(bf16), normed)


def solution(mesh):
    blk_count, wide_count = mesh.shape["blk"], mesh.shape["wide"]

    def shards(*operands):
        pairs, tok_count = operands[2].shape[0], operands[7].shape[0]
        low_rank = 2 * wide_count * pairs <= 3 * tok_count
        per_pair = tok_count // pairs
        aligned = operands[9].shape[0] % (lane * operands[0].shape[0]) == 0
        if low_rank and blk_count == 4 and aligned and per_pair * pairs == tok_count and wide_count & (wide_count - 1) == 0:
            return low_rank_shards(*operands)
        return row_shards(*operands)

    return jax.shard_map(
        shards,
        mesh=mesh,
        in_specs=(
            P(("wide", "blk"), None),
            P(("wide", "blk"), None),
            P("wide"),
            P("wide"),
            P("wide", None),
            P("wide", None),
            P("wide", "blk"),
            P("wide", "blk"),
            P("blk", None),
            P("blk"),
        ),
        out_specs=(P(("wide", "blk"), None), P("wide", "blk"), P("wide", "blk"), P("wide", "blk")),
        check_vma=False,
    )
```

```python
import jax
import jax.numpy as jnp
from jax import lax
from jax.experimental import pallas as pl
from jax.experimental.pallas import tpu as pltpu
from jax.sharding import PartitionSpec as P

logit_scale = 24.0
norm_eps = 1e-06
f32 = jnp.float32
bf16 = jnp.bfloat16
i32 = jnp.int32
lane = 128
kernel_vmem = 46 * 1024 * 1024


def params():
    return pltpu.CompilerParams(vmem_limit_bytes=kernel_vmem)


def cost(flops, nbytes):
    return pl.CostEstimate(flops=flops, bytes_accessed=nbytes, transcendentals=0)


def tile_of(extent, most):
    tile = most
    while extent % tile:
        tile //= 2
    return tile


def iota(shape, dim):
    return lax.broadcasted_iota(i32, shape, dim)


def dot(left, right):
    return jnp.dot(left, right, preferred_element_type=f32)


def dot_t(left, right):
    return lax.dot_general(left, right, (((1,), (1,)), ((), ())), preferred_element_type=f32)


def swap(rows, k, axis="blk"):
    return lax.ppermute(rows, axis, [(i, i ^ k) for i in range(lax.axis_size(axis))])


def after(first, *later):
    return lax.optimization_barrier((first, *later))


def project_body(has_resid, group_ref, act_hbm, w_hbm, *refs):
    out_ref, act, weights, act_sem, sems = refs[has_resid:]
    width = out_ref.shape[1]
    count, _, tile = weights.shape
    first = group_ref[0] * width

    def weight_copy(i):
        columns = pl.ds(pl.multiple_of(first + i * tile, lane), tile)
        return pltpu.make_async_copy(w_hbm.at[:, columns], weights.at[i], sems.at[i])

    act_copy = pltpu.make_async_copy(act_hbm, act, act_sem)
    act_copy.start()
    for i in range(count):
        weight_copy(i).start()
    act_copy.wait()

    @pl.loop(0, count)
    def _(i):
        weight_copy(i).wait()
        columns = pl.ds(pl.multiple_of(i * tile, lane), tile)
        term = dot(act[...], weights[i])
        if has_resid:
            term = term + refs[0][:, columns].astype(f32)
        out_ref[:, columns] = term.astype(out_ref.dtype)


def project(group, act, w_down, width, resid=None):
    rows, depth = act.shape
    tile = tile_of(width, 256)
    count = width // tile
    own = [] if resid is None else [resid]
    return pl.pallas_call(
        lambda *refs: project_body(len(own), *refs),
        in_specs=[pl.BlockSpec(memory_space=pltpu.SMEM)]
        + [pl.BlockSpec(memory_space=pl.ANY)] * 2
        + [pl.BlockSpec(memory_space=pltpu.VMEM)] * len(own),
        out_specs=pl.BlockSpec(memory_space=pltpu.VMEM),
        out_shape=jax.ShapeDtypeStruct((rows, width), f32 if own else bf16),
        scratch_shapes=[
            pltpu.VMEM((rows, depth), bf16),
            pltpu.VMEM((count, depth, tile), bf16),
            pltpu.SemaphoreType.DMA,
            pltpu.SemaphoreType.DMA((count,)),
        ],
        compiler_params=params(),
        cost_estimate=cost(2 * rows * depth * width, 2 * depth * width + 2 * rows * depth),
    )(group, act, w_down, *own)


def payload_body(query_ref, passage_ref, gain_ref, out_ref, gains):
    own, features = query_ref.shape
    piece = gains.shape[1]
    for row in range(own):
        gains[row : row + 1] = gain_ref[:, row * piece : (row + 1) * piece]
    gain = gains[...]
    high = gain.astype(bf16)
    out_ref[:, :features] = query_ref[...]
    out_ref[:, features : 2 * features] = passage_ref[...]
    out_ref[:, 2 * features : 2 * features + piece] = high
    out_ref[:, 2 * features + piece :] = (gain - high.astype(f32)).astype(bf16)


def payload(query_emb, passage_emb, gain):
    own, features = query_emb.shape
    piece = gain.shape[0] // own
    return pl.pallas_call(
        payload_body,
        out_shape=jax.ShapeDtypeStruct((own, 2 * features + 2 * piece), bf16),
        scratch_shapes=[pltpu.VMEM((own, piece), f32)],
        compiler_params=params(),
        cost_estimate=cost(own * features, 8 * own * features),
    )(query_emb, passage_emb, gain[None])


def group_body(count, blk_ref, *refs):
    parts, refs = refs[:count], refs[count:]
    lse_ref, pos_ref, dest_ref, len_ref = refs[:4]
    query_grad_ref, low_ref, query_all, passage_all, gain_all = refs[4:]
    own, features = query_grad_ref.shape
    pairs = own * count
    piece = features // pairs
    blk = blk_ref[0]
    for k in range(count):
        query_all[k * own : (k + 1) * own] = parts[k][:, :features].astype(f32)
        passage_all[k * own : (k + 1) * own] = parts[k][:, features : 2 * features].astype(f32)
        gains = parts[k][:, 2 * features : 2 * features + piece].astype(f32)
        gains = gains + parts[k][:, 2 * features + piece :].astype(f32)
        for row in range(own):
            first = pl.multiple_of(((blk ^ k) * own + row) * piece, lane)
            gain_all[:, pl.ds(first, piece)] = gains[row : row + 1]
    queries = query_all[...].astype(bf16)
    passages = passage_all[...].astype(bf16)

    def named(dim):
        place = iota((pairs, pairs), dim)
        return (blk ^ (place // own)) * own + place % own

    here_rows, here_cols = named(0), named(1)
    at_rows = here_rows == iota((pairs, pairs), 1)
    at_cols = here_cols == iota((pairs, pairs), 0)
    lse = jnp.sum(jnp.where(at_rows, lse_ref[...], 0.0), axis=1, keepdims=True)
    pos = jnp.sum(jnp.where(at_rows, pos_ref[...], 0), axis=1, keepdims=True)
    hit = (pos == here_cols).astype(f32)
    coef = (jnp.exp(logit_scale * dot_t(queries, passages) - lse) - hit).astype(bf16)
    query_grad_ref[...] = (logit_scale * dot(coef, passages))[:own].astype(bf16)
    same = iota((pairs, pairs), 0) == iota((pairs, pairs), 1)
    lse = jnp.sum(jnp.where(same, lse, 0.0), axis=0, keepdims=True)
    pos = jnp.sum(jnp.where(same, pos, 0), axis=0, keepdims=True)
    hit = (pos == here_rows).astype(f32)
    turned = (jnp.exp(logit_scale * dot_t(passages, queries) - lse) - hit).astype(bf16)
    turned = dot(at_cols.astype(f32).astype(bf16), turned).astype(bf16)
    pass_grad = logit_scale * dot(turned, queries)
    low_ref[:, :features] = (gain_all[...] * pass_grad).astype(bf16)
    row = iota((pairs, lane), 0)
    tokens = dest_ref.shape[1]
    table = jnp.zeros((pairs, lane), f32)
    for n in range(-(-tokens // lane)):
        some = dest_ref[:, n * lane : min(tokens, (n + 1) * lane)].astype(f32)
        table = jnp.where(row == n, widen(some), table)
    table = jnp.where(row == -(-tokens // lane), widen(len_ref[...].astype(f32)), table)
    low_ref[:, features:] = table.astype(bf16)


def widen(row):
    short = lane - row.shape[1]
    return jnp.concatenate([row, jnp.zeros((1, short), f32)], axis=1) if short else row


def group_part(parts, row_lse, positive, token_lengths, destination, features, blk):
    own = parts[0].shape[0]
    pairs = row_lse.shape[0]
    return pl.pallas_call(
        lambda *refs: group_body(pairs // own, *refs),
        in_specs=[pl.BlockSpec(memory_space=pltpu.SMEM)]
        + [pl.BlockSpec(memory_space=pltpu.VMEM)] * (len(parts) + 4),
        out_specs=[pl.BlockSpec(memory_space=pltpu.VMEM)] * 2,
        out_shape=[
            jax.ShapeDtypeStruct((own, features), bf16),
            jax.ShapeDtypeStruct((pairs, features + lane), bf16),
        ],
        scratch_shapes=[
            pltpu.VMEM((pairs, features), f32),
            pltpu.VMEM((pairs, features), f32),
            pltpu.VMEM((1, features), f32),
        ],
        compiler_params=params(),
        cost_estimate=cost(8 * pairs * pairs * features, 8 * pairs * features),
    )(
        blk[None],
        *parts,
        row_lse[None],
        positive[None],
        destination.reshape(1, -1),
        token_lengths,
    )


def earlier_of(tokens):
    return (iota((tokens, tokens), 0) < iota((tokens, tokens), 1)).astype(bf16)


def pack_body(terms, wide_ref, dest_ref, own_ref, *rest):
    outs = rest[terms:]
    groups, slots = len(outs), outs[0].shape[0]
    tokens = dest_ref.shape[1]
    stride = -(-slots // 16) * 16
    hidden = own_ref[...]
    for term in rest[:terms]:
        hidden = hidden + term[...].astype(f32)
    partner = dest_ref[...] ^ wide_ref[0]
    hit = (partner == iota((groups, tokens), 0)).astype(f32)
    rank = dot(hit.astype(bf16), earlier_of(tokens))
    rank = jnp.sum(rank * hit, axis=0, keepdims=True).astype(i32)
    place = iota((groups * stride, tokens), 0) == partner * stride + rank
    packed = dot(place.astype(f32).astype(bf16), hidden.astype(bf16)).astype(bf16)
    for k in range(groups):
        outs[k][...] = packed[k * stride : k * stride + slots]


def pack(wide, destination, own, terms, groups, slots):
    tokens, width = own.shape
    tile = tile_of(width, 512)
    column_spec = pl.BlockSpec((tokens, tile), lambda j, g: (0, j))
    return pl.pallas_call(
        lambda *refs: pack_body(len(terms), *refs),
        grid_spec=pltpu.PrefetchScalarGridSpec(
            num_scalar_prefetch=1,
            grid=(width // tile,),
            in_specs=[pl.BlockSpec((1, tokens), lambda j, g: (0, 0))]
            + [column_spec] * (1 + len(terms)),
            out_specs=[pl.BlockSpec((slots, tile), lambda j, g: (0, j))] * groups,
        ),
        out_shape=[jax.ShapeDtypeStruct((slots, width), bf16)] * groups,
        compiler_params=params(),
        cost_estimate=cost(4 * groups * slots * tokens * width, 10 * tokens * width),
    )(wide[None], destination.reshape(1, tokens), own, *terms)


def assemble_body(wide_ref, *refs):
    parts, out_ref = refs[:-1], refs[-1]
    slots = parts[0].shape[0]
    rows = out_ref.shape[0]
    row, column = iota((rows, slots), 0), iota((rows, slots), 1)
    total = 0.0
    for k, part in enumerate(parts):
        group = wide_ref[0] ^ k
        place = (row == group * slots + column).astype(f32).astype(bf16)
        total = total + dot(place, part[...])
    out_ref[...] = total.astype(bf16)


def assemble(wide, parts):
    slots, width = parts[0].shape
    rows = slots * len(parts)
    return pl.pallas_call(
        assemble_body,
        in_specs=[pl.BlockSpec(memory_space=pltpu.SMEM)]
        + [pl.BlockSpec(memory_space=pltpu.VMEM)] * len(parts),
        out_specs=pl.BlockSpec(memory_space=pltpu.VMEM),
        out_shape=jax.ShapeDtypeStruct((rows, width), bf16),
        compiler_params=params(),
        cost_estimate=cost(2 * rows * rows * width, 4 * rows * width),
    )(wide[None], *parts)


def slots_body(groups, slots, wide_ref, table_ref, hot_ref, share_ref):
    rows, columns = hot_ref.shape
    pairs = columns // groups
    blocks = -(-slots * groups * 2 // 3 // lane)
    table = table_ref[...]

    def tables(n):
        at = iota((groups, columns), 1) == iota((groups, columns), 0) * pairs + n
        return dot(at.astype(f32).astype(bf16), table)

    spread = (iota((rows, groups), 0) // slots == iota((rows, groups), 1)).astype(f32).astype(bf16)
    lengths = tables(blocks)
    upto = (iota((lane, lane), 0) <= iota((lane, lane), 1)).astype(f32).astype(bf16)
    ends = dot(lengths.astype(bf16), upto)
    slot = iota((rows, lane), 0) % slots
    before = jnp.zeros((groups, 1), f32)
    taken = jnp.zeros((rows, 1), f32)
    for n in range(blocks):
        token = iota((groups, lane), 1) + n * lane
        hit = (tables(n).astype(i32) == wide_ref[0]) & (token < slots * groups * 2 // 3)
        count = hit.astype(f32)
        rank = before + dot(count.astype(bf16), earlier_of(lane))
        before = before + jnp.sum(count, axis=1, keepdims=True)
        passage = jnp.ones((groups, lane), f32)
        for pair in range(pairs):
            passage = passage + (token.astype(f32) >= ends[:, pair : pair + 1]).astype(f32)
        code = jnp.where(hit, passage, 0.0)
        rank_rows = dot(spread, rank.astype(bf16)).astype(i32)
        code_rows = dot(spread, code.astype(bf16))
        taken = taken + jnp.sum(
            jnp.where(rank_rows == slot, code_rows, 0.0), axis=1, keepdims=True
        )
    taken = taken.astype(i32)
    column = iota((rows, columns), 1)
    first = iota((rows, columns), 0) // slots * pairs
    hot = (taken > 0) & (column == first + taken - 1)
    hot_ref[...] = hot.astype(f32).astype(bf16)
    length_rows = dot(spread, lengths.astype(bf16))
    length = jnp.where(iota((rows, lane), 1) == taken - 1, length_rows, 0.0)
    length = jnp.sum(length, axis=1, keepdims=True)
    share_ref[...] = jnp.where(taken > 0, 1.0 / jnp.maximum(length, 1.0), 0.0)


def slot_passages(wide, low, features, groups, slots, rows):
    columns = low.shape[0]
    return pl.pallas_call(
        lambda *refs: slots_body(groups, slots, *refs),
        grid=(1,),
        in_specs=[
            pl.BlockSpec(memory_space=pltpu.SMEM),
            pl.BlockSpec((columns, lane), lambda j: (0, features // lane)),
        ],
        out_specs=[
            pl.BlockSpec((rows, columns), lambda j: (0, 0)),
            pl.BlockSpec((rows, 1), lambda j: (0, 0)),
        ],
        out_shape=[
            jax.ShapeDtypeStruct((rows, columns), bf16),
            jax.ShapeDtypeStruct((rows, 1), f32),
        ],
        compiler_params=params(),
        cost_estimate=cost(4 * rows * groups * lane, 2 * rows * columns),
    )(wide[None], low)


def low_act_body(low_ref, w_hbm, out_ref, weights, sems):
    count, tile, _ = weights.shape

    def weight_copy(t):
        rows = pl.ds(pl.multiple_of(t * tile, tile), tile)
        return pltpu.make_async_copy(w_hbm.at[rows], weights.at[t], sems.at[t])

    for t in range(count):
        weight_copy(t).start()

    @pl.loop(0, count)
    def _(t):
        weight_copy(t).wait()
        rows = pl.ds(pl.multiple_of(t * tile, tile), tile)
        out_ref[rows] = dot_t(weights[t], low_ref[...]).astype(bf16)


def low_activations(low, features, w_down):
    pairs = low.shape[0]
    depth = w_down.shape[0]
    tile = tile_of(depth, 512)
    count = depth // tile
    return pl.pallas_call(
        low_act_body,
        grid=(1,),
        in_specs=[
            pl.BlockSpec((pairs, features), lambda j: (0, 0)),
            pl.BlockSpec(memory_space=pl.ANY),
        ],
        out_specs=pl.BlockSpec((depth, pairs), lambda j: (0, 0)),
        out_shape=jax.ShapeDtypeStruct((depth, pairs), bf16),
        scratch_shapes=[
            pltpu.VMEM((count, tile, features), bf16),
            pltpu.SemaphoreType.DMA((count,)),
        ],
        compiler_params=params(),
        cost_estimate=cost(2 * pairs * depth * features, 2 * depth * features),
    )(low, w_down)


def statistics(hids, lows):
    squares, cross = 0.0, 0.0
    for hid_ref, low_ref in zip(hids, lows):
        hid = hid_ref[...].astype(f32)
        squares = squares + jnp.sum(hid * hid, axis=1, keepdims=True)
        cross = cross + dot_t(hid_ref[...], low_ref[...])
    return squares, cross


def weight_copies(places_ref, w_hbm, weights, sems):
    count, tile, across = weights.shape
    groups = sems.shape[1]
    width = across // groups

    def copies(t):
        rows = pl.ds(pl.multiple_of(t * tile, tile), tile)
        return [
            pltpu.make_async_copy(
                w_hbm.at[rows, pl.ds(pl.multiple_of(places_ref[n] * width, lane), width)],
                weights.at[t, :, n * width : (n + 1) * width],
                sems.at[t, n],
            )
            for n in range(groups)
        ]

    return copies


def back_body(count, places_ref, *refs):
    hids, lows, w_hbm, refs = refs[:count], refs[count : 2 * count], refs[2 * count], refs[2 * count + 1 :]
    acc_hbm, squares_ref, cross_ref, hid, weights, acc, sems, out_sems = refs
    copies = weight_copies(places_ref, w_hbm, weights, sems)
    rows, width = hids[0].shape

    def acc_out(t):
        return pltpu.make_async_copy(acc.at[t], acc_hbm.at[t], out_sems.at[t])

    for t in range(weights.shape[0]):
        for copy in copies(t):
            copy.start()
    for n in range(count):
        hid[:rows, n * width : (n + 1) * width] = hids[n][...]
    hid[rows:] = jnp.zeros((hid.shape[0] - rows, count * width), bf16)
    squares_ref[...], cross_ref[...] = statistics(hids, lows)

    @pl.loop(0, weights.shape[0])
    def _(t):
        for copy in copies(t):
            copy.wait()
        acc[t] = dot_t(weights[t], hid[...])
        acc_out(t).start()

    @pl.loop(0, weights.shape[0])
    def _(t):
        acc_out(t).wait()


def back(places, pieces, w_down, low, padded):
    count = len(pieces)
    rows, width = pieces[0].shape
    depth = w_down.shape[0]
    pairs = low.shape[0]
    tile = tile_of(depth, 512)
    tiles = depth // tile
    anywhere = pl.BlockSpec(memory_space=pl.ANY)
    return pl.pallas_call(
        lambda *refs: back_body(count, *refs),
        grid_spec=pltpu.PrefetchScalarGridSpec(
            num_scalar_prefetch=1,
            grid=(1,),
            in_specs=[pl.BlockSpec((rows, width), lambda j, g: (0, 0))] * count
            + [pl.BlockSpec((pairs, width), lambda j, g, n=n: (0, g[n])) for n in range(count)]
            + [anywhere],
            out_specs=[
                anywhere,
                pl.BlockSpec((rows, 1), lambda j, g: (0, 0)),
                pl.BlockSpec((rows, pairs), lambda j, g: (0, 0)),
            ],
            scratch_shapes=[
                pltpu.VMEM((padded, count * width), bf16),
                pltpu.VMEM((tiles, tile, count * width), bf16),
                pltpu.VMEM((tiles, tile, padded), f32),
                pltpu.SemaphoreType.DMA((tiles, count)),
                pltpu.SemaphoreType.DMA((tiles,)),
            ],
        ),
        out_shape=[
            jax.ShapeDtypeStruct((tiles, tile, padded), f32),
            jax.ShapeDtypeStruct((rows, 1), f32),
            jax.ShapeDtypeStruct((rows, pairs), f32),
        ],
        compiler_params=params(),
        cost_estimate=cost(2 * rows * depth * width * count, 2 * depth * width * count),
    )(places, *pieces, *[low] * count, w_down)


def finish_body(features, count, places_ref, *refs):
    hids, refs = refs[:count], refs[count:]
    low_ref, w_hbm, acc_hbm, squares_ref, cross_ref, hot_ref, share_ref, low_act_ref = refs[:8]
    own_ref, own_low_ref, gain_ref, act_hbm, resid_out, normed_out = refs[8:14]
    hid, weights, acc, act, sems, in_sems, out_sems = refs[14:]
    tiles, tile, _ = weights.shape
    rows = own_ref.shape[0]
    padded = hid.shape[0]
    copies = weight_copies(places_ref, w_hbm, weights, sems)

    def acc_in(t):
        return pltpu.make_async_copy(acc_hbm.at[t], acc.at[t], in_sems.at[t])

    def act_out(t):
        columns = pl.ds(pl.multiple_of(t * tile, lane), tile)
        return pltpu.make_async_copy(act.at[t], act_hbm.at[:, columns], out_sems.at[t])

    for t in range(tiles):
        for copy in copies(t):
            copy.start()
        acc_in(t).start()
    part = rows // count
    for n in range(count):
        hid[n * part : (n + 1) * part] = hids[n][...]
    hid[rows:] = jnp.zeros((padded - rows, hid.shape[1]), bf16)
    squares, cross = statistics([hid.at[:rows]], [low_ref])
    hot = hot_ref[:rows]
    share = share_ref[:rows]
    inner = jnp.sum((cross_ref[...] + cross) * hot.astype(f32), axis=1, keepdims=True) * share
    inv_rms = lax.rsqrt((squares_ref[...] + squares) / features + norm_eps)
    lead = inv_rms * share
    pull = inv_rms * inv_rms * inv_rms * inner / features
    own = own_ref[...].astype(f32)
    resid_out[...] = (lead * dot(hot, own_low_ref[...]) - own * pull).astype(bf16)
    normed_out[...] = (gain_ref[...] * own * inv_rms).astype(bf16)
    same = iota((rows, padded), 0) == iota((rows, padded), 1)
    lead = jnp.sum(jnp.where(same, lead, 0.0), axis=0, keepdims=True)
    pull = jnp.sum(jnp.where(same, pull, 0.0), axis=0, keepdims=True)

    @pl.loop(0, tiles)
    def _(t):
        at = pl.ds(pl.multiple_of(t * tile, tile), tile)
        low_act = dot_t(low_act_ref[at], hot_ref[...])
        for copy in copies(t):
            copy.wait()
        total = dot_t(weights[t], hid[...])
        acc_in(t).wait()
        turned = (lead * low_act - pull * (total + acc[t])).astype(bf16).T
        act[t] = turned[:rows]
        act_out(t).start()

    @pl.loop(0, tiles)
    def _(t):
        act_out(t).wait()


def finish(places, pieces, w_down, low, before, hot, share, low_act, own, gain):
    count = len(pieces)
    rows, width = own.shape
    depth, features = w_down.shape
    padded, pairs = hot.shape
    tile = tile_of(depth, 512)
    tiles = depth // tile
    anywhere = pl.BlockSpec(memory_space=pl.ANY)

    def whole(shape):
        return pl.BlockSpec(shape, lambda j, g: (0, 0))

    return pl.pallas_call(
        lambda *refs: finish_body(features, count, *refs),
        grid_spec=pltpu.PrefetchScalarGridSpec(
            num_scalar_prefetch=1,
            grid=(1,),
            in_specs=[whole((rows // count, width))] * count
            + [
                pl.BlockSpec((pairs, width), lambda j, g: (0, g[0])),
                anywhere,
                anywhere,
                whole((rows, 1)),
                whole((rows, pairs)),
                whole((padded, pairs)),
                whole((padded, 1)),
                whole((depth, pairs)),
                whole((rows, width)),
                pl.BlockSpec((pairs, width), lambda j, g: (0, g[1])),
                whole((1, width)),
            ],
            out_specs=[anywhere, whole((rows, width)), whole((rows, width))],
            scratch_shapes=[
                pltpu.VMEM((padded, width), bf16),
                pltpu.VMEM((tiles, tile, width), bf16),
                pltpu.VMEM((tiles, tile, padded), f32),
                pltpu.VMEM((tiles, rows, tile), bf16),
                pltpu.SemaphoreType.DMA((tiles, 1)),
                pltpu.SemaphoreType.DMA((tiles,)),
                pltpu.SemaphoreType.DMA((tiles,)),
            ],
        ),
        out_shape=[
            jax.ShapeDtypeStruct((rows, depth), bf16),
            jax.ShapeDtypeStruct((rows, width), bf16),
            jax.ShapeDtypeStruct((rows, width), bf16),
        ],
        compiler_params=params(),
        cost_estimate=cost(2 * rows * depth * width, 2 * depth * width + 6 * rows * depth),
    )(places, *pieces, low, w_down, *before, hot, share, low_act, own, low, gain)


def low_rank_shards(
    query_emb,
    passage_emb,
    row_lse,
    positive,
    token_lengths,
    destination,
    mlp_act,
    resid,
    w_down,
    gain,
):
    wide_count = lax.axis_size("wide")
    blk, wide = lax.axis_index("blk"), lax.axis_index("wide")
    tok_count, width = resid.shape
    features = w_down.shape[1]
    pairs = row_lse.shape[0]
    slot_count = 3 * tok_count // (2 * wide_count)
    rows = wide_count * slot_count

    both = payload(query_emb, passage_emb, gain)
    parts = [both] + [swap(both, k) for k in (1, 2, 3)]
    first_term = project((blk ^ 3)[None], mlp_act, w_down, width)
    arrived = [swap(first_term, 3)]
    parts = after(first_term, *parts)[1:]
    query_grad, low_own = group_part(
        parts, row_lse, positive, token_lengths, destination, features, blk
    )
    mlp_act = after(low_own, mlp_act)[1]
    for k in (1, 2):
        arrived.append(swap(project((blk ^ k)[None], mlp_act, w_down, width), k))
    own_term = project(blk[None], mlp_act, w_down, width, resid)

    low = lax.all_gather(low_own, "wide", axis=0, tiled=True)
    packed = pack(wide, destination, own_term, arrived, wide_count, slot_count)
    routed = [packed[k] if k == 0 else swap(packed[k], k, "wide") for k in range(wide_count)]
    own = assemble(wide, routed)

    padded = -(-rows // lane) * lane
    low_act = low_activations(low, features, w_down)
    hot, share = slot_passages(wide, low, features, wide_count, slot_count, padded)

    beside, above = swap(own, 1), swap(own, 2)
    top = swap(beside[: rows // 2], 2)
    bottom = swap(above[rows // 2 :], 1)
    low_act, hot, share, beside, above = lax.optimization_barrier(
        (low_act, hot, share, beside, above)
    )
    totals = back(blk ^ jnp.arange(3, dtype=i32), [own, beside, above], w_down, low, padded)
    act_grad, resid_grad, normed_out = finish(
        jnp.stack([blk ^ 3, blk]),
        [top, bottom],
        w_down,
        low,
        totals,
        hot,
        share,
        low_act,
        own,
        gain[None],
    )
    return (query_grad, resid_grad, act_grad, normed_out)


def coefficients(scores, lse_part, pos_part):
    columns = lax.broadcasted_iota(jnp.int32, scores.shape, 1)
    target = (pos_part[:, None] == columns).astype(jnp.float32)
    return (jnp.exp(scores - lse_part[:, None]) - target).astype(jnp.bfloat16)


def place_rows(destination, wide_count, slot_count):
    tok_count = destination.shape[0]
    dest_hot = (destination == lax.broadcasted_iota(jnp.int32, (tok_count, wide_count), 1)).astype(
        bf16
    )
    token = lax.iota(jnp.int32, tok_count)
    earlier = (token[None, :] < token[:, None]).astype(bf16)
    rank_of = jnp.dot(earlier, dest_hot, preferred_element_type=f32)
    slot_of = jnp.sum(rank_of * dest_hot.astype(f32), axis=1).astype(jnp.int32)
    slot_of = slot_of + destination[:, 0] * slot_count
    return (
        lax.broadcasted_iota(jnp.int32, (wide_count * slot_count, tok_count), 0) == slot_of[None, :]
    ).astype(bf16)


def row_shards(
    query_emb,
    passage_emb,
    row_lse,
    positive,
    token_lengths,
    destination,
    mlp_act,
    resid,
    w_down,
    gain,
):
    pair_rows = query_emb.shape[0]
    tok_count, feat_width = resid.shape
    features = w_down.shape[1]
    blk_index = lax.axis_index("blk")
    wide_count = lax.axis_size("wide")
    slot_count = 3 * tok_count // (2 * wide_count)
    offset = blk_index * feat_width
    query_all = lax.all_gather(query_emb, "blk", axis=0, tiled=True)
    passage_all = lax.all_gather(passage_emb, "blk", axis=0, tiled=True)
    scores = logit_scale * jnp.dot(query_all, passage_all.T, preferred_element_type=f32)
    coef_full = coefficients(scores, row_lse, positive)
    own_coef = lax.dynamic_slice_in_dim(coef_full, blk_index * pair_rows, pair_rows, 0)
    query_grad = (
        logit_scale * jnp.dot(own_coef, passage_all, preferred_element_type=f32)
    ).astype(bf16)
    query_cols = lax.dynamic_slice_in_dim(query_all, offset, feat_width, 1)
    grad_cols = logit_scale * lax.dot_general(
        query_cols, coef_full, (((0,), (0,)), ((), ())), preferred_element_type=f32
    )
    lengths_row = token_lengths[0]
    starts = jnp.cumsum(lengths_row) - lengths_row
    positions = lax.broadcasted_iota(jnp.int32, (tok_count, lengths_row.shape[0]), 0)
    member = (positions >= starts[None, :]) & (positions < (starts + lengths_row)[None, :])
    weights = member.astype(f32) * (1.0 / lengths_row.astype(f32))[None, :]
    tok_grad = lax.dot_general(
        weights,
        grad_cols,
        (((1,), (1,)), ((), ())),
        precision=lax.Precision.HIGHEST,
        preferred_element_type=f32,
    ).astype(bf16)
    terms = jnp.dot(mlp_act, w_down, preferred_element_type=f32)
    own = lax.dynamic_slice_in_dim(terms, offset, feat_width, 1) + resid.astype(f32)
    terms = lax.dynamic_update_slice_in_dim(terms, own, offset, 1)
    hidden = lax.psum_scatter(terms.astype(bf16), "blk", scatter_dimension=1, tiled=True)
    placer = place_rows(destination, wide_count, slot_count)
    payload = jnp.concatenate([hidden, tok_grad], axis=1)
    packed = jnp.dot(placer, payload, preferred_element_type=f32).astype(bf16)
    packed = packed.reshape(wide_count, slot_count, 2 * feat_width)
    rows = lax.all_to_all(packed, "wide", split_axis=0, concat_axis=0, tiled=True).reshape(
        wide_count * slot_count, 2 * feat_width
    )
    hidden = rows[:, :feat_width].astype(f32)
    gained = gain[None, :] * rows[:, feat_width:].astype(f32)
    squares, inner_sum = lax.psum(
        (jnp.sum(hidden * hidden, axis=1), jnp.sum(gained * hidden, axis=1)), "blk"
    )
    inv_rms = lax.rsqrt(squares / features + norm_eps)[:, None]
    normed = (gain[None, :] * hidden * inv_rms).astype(bf16)
    resid_back = (
        inv_rms * gained - hidden * (inv_rms * inv_rms * inv_rms) * inner_sum[:, None] / features
    ).astype(bf16)
    act_back = dot_t(lax.all_gather(resid_back, "blk", axis=1, tiled=True), w_down)
    return (query_grad, resid_back, act_back.astype(bf16), normed)


def solution(mesh):
    blk_count, wide_count = mesh.shape["blk"], mesh.shape["wide"]

    def shards(*operands):
        pairs, tok_count = operands[2].shape[0], operands[7].shape[0]
        low_rank = 2 * wide_count * pairs <= 3 * tok_count
        per_pair = tok_count // pairs
        aligned = operands[9].shape[0] % (lane * operands[0].shape[0]) == 0
        if low_rank and blk_count == 4 and aligned and per_pair * pairs == tok_count and wide_count & (wide_count - 1) == 0:
            return low_rank_shards(*operands)
        return row_shards(*operands)

    return jax.shard_map(
        shards,
        mesh=mesh,
        in_specs=(
            P(("wide", "blk"), None),
            P(("wide", "blk"), None),
            P("wide"),
            P("wide"),
            P("wide", None),
            P("wide", None),
            P("wide", "blk"),
            P("wide", "blk"),
            P("blk", None),
            P("blk"),
        ),
        out_specs=(P(("wide", "blk"), None), P("wide", "blk"), P("wide", "blk"), P("wide", "blk")),
        check_vma=False,
    )
```

```python
import jax
import jax.numpy as jnp
from jax import lax
from jax.experimental import pallas as pl
from jax.experimental.pallas import tpu as pltpu
from jax.sharding import PartitionSpec as P

logit_scale = 24.0
norm_eps = 1e-06
f32 = jnp.float32
bf16 = jnp.bfloat16
i32 = jnp.int32
lane = 128
kernel_vmem = 46 * 1024 * 1024


def params():
    return pltpu.CompilerParams(vmem_limit_bytes=kernel_vmem)


def cost(flops, nbytes):
    return pl.CostEstimate(flops=flops, bytes_accessed=nbytes, transcendentals=0)


def tile_of(extent, most):
    tile = most
    while extent % tile:
        tile //= 2
    return tile


def iota(shape, dim):
    return lax.broadcasted_iota(i32, shape, dim)


def dot(left, right):
    return jnp.dot(left, right, preferred_element_type=f32)


def dot_t(left, right):
    return lax.dot_general(left, right, (((1,), (1,)), ((), ())), preferred_element_type=f32)


def swap(rows, k, axis="blk"):
    return lax.ppermute(rows, axis, [(i, i ^ k) for i in range(lax.axis_size(axis))])


def after(first, *later):
    return lax.optimization_barrier((first, *later))


def project_body(has_resid, group_ref, act_hbm, w_hbm, *refs):
    out_ref, act, weights, act_sem, sems = refs[has_resid:]
    width = out_ref.shape[1]
    count, _, tile = weights.shape
    first = group_ref[0] * width

    def weight_copy(i):
        columns = pl.ds(pl.multiple_of(first + i * tile, lane), tile)
        return pltpu.make_async_copy(w_hbm.at[:, columns], weights.at[i], sems.at[i])

    act_copy = pltpu.make_async_copy(act_hbm, act, act_sem)
    act_copy.start()
    for i in range(count):
        weight_copy(i).start()
    act_copy.wait()

    @pl.loop(0, count)
    def _(i):
        weight_copy(i).wait()
        columns = pl.ds(pl.multiple_of(i * tile, lane), tile)
        term = dot(act[...], weights[i])
        if has_resid:
            term = term + refs[0][:, columns].astype(f32)
        out_ref[:, columns] = term.astype(out_ref.dtype)


def project(group, act, w_down, width, resid=None):
    rows, depth = act.shape
    tile = tile_of(width, 256)
    count = width // tile
    own = [] if resid is None else [resid]
    return pl.pallas_call(
        lambda *refs: project_body(len(own), *refs),
        in_specs=[pl.BlockSpec(memory_space=pltpu.SMEM)]
        + [pl.BlockSpec(memory_space=pl.ANY)] * 2
        + [pl.BlockSpec(memory_space=pltpu.VMEM)] * len(own),
        out_specs=pl.BlockSpec(memory_space=pltpu.VMEM),
        out_shape=jax.ShapeDtypeStruct((rows, width), f32 if own else bf16),
        scratch_shapes=[
            pltpu.VMEM((rows, depth), bf16),
            pltpu.VMEM((count, depth, tile), bf16),
            pltpu.SemaphoreType.DMA,
            pltpu.SemaphoreType.DMA((count,)),
        ],
        compiler_params=params(),
        cost_estimate=cost(2 * rows * depth * width, 2 * depth * width + 2 * rows * depth),
    )(group, act, w_down, *own)


def payload_body(query_ref, passage_ref, gain_ref, out_ref, gains):
    own, features = query_ref.shape
    piece = gains.shape[1]
    for row in range(own):
        gains[row : row + 1] = gain_ref[:, row * piece : (row + 1) * piece]
    gain = gains[...]
    high = gain.astype(bf16)
    out_ref[:, :features] = query_ref[...]
    out_ref[:, features : 2 * features] = passage_ref[...]
    out_ref[:, 2 * features : 2 * features + piece] = high
    out_ref[:, 2 * features + piece :] = (gain - high.astype(f32)).astype(bf16)


def payload(query_emb, passage_emb, gain):
    own, features = query_emb.shape
    piece = gain.shape[0] // own
    return pl.pallas_call(
        payload_body,
        out_shape=jax.ShapeDtypeStruct((own, 2 * features + 2 * piece), bf16),
        scratch_shapes=[pltpu.VMEM((own, piece), f32)],
        compiler_params=params(),
        cost_estimate=cost(own * features, 8 * own * features),
    )(query_emb, passage_emb, gain[None])


def group_body(count, blk_ref, *refs):
    parts, refs = refs[:count], refs[count:]
    lse_ref, pos_ref, dest_ref, len_ref = refs[:4]
    query_grad_ref, low_ref, query_all, passage_all, gain_all = refs[4:]
    own, features = query_grad_ref.shape
    pairs = own * count
    piece = features // pairs
    blk = blk_ref[0]
    for k in range(count):
        query_all[k * own : (k + 1) * own] = parts[k][:, :features].astype(f32)
        passage_all[k * own : (k + 1) * own] = parts[k][:, features : 2 * features].astype(f32)
        gains = parts[k][:, 2 * features : 2 * features + piece].astype(f32)
        gains = gains + parts[k][:, 2 * features + piece :].astype(f32)
        for row in range(own):
            first = pl.multiple_of(((blk ^ k) * own + row) * piece, lane)
            gain_all[:, pl.ds(first, piece)] = gains[row : row + 1]
    queries = query_all[...].astype(bf16)
    passages = passage_all[...].astype(bf16)

    def named(dim):
        place = iota((pairs, pairs), dim)
        return (blk ^ (place // own)) * own + place % own

    here_rows, here_cols = named(0), named(1)
    at_rows = here_rows == iota((pairs, pairs), 1)
    at_cols = here_cols == iota((pairs, pairs), 0)
    lse = jnp.sum(jnp.where(at_rows, lse_ref[...], 0.0), axis=1, keepdims=True)
    pos = jnp.sum(jnp.where(at_rows, pos_ref[...], 0), axis=1, keepdims=True)
    hit = (pos == here_cols).astype(f32)
    coef = (jnp.exp(logit_scale * dot_t(queries, passages) - lse) - hit).astype(bf16)
    query_grad_ref[...] = (logit_scale * dot(coef, passages))[:own].astype(bf16)
    same = iota((pairs, pairs), 0) == iota((pairs, pairs), 1)
    lse = jnp.sum(jnp.where(same, lse, 0.0), axis=0, keepdims=True)
    pos = jnp.sum(jnp.where(same, pos, 0), axis=0, keepdims=True)
    hit = (pos == here_rows).astype(f32)
    turned = (jnp.exp(logit_scale * dot_t(passages, queries) - lse) - hit).astype(bf16)
    turned = dot(at_cols.astype(f32).astype(bf16), turned).astype(bf16)
    pass_grad = logit_scale * dot(turned, queries)
    low_ref[:, :features] = (gain_all[...] * pass_grad).astype(bf16)
    row = iota((pairs, lane), 0)
    tokens = dest_ref.shape[1]
    table = jnp.zeros((pairs, lane), f32)
    for n in range(-(-tokens // lane)):
        some = dest_ref[:, n * lane : min(tokens, (n + 1) * lane)].astype(f32)
        table = jnp.where(row == n, widen(some), table)
    table = jnp.where(row == -(-tokens // lane), widen(len_ref[...].astype(f32)), table)
    low_ref[:, features:] = table.astype(bf16)


def widen(row):
    short = lane - row.shape[1]
    return jnp.concatenate([row, jnp.zeros((1, short), f32)], axis=1) if short else row


def group_part(parts, row_lse, positive, token_lengths, destination, features, blk):
    own = parts[0].shape[0]
    pairs = row_lse.shape[0]
    return pl.pallas_call(
        lambda *refs: group_body(pairs // own, *refs),
        in_specs=[pl.BlockSpec(memory_space=pltpu.SMEM)]
        + [pl.BlockSpec(memory_space=pltpu.VMEM)] * (len(parts) + 4),
        out_specs=[pl.BlockSpec(memory_space=pltpu.VMEM)] * 2,
        out_shape=[
            jax.ShapeDtypeStruct((own, features), bf16),
            jax.ShapeDtypeStruct((pairs, features + lane), bf16),
        ],
        scratch_shapes=[
            pltpu.VMEM((pairs, features), f32),
            pltpu.VMEM((pairs, features), f32),
            pltpu.VMEM((1, features), f32),
        ],
        compiler_params=params(),
        cost_estimate=cost(8 * pairs * pairs * features, 8 * pairs * features),
    )(
        blk[None],
        *parts,
        row_lse[None],
        positive[None],
        destination.reshape(1, -1),
        token_lengths,
    )


def earlier_of(tokens):
    return (iota((tokens, tokens), 0) < iota((tokens, tokens), 1)).astype(bf16)


def pack_body(terms, wide_ref, dest_ref, own_ref, *rest):
    outs = rest[terms:]
    groups, slots = len(outs), outs[0].shape[0]
    tokens = dest_ref.shape[1]
    stride = -(-slots // 16) * 16
    hidden = own_ref[...]
    for term in rest[:terms]:
        hidden = hidden + term[...].astype(f32)
    partner = dest_ref[...] ^ wide_ref[0]
    hit = (partner == iota((groups, tokens), 0)).astype(f32)
    rank = dot(hit.astype(bf16), earlier_of(tokens))
    rank = jnp.sum(rank * hit, axis=0, keepdims=True).astype(i32)
    place = iota((groups * stride, tokens), 0) == partner * stride + rank
    packed = dot(place.astype(f32).astype(bf16), hidden.astype(bf16)).astype(bf16)
    for k in range(groups):
        outs[k][...] = packed[k * stride : k * stride + slots]


def pack(wide, destination, own, terms, groups, slots):
    tokens, width = own.shape
    tile = tile_of(width, 512)
    column_spec = pl.BlockSpec((tokens, tile), lambda j, g: (0, j))
    return pl.pallas_call(
        lambda *refs: pack_body(len(terms), *refs),
        grid_spec=pltpu.PrefetchScalarGridSpec(
            num_scalar_prefetch=1,
            grid=(width // tile,),
            in_specs=[pl.BlockSpec((1, tokens), lambda j, g: (0, 0))]
            + [column_spec] * (1 + len(terms)),
            out_specs=[pl.BlockSpec((slots, tile), lambda j, g: (0, j))] * groups,
        ),
        out_shape=[jax.ShapeDtypeStruct((slots, width), bf16)] * groups,
        compiler_params=params(),
        cost_estimate=cost(4 * groups * slots * tokens * width, 10 * tokens * width),
    )(wide[None], destination.reshape(1, tokens), own, *terms)


def assemble_body(wide_ref, *refs):
    parts, out_ref = refs[:-1], refs[-1]
    slots = parts[0].shape[0]
    rows = out_ref.shape[0]
    row, column = iota((rows, slots), 0), iota((rows, slots), 1)
    total = 0.0
    for k, part in enumerate(parts):
        group = wide_ref[0] ^ k
        place = (row == group * slots + column).astype(f32).astype(bf16)
        total = total + dot(place, part[...])
    out_ref[...] = total.astype(bf16)


def assemble(wide, parts):
    slots, width = parts[0].shape
    rows = slots * len(parts)
    return pl.pallas_call(
        assemble_body,
        in_specs=[pl.BlockSpec(memory_space=pltpu.SMEM)]
        + [pl.BlockSpec(memory_space=pltpu.VMEM)] * len(parts),
        out_specs=pl.BlockSpec(memory_space=pltpu.VMEM),
        out_shape=jax.ShapeDtypeStruct((rows, width), bf16),
        compiler_params=params(),
        cost_estimate=cost(2 * rows * rows * width, 4 * rows * width),
    )(wide[None], *parts)


def slots_body(groups, slots, wide_ref, table_ref, hot_ref, share_ref):
    rows, columns = hot_ref.shape
    pairs = columns // groups
    blocks = -(-slots * groups * 2 // 3 // lane)
    table = table_ref[...]

    def tables(n):
        at = iota((groups, columns), 1) == iota((groups, columns), 0) * pairs + n
        return dot(at.astype(f32).astype(bf16), table)

    spread = (iota((rows, groups), 0) // slots == iota((rows, groups), 1)).astype(f32).astype(bf16)
    lengths = tables(blocks)
    upto = (iota((lane, lane), 0) <= iota((lane, lane), 1)).astype(f32).astype(bf16)
    ends = dot(lengths.astype(bf16), upto)
    slot = iota((rows, lane), 0) % slots
    before = jnp.zeros((groups, 1), f32)
    taken = jnp.zeros((rows, 1), f32)
    for n in range(blocks):
        token = iota((groups, lane), 1) + n * lane
        hit = (tables(n).astype(i32) == wide_ref[0]) & (token < slots * groups * 2 // 3)
        count = hit.astype(f32)
        rank = before + dot(count.astype(bf16), earlier_of(lane))
        before = before + jnp.sum(count, axis=1, keepdims=True)
        passage = jnp.ones((groups, lane), f32)
        for pair in range(pairs):
            passage = passage + (token.astype(f32) >= ends[:, pair : pair + 1]).astype(f32)
        code = jnp.where(hit, passage, 0.0)
        rank_rows = dot(spread, rank.astype(bf16)).astype(i32)
        code_rows = dot(spread, code.astype(bf16))
        taken = taken + jnp.sum(
            jnp.where(rank_rows == slot, code_rows, 0.0), axis=1, keepdims=True
        )
    taken = taken.astype(i32)
    column = iota((rows, columns), 1)
    first = iota((rows, columns), 0) // slots * pairs
    hot = (taken > 0) & (column == first + taken - 1)
    hot_ref[...] = hot.astype(f32).astype(bf16)
    length_rows = dot(spread, lengths.astype(bf16))
    length = jnp.where(iota((rows, lane), 1) == taken - 1, length_rows, 0.0)
    length = jnp.sum(length, axis=1, keepdims=True)
    share_ref[...] = jnp.where(taken > 0, 1.0 / jnp.maximum(length, 1.0), 0.0)


def slot_passages(wide, low, features, groups, slots, rows):
    columns = low.shape[0]
    return pl.pallas_call(
        lambda *refs: slots_body(groups, slots, *refs),
        grid=(1,),
        in_specs=[
            pl.BlockSpec(memory_space=pltpu.SMEM),
            pl.BlockSpec((columns, lane), lambda j: (0, features // lane)),
        ],
        out_specs=[
            pl.BlockSpec((rows, columns), lambda j: (0, 0)),
            pl.BlockSpec((rows, 1), lambda j: (0, 0)),
        ],
        out_shape=[
            jax.ShapeDtypeStruct((rows, columns), bf16),
            jax.ShapeDtypeStruct((rows, 1), f32),
        ],
        compiler_params=params(),
        cost_estimate=cost(4 * rows * groups * lane, 2 * rows * columns),
    )(wide[None], low)


def low_act_body(low_ref, w_hbm, out_ref, weights, sems):
    count, tile, _ = weights.shape

    def weight_copy(t):
        rows = pl.ds(pl.multiple_of(t * tile, tile), tile)
        return pltpu.make_async_copy(w_hbm.at[rows], weights.at[t], sems.at[t])

    for t in range(count):
        weight_copy(t).start()

    @pl.loop(0, count)
    def _(t):
        weight_copy(t).wait()
        rows = pl.ds(pl.multiple_of(t * tile, tile), tile)
        out_ref[rows] = dot_t(weights[t], low_ref[...]).astype(bf16)


def low_activations(low, features, w_down):
    pairs = low.shape[0]
    depth = w_down.shape[0]
    tile = tile_of(depth, 512)
    count = depth // tile
    return pl.pallas_call(
        low_act_body,
        grid=(1,),
        in_specs=[
            pl.BlockSpec((pairs, features), lambda j: (0, 0)),
            pl.BlockSpec(memory_space=pl.ANY),
        ],
        out_specs=pl.BlockSpec((depth, pairs), lambda j: (0, 0)),
        out_shape=jax.ShapeDtypeStruct((depth, pairs), bf16),
        scratch_shapes=[
            pltpu.VMEM((count, tile, features), bf16),
            pltpu.SemaphoreType.DMA((count,)),
        ],
        compiler_params=params(),
        cost_estimate=cost(2 * pairs * depth * features, 2 * depth * features),
    )(low, w_down)


def statistics(hids, lows):
    squares, cross = 0.0, 0.0
    for hid, low_ref in zip(hids, lows):
        wide_hid = hid.astype(f32)
        squares = squares + jnp.sum(wide_hid * wide_hid, axis=1, keepdims=True)
        cross = cross + dot_t(hid, low_ref[...])
    return squares, cross


def product(hids, weights):
    total = 0.0
    for hid, w_ref in zip(hids, weights):
        total = total + dot_t(hid, w_ref[...])
    return total


def group_specs(count, rows_of_block, width, row_step):
    half = width // 2
    return [
        pl.BlockSpec(
            (rows_of_block, half), lambda j, g, n=n, side=side: (row_step * j, 2 * g[n] + side)
        )
        for n in range(count)
        for side in range(2)
    ]


def halves_of(ref):
    half = ref.shape[1] // 2
    return [ref[:, :half], ref[:, half:]]


def back_body(count, carried, places_ref, *refs):
    hids, refs = refs[:count], refs[count:]
    weights, lows, refs = refs[: 2 * count], refs[2 * count : 4 * count], refs[4 * count :]
    before, (acc_ref, squares_ref, cross_ref) = refs[:carried], refs[carried:]
    halves = [half for hid in hids for half in halves_of(hid)]

    @pl.when(pl.program_id(0) == 0)
    def _():
        squares, cross = statistics(halves, lows)
        if carried:
            squares, cross = before[1][...] + squares, before[2][...] + cross
        squares_ref[...], cross_ref[...] = squares, cross

    total = product(halves, weights)
    acc_ref[...] = before[0][...] + total if carried else total


def carried_specs(rows, pairs, tile):
    return [
        pl.BlockSpec((rows, tile), lambda j, g: (0, j)),
        pl.BlockSpec((rows, 1), lambda j, g: (0, 0)),
        pl.BlockSpec((rows, pairs), lambda j, g: (0, 0)),
    ]


def back(places, pieces, w_down, low, before=()):
    count = len(pieces)
    rows, width = pieces[0].shape
    depth = w_down.shape[0]
    pairs = low.shape[0]
    tile = tile_of(depth, 512)
    totals = carried_specs(rows, pairs, tile)
    return pl.pallas_call(
        lambda *refs: back_body(count, len(before), *refs),
        grid_spec=pltpu.PrefetchScalarGridSpec(
            num_scalar_prefetch=1,
            grid=(depth // tile,),
            in_specs=[pl.BlockSpec((rows, width), lambda j, g: (0, 0))] * count
            + group_specs(count, tile, width, 1)
            + group_specs(count, pairs, width, 0)
            + totals[: len(before)],
            out_specs=totals,
        ),
        out_shape=[
            jax.ShapeDtypeStruct((rows, depth), f32),
            jax.ShapeDtypeStruct((rows, 1), f32),
            jax.ShapeDtypeStruct((rows, pairs), f32),
        ],
        compiler_params=params(),
        cost_estimate=cost(2 * rows * depth * width * count, 2 * depth * width * count),
    )(places, *pieces, *[w_down] * 2 * count, *[low] * 2 * count, *before)


def finish_body(features, count, places_ref, *refs):
    hids, weights, lows, refs = refs[:count], refs[count : count + 2], refs[count + 2 : count + 4], refs[count + 4 :]
    acc_ref, squares_ref, cross_ref, hot_ref, share_ref, low_act_ref = refs[:6]
    own_ref, own_low_ref, gain_ref, act_out, resid_out, normed_out, hid, lead, pull = refs[6:]
    rows = own_ref.shape[0]
    part = rows // count

    @pl.when(pl.program_id(0) == 0)
    def _():
        for n in range(count):
            hid[n * part : (n + 1) * part] = hids[n][...]
        squares, cross = statistics(halves_of(hid), lows)
        hot = hot_ref[...]
        inner = jnp.sum((cross_ref[...] + cross) * hot.astype(f32), axis=1, keepdims=True)
        inner = inner * share_ref[...]
        inv_rms = lax.rsqrt((squares_ref[...] + squares) / features + norm_eps)
        lead[...] = inv_rms * share_ref[...]
        pull[...] = inv_rms * inv_rms * inv_rms * inner / features
        own = own_ref[...].astype(f32)
        own_low = dot(hot, own_low_ref[...])
        resid_out[...] = (lead[...] * own_low - own * pull[...]).astype(bf16)
        normed_out[...] = (gain_ref[...] * own * inv_rms).astype(bf16)

    low_act = dot_t(hot_ref[...], low_act_ref[...])
    hid_act = acc_ref[...] + product(halves_of(hid), weights)
    act_out[...] = (lead[...] * low_act - pull[...] * hid_act).astype(bf16)


def finish(places, pieces, w_down, low, before, hot, share, low_act, own, gain):
    count = len(pieces)
    rows, width = own.shape
    depth, features = w_down.shape
    pairs = hot.shape[1]
    tile = tile_of(depth, 512)

    def whole(shape):
        return pl.BlockSpec(shape, lambda j, g: (0, 0))

    return pl.pallas_call(
        lambda *refs: finish_body(features, count, *refs),
        grid_spec=pltpu.PrefetchScalarGridSpec(
            num_scalar_prefetch=1,
            grid=(depth // tile,),
            in_specs=[whole((rows // count, width))] * count
            + group_specs(1, tile, width, 1)
            + group_specs(1, pairs, width, 0)
            + carried_specs(rows, pairs, tile)
            + [
                whole((rows, pairs)),
                whole((rows, 1)),
                pl.BlockSpec((tile, pairs), lambda j, g: (j, 0)),
                whole((rows, width)),
                pl.BlockSpec((pairs, width), lambda j, g: (0, g[1])),
                whole((1, width)),
            ],
            out_specs=[
                pl.BlockSpec((rows, tile), lambda j, g: (0, j)),
                whole((rows, width)),
                whole((rows, width)),
            ],
            scratch_shapes=[
                pltpu.VMEM((rows, width), bf16),
                pltpu.VMEM((rows, 1), f32),
                pltpu.VMEM((rows, 1), f32),
            ],
        ),
        out_shape=[
            jax.ShapeDtypeStruct((rows, depth), bf16),
            jax.ShapeDtypeStruct((rows, width), bf16),
            jax.ShapeDtypeStruct((rows, width), bf16),
        ],
        compiler_params=params(),
        cost_estimate=cost(2 * rows * depth * width, 2 * depth * width + 6 * rows * depth),
    )(
        places,
        *pieces,
        *[w_down] * 2,
        *[low] * 2,
        *before,
        hot,
        share,
        low_act,
        own,
        low,
        gain,
    )


def low_rank_shards(
    query_emb,
    passage_emb,
    row_lse,
    positive,
    token_lengths,
    destination,
    mlp_act,
    resid,
    w_down,
    gain,
):
    wide_count = lax.axis_size("wide")
    blk, wide = lax.axis_index("blk"), lax.axis_index("wide")
    tok_count, width = resid.shape
    features = w_down.shape[1]
    pairs = row_lse.shape[0]
    slot_count = 3 * tok_count // (2 * wide_count)
    rows = wide_count * slot_count

    both = payload(query_emb, passage_emb, gain)
    parts = [both] + [swap(both, k) for k in (1, 2, 3)]
    first_term = project((blk ^ 3)[None], mlp_act, w_down, width)
    arrived = [swap(first_term, 3)]
    parts = after(first_term, *parts)[1:]
    query_grad, low_own = group_part(
        parts, row_lse, positive, token_lengths, destination, features, blk
    )
    mlp_act = after(low_own, mlp_act)[1]
    for k in (1, 2):
        arrived.append(swap(project((blk ^ k)[None], mlp_act, w_down, width), k))
    own_term = project(blk[None], mlp_act, w_down, width, resid)

    low = lax.all_gather(low_own, "wide", axis=0, tiled=True)
    packed = pack(wide, destination, own_term, arrived, wide_count, slot_count)
    routed = [packed[k] if k == 0 else swap(packed[k], k, "wide") for k in range(wide_count)]
    low_act = low_activations(low, features, w_down)
    hot, share = slot_passages(wide, low, features, wide_count, slot_count, rows)
    low_act, hot, share, *routed = lax.optimization_barrier((low_act, hot, share, *routed))
    own = assemble(wide, routed)

    beside, above = swap(own, 1), swap(own, 2)
    totals = back(blk[None], [own], w_down, low)
    *totals, beside, above = lax.optimization_barrier((*totals, beside, above))
    top = swap(beside[: rows // 2], 2)
    bottom = swap(above[rows // 2 :], 1)
    totals = back(jnp.stack([blk ^ 1, blk ^ 2]), [beside, above], w_down, low, totals)
    act_grad, resid_grad, normed_out = finish(
        jnp.stack([blk ^ 3, blk]),
        [top, bottom],
        w_down,
        low,
        totals,
        hot,
        share,
        low_act,
        own,
        gain[None],
    )
    return (query_grad, resid_grad, act_grad, normed_out)


def coefficients(scores, lse_part, pos_part):
    columns = lax.broadcasted_iota(jnp.int32, scores.shape, 1)
    target = (pos_part[:, None] == columns).astype(jnp.float32)
    return (jnp.exp(scores - lse_part[:, None]) - target).astype(jnp.bfloat16)


def place_rows(destination, wide_count, slot_count):
    tok_count = destination.shape[0]
    dest_hot = (destination == lax.broadcasted_iota(jnp.int32, (tok_count, wide_count), 1)).astype(
        bf16
    )
    token = lax.iota(jnp.int32, tok_count)
    earlier = (token[None, :] < token[:, None]).astype(bf16)
    rank_of = jnp.dot(earlier, dest_hot, preferred_element_type=f32)
    slot_of = jnp.sum(rank_of * dest_hot.astype(f32), axis=1).astype(jnp.int32)
    slot_of = slot_of + destination[:, 0] * slot_count
    return (
        lax.broadcasted_iota(jnp.int32, (wide_count * slot_count, tok_count), 0) == slot_of[None, :]
    ).astype(bf16)


def row_shards(
    query_emb,
    passage_emb,
    row_lse,
    positive,
    token_lengths,
    destination,
    mlp_act,
    resid,
    w_down,
    gain,
):
    pair_rows = query_emb.shape[0]
    tok_count, feat_width = resid.shape
    features = w_down.shape[1]
    blk_index = lax.axis_index("blk")
    wide_count = lax.axis_size("wide")
    slot_count = 3 * tok_count // (2 * wide_count)
    offset = blk_index * feat_width
    query_all = lax.all_gather(query_emb, "blk", axis=0, tiled=True)
    passage_all = lax.all_gather(passage_emb, "blk", axis=0, tiled=True)
    scores = logit_scale * jnp.dot(query_all, passage_all.T, preferred_element_type=f32)
    coef_full = coefficients(scores, row_lse, positive)
    own_coef = lax.dynamic_slice_in_dim(coef_full, blk_index * pair_rows, pair_rows, 0)
    query_grad = (
        logit_scale * jnp.dot(own_coef, passage_all, preferred_element_type=f32)
    ).astype(bf16)
    query_cols = lax.dynamic_slice_in_dim(query_all, offset, feat_width, 1)
    grad_cols = logit_scale * lax.dot_general(
        query_cols, coef_full, (((0,), (0,)), ((), ())), preferred_element_type=f32
    )
    lengths_row = token_lengths[0]
    starts = jnp.cumsum(lengths_row) - lengths_row
    positions = lax.broadcasted_iota(jnp.int32, (tok_count, lengths_row.shape[0]), 0)
    member = (positions >= starts[None, :]) & (positions < (starts + lengths_row)[None, :])
    weights = member.astype(f32) * (1.0 / lengths_row.astype(f32))[None, :]
    tok_grad = lax.dot_general(
        weights,
        grad_cols,
        (((1,), (1,)), ((), ())),
        precision=lax.Precision.HIGHEST,
        preferred_element_type=f32,
    ).astype(bf16)
    terms = jnp.dot(mlp_act, w_down, preferred_element_type=f32)
    own = lax.dynamic_slice_in_dim(terms, offset, feat_width, 1) + resid.astype(f32)
    terms = lax.dynamic_update_slice_in_dim(terms, own, offset, 1)
    hidden = lax.psum_scatter(terms.astype(bf16), "blk", scatter_dimension=1, tiled=True)
    placer = place_rows(destination, wide_count, slot_count)
    payload = jnp.concatenate([hidden, tok_grad], axis=1)
    packed = jnp.dot(placer, payload, preferred_element_type=f32).astype(bf16)
    packed = packed.reshape(wide_count, slot_count, 2 * feat_width)
    rows = lax.all_to_all(packed, "wide", split_axis=0, concat_axis=0, tiled=True).reshape(
        wide_count * slot_count, 2 * feat_width
    )
    hidden = rows[:, :feat_width].astype(f32)
    gained = gain[None, :] * rows[:, feat_width:].astype(f32)
    squares, inner_sum = lax.psum(
        (jnp.sum(hidden * hidden, axis=1), jnp.sum(gained * hidden, axis=1)), "blk"
    )
    inv_rms = lax.rsqrt(squares / features + norm_eps)[:, None]
    normed = (gain[None, :] * hidden * inv_rms).astype(bf16)
    resid_back = (
        inv_rms * gained - hidden * (inv_rms * inv_rms * inv_rms) * inner_sum[:, None] / features
    ).astype(bf16)
    act_back = dot_t(lax.all_gather(resid_back, "blk", axis=1, tiled=True), w_down)
    return (query_grad, resid_back, act_back.astype(bf16), normed)


def solution(mesh):
    blk_count, wide_count = mesh.shape["blk"], mesh.shape["wide"]

    def shards(*operands):
        pairs, tok_count = operands[2].shape[0], operands[7].shape[0]
        low_rank = 2 * wide_count * pairs <= 3 * tok_count
        per_pair = tok_count // pairs
        aligned = operands[9].shape[0] % (lane * operands[0].shape[0]) == 0
        if low_rank and blk_count == 4 and aligned and per_pair * pairs == tok_count and wide_count & (wide_count - 1) == 0:
            return low_rank_shards(*operands)
        return row_shards(*operands)

    return jax.shard_map(
        shards,
        mesh=mesh,
        in_specs=(
            P(("wide", "blk"), None),
            P(("wide", "blk"), None),
            P("wide"),
            P("wide"),
            P("wide", None),
            P("wide", None),
            P("wide", "blk"),
            P("wide", "blk"),
            P("blk", None),
            P("blk"),
        ),
        out_specs=(P(("wide", "blk"), None), P("wide", "blk"), P("wide", "blk"), P("wide", "blk")),
        check_vma=False,
    )
```

```python
import jax
import jax.numpy as jnp
from jax import lax
from jax.experimental import pallas as pl
from jax.experimental.pallas import tpu as pltpu
from jax.sharding import PartitionSpec as P

logit_scale = 24.0
norm_eps = 1e-06
f32 = jnp.float32
bf16 = jnp.bfloat16
i32 = jnp.int32
lane = 128
kernel_vmem = 46 * 1024 * 1024


def params():
    return pltpu.CompilerParams(vmem_limit_bytes=kernel_vmem)


def cost(flops, nbytes):
    return pl.CostEstimate(flops=flops, bytes_accessed=nbytes, transcendentals=0)


def tile_of(extent, most):
    tile = most
    while extent % tile:
        tile //= 2
    return tile


def iota(shape, dim):
    return lax.broadcasted_iota(i32, shape, dim)


def dot(left, right):
    return jnp.dot(left, right, preferred_element_type=f32)


def dot_t(left, right):
    return lax.dot_general(left, right, (((1,), (1,)), ((), ())), preferred_element_type=f32)


def swap(rows, k, axis="blk"):
    return lax.ppermute(rows, axis, [(i, i ^ k) for i in range(lax.axis_size(axis))])


def project_body(has_resid, group_ref, act_hbm, w_hbm, *refs):
    out_ref, act, weights, act_sem, sems = refs[has_resid:]
    width = out_ref.shape[1]
    count, _, tile = weights.shape
    first = group_ref[0] * width

    def weight_copy(i):
        columns = pl.ds(pl.multiple_of(first + i * tile, lane), tile)
        return pltpu.make_async_copy(w_hbm.at[:, columns], weights.at[i], sems.at[i])

    act_copy = pltpu.make_async_copy(act_hbm, act, act_sem)
    act_copy.start()
    for i in range(count):
        weight_copy(i).start()
    act_copy.wait()

    @pl.loop(0, count)
    def _(i):
        weight_copy(i).wait()
        columns = pl.ds(pl.multiple_of(i * tile, lane), tile)
        term = dot(act[...], weights[i])
        if has_resid:
            term = term + refs[0][:, columns].astype(f32)
        out_ref[:, columns] = term.astype(out_ref.dtype)


def project(group, act, w_down, width, resid=None):
    rows, depth = act.shape
    tile = tile_of(width, 256)
    count = width // tile
    own = [] if resid is None else [resid]
    return pl.pallas_call(
        lambda *refs: project_body(len(own), *refs),
        in_specs=[pl.BlockSpec(memory_space=pltpu.SMEM)]
        + [pl.BlockSpec(memory_space=pl.ANY)] * 2
        + [pl.BlockSpec(memory_space=pltpu.VMEM)] * len(own),
        out_specs=pl.BlockSpec(memory_space=pltpu.VMEM),
        out_shape=jax.ShapeDtypeStruct((rows, width), f32 if own else bf16),
        scratch_shapes=[
            pltpu.VMEM((rows, depth), bf16),
            pltpu.VMEM((count, depth, tile), bf16),
            pltpu.SemaphoreType.DMA,
            pltpu.SemaphoreType.DMA((count,)),
        ],
        compiler_params=params(),
        cost_estimate=cost(rows * depth * width // 8, depth * width // 8),
    )(group, act, w_down, *own)


def payload_body(query_ref, passage_ref, gain_ref, out_ref, gains):
    own, features = query_ref.shape
    piece = gains.shape[1]
    for row in range(own):
        gains[row : row + 1] = gain_ref[:, row * piece : (row + 1) * piece]
    gain = gains[...]
    high = gain.astype(bf16)
    out_ref[:, :features] = query_ref[...]
    out_ref[:, features : 2 * features] = passage_ref[...]
    out_ref[:, 2 * features : 2 * features + piece] = high
    out_ref[:, 2 * features + piece :] = (gain - high.astype(f32)).astype(bf16)


def payload(query_emb, passage_emb, gain):
    own, features = query_emb.shape
    piece = gain.shape[0] // own
    return pl.pallas_call(
        payload_body,
        out_shape=jax.ShapeDtypeStruct((own, 2 * features + 2 * piece), bf16),
        scratch_shapes=[pltpu.VMEM((own, piece), f32)],
        compiler_params=params(),
        cost_estimate=cost(own * features, 8 * own * features),
    )(query_emb, passage_emb, gain[None])


def group_body(count, blk_ref, *refs):
    parts, refs = refs[:count], refs[count:]
    lse_ref, pos_ref, dest_ref, len_ref = refs[:4]
    query_grad_ref, low_ref, query_all, passage_all, gain_all = refs[4:]
    own, features = query_grad_ref.shape
    pairs = own * count
    piece = features // pairs
    blk = blk_ref[0]
    for k in range(count):
        query_all[k * own : (k + 1) * own] = parts[k][:, :features].astype(f32)
        passage_all[k * own : (k + 1) * own] = parts[k][:, features : 2 * features].astype(f32)
        gains = parts[k][:, 2 * features : 2 * features + piece].astype(f32)
        gains = gains + parts[k][:, 2 * features + piece :].astype(f32)
        for row in range(own):
            first = pl.multiple_of(((blk ^ k) * own + row) * piece, lane)
            gain_all[:, pl.ds(first, piece)] = gains[row : row + 1]
    queries = query_all[...].astype(bf16)
    passages = passage_all[...].astype(bf16)

    def named(dim):
        place = iota((pairs, pairs), dim)
        return (blk ^ (place // own)) * own + place % own

    here_rows, here_cols = named(0), named(1)
    at_rows = here_rows == iota((pairs, pairs), 1)
    at_cols = here_cols == iota((pairs, pairs), 0)
    lse = jnp.sum(jnp.where(at_rows, lse_ref[...], 0.0), axis=1, keepdims=True)
    pos = jnp.sum(jnp.where(at_rows, pos_ref[...], 0), axis=1, keepdims=True)
    hit = (pos == here_cols).astype(f32)
    coef = (jnp.exp(logit_scale * dot_t(queries, passages) - lse) - hit).astype(bf16)
    query_grad_ref[...] = (logit_scale * dot(coef, passages))[:own].astype(bf16)
    same = iota((pairs, pairs), 0) == iota((pairs, pairs), 1)
    lse = jnp.sum(jnp.where(same, lse, 0.0), axis=0, keepdims=True)
    pos = jnp.sum(jnp.where(same, pos, 0), axis=0, keepdims=True)
    hit = (pos == here_rows).astype(f32)
    turned = (jnp.exp(logit_scale * dot_t(passages, queries) - lse) - hit).astype(bf16)
    turned = dot(at_cols.astype(f32).astype(bf16), turned).astype(bf16)
    pass_grad = logit_scale * dot(turned, queries)
    low_ref[:, :features] = (gain_all[...] * pass_grad).astype(bf16)
    row = iota((pairs, lane), 0)
    tokens = dest_ref.shape[1]
    table = jnp.zeros((pairs, lane), f32)
    for n in range(-(-tokens // lane)):
        some = dest_ref[:, n * lane : min(tokens, (n + 1) * lane)].astype(f32)
        table = jnp.where(row == n, widen(some), table)
    table = jnp.where(row == -(-tokens // lane), widen(len_ref[...].astype(f32)), table)
    low_ref[:, features:] = table.astype(bf16)


def widen(row):
    short = lane - row.shape[1]
    return jnp.concatenate([row, jnp.zeros((1, short), f32)], axis=1) if short else row


def group_part(parts, row_lse, positive, token_lengths, destination, features, blk):
    own = parts[0].shape[0]
    pairs = row_lse.shape[0]
    return pl.pallas_call(
        lambda *refs: group_body(pairs // own, *refs),
        in_specs=[pl.BlockSpec(memory_space=pltpu.SMEM)]
        + [pl.BlockSpec(memory_space=pltpu.VMEM)] * (len(parts) + 4),
        out_specs=[pl.BlockSpec(memory_space=pltpu.VMEM)] * 2,
        out_shape=[
            jax.ShapeDtypeStruct((own, features), bf16),
            jax.ShapeDtypeStruct((pairs, features + lane), bf16),
        ],
        scratch_shapes=[
            pltpu.VMEM((pairs, features), f32),
            pltpu.VMEM((pairs, features), f32),
            pltpu.VMEM((1, features), f32),
        ],
        compiler_params=params(),
        cost_estimate=cost(8 * pairs * pairs * features, 8 * pairs * features),
    )(
        blk[None],
        *parts,
        row_lse[None],
        positive[None],
        destination.reshape(1, -1),
        token_lengths,
    )


def earlier_of(tokens):
    return (iota((tokens, tokens), 0) < iota((tokens, tokens), 1)).astype(bf16)


def pack_body(terms, wide_ref, dest_ref, own_ref, *rest):
    outs = rest[terms:]
    groups, slots = len(outs), outs[0].shape[0]
    tokens = dest_ref.shape[1]
    stride = -(-slots // 16) * 16
    hidden = own_ref[...]
    for term in rest[:terms]:
        hidden = hidden + term[...].astype(f32)
    partner = dest_ref[...] ^ wide_ref[0]
    hit = (partner == iota((groups, tokens), 0)).astype(f32)
    rank = dot(hit.astype(bf16), earlier_of(tokens))
    rank = jnp.sum(rank * hit, axis=0, keepdims=True).astype(i32)
    place = iota((groups * stride, tokens), 0) == partner * stride + rank
    packed = dot(place.astype(f32).astype(bf16), hidden.astype(bf16)).astype(bf16)
    for k in range(groups):
        outs[k][...] = packed[k * stride : k * stride + slots]


def pack(wide, destination, own, terms, groups, slots):
    tokens, width = own.shape
    tile = tile_of(width, 512)
    column_spec = pl.BlockSpec((tokens, tile), lambda j, g: (0, j))
    return pl.pallas_call(
        lambda *refs: pack_body(len(terms), *refs),
        grid_spec=pltpu.PrefetchScalarGridSpec(
            num_scalar_prefetch=1,
            grid=(width // tile,),
            in_specs=[pl.BlockSpec((1, tokens), lambda j, g: (0, 0))]
            + [column_spec] * (1 + len(terms)),
            out_specs=[pl.BlockSpec((slots, tile), lambda j, g: (0, j))] * groups,
        ),
        out_shape=[jax.ShapeDtypeStruct((slots, width), bf16)] * groups,
        compiler_params=params(),
        cost_estimate=cost(4 * groups * slots * tokens * width, 10 * tokens * width),
    )(wide[None], destination.reshape(1, tokens), own, *terms)


def assemble_body(wide_ref, *refs):
    parts, (left_ref, right_ref) = refs[:-2], refs[-2:]
    slots = parts[0].shape[0]
    rows, half = left_ref.shape
    row, column = iota((rows, slots), 0), iota((rows, slots), 1)
    total = 0.0
    for k, part in enumerate(parts):
        group = wide_ref[0] ^ k
        place = (row == group * slots + column).astype(f32).astype(bf16)
        total = total + dot(place, part[...])
    left_ref[...] = total[:, :half].astype(bf16)
    right_ref[...] = total[:, half:].astype(bf16)


def assemble(wide, parts):
    slots, width = parts[0].shape
    rows = slots * len(parts)
    return pl.pallas_call(
        assemble_body,
        in_specs=[pl.BlockSpec(memory_space=pltpu.SMEM)]
        + [pl.BlockSpec(memory_space=pltpu.VMEM)] * len(parts),
        out_specs=[pl.BlockSpec(memory_space=pltpu.VMEM)] * 2,
        out_shape=[jax.ShapeDtypeStruct((rows, width // 2), bf16)] * 2,
        compiler_params=params(),
        cost_estimate=cost(2 * rows * rows * width, 4 * rows * width),
    )(wide[None], *parts)


def slots_body(groups, slots, wide_ref, table_ref, hot_ref, share_ref):
    rows, columns = hot_ref.shape
    pairs = columns // groups
    blocks = -(-slots * groups * 2 // 3 // lane)
    table = table_ref[...]

    def tables(n):
        at = iota((groups, columns), 1) == iota((groups, columns), 0) * pairs + n
        return dot(at.astype(f32).astype(bf16), table)

    spread = (iota((rows, groups), 0) // slots == iota((rows, groups), 1)).astype(f32).astype(bf16)
    lengths = tables(blocks)
    upto = (iota((lane, lane), 0) <= iota((lane, lane), 1)).astype(f32).astype(bf16)
    ends = dot(lengths.astype(bf16), upto)
    slot = iota((rows, lane), 0) % slots
    before = jnp.zeros((groups, 1), f32)
    taken = jnp.zeros((rows, 1), f32)
    for n in range(blocks):
        token = iota((groups, lane), 1) + n * lane
        hit = (tables(n).astype(i32) == wide_ref[0]) & (token < slots * groups * 2 // 3)
        count = hit.astype(f32)
        rank = before + dot(count.astype(bf16), earlier_of(lane))
        before = before + jnp.sum(count, axis=1, keepdims=True)
        passage = jnp.ones((groups, lane), f32)
        for pair in range(pairs):
            passage = passage + (token.astype(f32) >= ends[:, pair : pair + 1]).astype(f32)
        code = jnp.where(hit, passage, 0.0)
        rank_rows = dot(spread, rank.astype(bf16)).astype(i32)
        code_rows = dot(spread, code.astype(bf16))
        taken = taken + jnp.sum(
            jnp.where(rank_rows == slot, code_rows, 0.0), axis=1, keepdims=True
        )
    taken = taken.astype(i32)
    column = iota((rows, columns), 1)
    first = iota((rows, columns), 0) // slots * pairs
    hot = (taken > 0) & (column == first + taken - 1)
    hot_ref[...] = hot.astype(f32).astype(bf16)
    length_rows = dot(spread, lengths.astype(bf16))
    length = jnp.where(iota((rows, lane), 1) == taken - 1, length_rows, 0.0)
    length = jnp.sum(length, axis=1, keepdims=True)
    share_ref[...] = jnp.where(taken > 0, 1.0 / jnp.maximum(length, 1.0), 0.0)


def slot_passages(wide, low, features, groups, slots, rows):
    columns = low.shape[0]
    return pl.pallas_call(
        lambda *refs: slots_body(groups, slots, *refs),
        grid=(1,),
        in_specs=[
            pl.BlockSpec(memory_space=pltpu.SMEM),
            pl.BlockSpec((columns, lane), lambda j: (0, features // lane)),
        ],
        out_specs=[
            pl.BlockSpec((rows, columns), lambda j: (0, 0)),
            pl.BlockSpec((rows, 1), lambda j: (0, 0)),
        ],
        out_shape=[
            jax.ShapeDtypeStruct((rows, columns), bf16),
            jax.ShapeDtypeStruct((rows, 1), f32),
        ],
        compiler_params=params(),
        cost_estimate=cost(4 * rows * groups * lane, 2 * rows * columns),
    )(wide[None], low)


def low_act_body(part, low_ref, w_hbm, *refs):
    out_ref, weights, sems = refs[-3:]
    count, tile, _ = weights.shape

    def weight_copy(t):
        rows = pl.ds(pl.multiple_of((part * count + t) * tile, tile), tile)
        return pltpu.make_async_copy(w_hbm.at[rows], weights.at[t], sems.at[t])

    for t in range(count):
        weight_copy(t).start()

    @pl.loop(0, count)
    def _(t):
        weight_copy(t).wait()
        rows = pl.ds(pl.multiple_of(t * tile, tile), tile)
        out_ref[rows] = dot_t(weights[t], low_ref[...]).astype(bf16)


def low_activations(low, features, w_down, part, parts, filled=()):
    pairs = low.shape[0]
    depth = w_down.shape[0]
    some = depth // parts
    tile = tile_of(some, 512)
    count = some // tile
    anywhere = pl.BlockSpec(memory_space=pl.ANY)
    return pl.pallas_call(
        lambda *refs: low_act_body(part, *refs),
        grid=(1,),
        in_specs=[pl.BlockSpec((pairs, features), lambda j: (0, 0)), anywhere]
        + [anywhere] * len(filled),
        out_specs=pl.BlockSpec((some, pairs), lambda j: (part, 0)),
        out_shape=jax.ShapeDtypeStruct((depth, pairs), bf16),
        scratch_shapes=[
            pltpu.VMEM((count, tile, features), bf16),
            pltpu.SemaphoreType.DMA((count,)),
        ],
        input_output_aliases={2: 0} if filled else {},
        compiler_params=params(),
        cost_estimate=cost(2 * pairs * some * features, 2 * some * features),
    )(low, w_down, *filled)


def statistics(hids, lows):
    squares, cross = 0.0, 0.0
    for hid_ref, low_ref in zip(hids, lows):
        hid = hid_ref[...].astype(f32)
        squares = squares + jnp.sum(hid * hid, axis=1, keepdims=True)
        cross = cross + dot_t(hid_ref[...], low_ref[...])
    return squares, cross


def product(hids, weights):
    total = 0.0
    for hid_ref, w_ref in zip(hids, weights):
        total = total + dot_t(hid_ref[...], w_ref[...])
    return total


def piece_specs(pieces, low, tile):
    hid_specs, w_specs, low_specs = [], [], []
    for n, piece in enumerate(pieces):
        width = piece.shape[1]
        hid_specs.append(pl.BlockSpec(piece.shape, lambda j, g: (0, 0)))
        w_specs.append(pl.BlockSpec((tile, width), lambda j, g, n=n: (j, g[n])))
        low_specs.append(pl.BlockSpec((low.shape[0], width), lambda j, g, n=n: (0, g[n])))
    return hid_specs + w_specs + low_specs


def back_body(count, carried, places_ref, *refs):
    hids, weights, lows = refs[:count], refs[count : 2 * count], refs[2 * count : 3 * count]
    before, (acc_ref, squares_ref, cross_ref) = refs[3 * count : -3], refs[-3:]

    @pl.when(pl.program_id(0) == 0)
    def _():
        squares, cross = statistics(hids, lows)
        if carried:
            squares, cross = before[1][...] + squares, before[2][...] + cross
        squares_ref[...], cross_ref[...] = squares, cross

    total = product(hids, weights)
    acc_ref[...] = before[0][...] + total if carried else total


def carried_specs(rows, pairs, tile):
    return [
        pl.BlockSpec((rows, tile), lambda j, g: (0, j)),
        pl.BlockSpec((rows, 1), lambda j, g: (0, 0)),
        pl.BlockSpec((rows, pairs), lambda j, g: (0, 0)),
    ]


def back(places, pieces, w_down, low, before=()):
    count = len(pieces)
    rows, width = pieces[0].shape
    depth = w_down.shape[0]
    pairs = low.shape[0]
    tile = tile_of(depth, 512)
    totals = carried_specs(rows, pairs, tile)
    return pl.pallas_call(
        lambda *refs: back_body(count, len(before), *refs),
        grid_spec=pltpu.PrefetchScalarGridSpec(
            num_scalar_prefetch=1,
            grid=(depth // tile,),
            in_specs=piece_specs(pieces, low, tile) + totals[: len(before)],
            out_specs=totals,
        ),
        out_shape=[
            jax.ShapeDtypeStruct((rows, depth), f32),
            jax.ShapeDtypeStruct((rows, 1), f32),
            jax.ShapeDtypeStruct((rows, pairs), f32),
        ],
        compiler_params=params(),
        cost_estimate=cost(2 * rows * depth * width * count, 2 * depth * width * count),
    )(places, *pieces, *[w_down] * count, *[low] * count, *before)


def finish_body(features, count, places_ref, *refs):
    hids, weights, lows = refs[:count], refs[count : 2 * count], refs[2 * count : 3 * count]
    refs = refs[3 * count :]
    acc_ref, squares_ref, cross_ref, hot_ref, share_ref, low_act_ref, left_ref, right_ref = refs[:8]
    own_low_ref, gain_ref, act_out, resid_out, normed_out, lead, pull = refs[8:]

    @pl.when(pl.program_id(0) == 0)
    def _():
        squares, cross = statistics(hids, lows)
        hot = hot_ref[...]
        inner = jnp.sum((cross_ref[...] + cross) * hot.astype(f32), axis=1, keepdims=True)
        inner = inner * share_ref[...]
        inv_rms = lax.rsqrt((squares_ref[...] + squares) / features + norm_eps)
        lead[...] = inv_rms * share_ref[...]
        pull[...] = inv_rms * inv_rms * inv_rms * inner / features
        half = left_ref.shape[1]
        for own_ref, at in ((left_ref, slice(0, half)), (right_ref, slice(half, 2 * half))):
            own = own_ref[...].astype(f32)
            own_low = dot(hot, own_low_ref[:, at])
            resid_out[:, at] = (lead[...] * own_low - own * pull[...]).astype(bf16)
            normed_out[:, at] = (gain_ref[:, at] * own * inv_rms).astype(bf16)

    low_act = dot_t(hot_ref[...], low_act_ref[...])
    hid_act = acc_ref[...] + product(hids, weights)
    act_out[...] = (lead[...] * low_act - pull[...] * hid_act).astype(bf16)


def finish(places, pieces, w_down, low, before, hot, share, low_act, own, gain):
    count = len(pieces)
    rows, half = own[0].shape
    width = 2 * half
    depth, features = w_down.shape
    pairs = hot.shape[1]
    tile = tile_of(depth, 512)

    def whole(shape):
        return pl.BlockSpec(shape, lambda j, g: (0, 0))

    return pl.pallas_call(
        lambda *refs: finish_body(features, count, *refs),
        grid_spec=pltpu.PrefetchScalarGridSpec(
            num_scalar_prefetch=1,
            grid=(depth // tile,),
            in_specs=piece_specs(pieces, low, tile)
            + carried_specs(rows, pairs, tile)
            + [
                whole((rows, pairs)),
                whole((rows, 1)),
                pl.BlockSpec((tile, pairs), lambda j, g: (j, 0)),
                whole((rows, half)),
                whole((rows, half)),
                pl.BlockSpec((pairs, width), lambda j, g: (0, g[count])),
                whole((1, width)),
            ],
            out_specs=[
                pl.BlockSpec((rows, tile), lambda j, g: (0, j)),
                whole((rows, width)),
                whole((rows, width)),
            ],
            scratch_shapes=[pltpu.VMEM((rows, 1), f32), pltpu.VMEM((rows, 1), f32)],
        ),
        out_shape=[
            jax.ShapeDtypeStruct((rows, depth), bf16),
            jax.ShapeDtypeStruct((rows, width), bf16),
            jax.ShapeDtypeStruct((rows, width), bf16),
        ],
        compiler_params=params(),
        cost_estimate=cost(2 * rows * depth * width, 2 * depth * width + 6 * rows * depth),
    )(
        places,
        *pieces,
        *[w_down] * count,
        *[low] * count,
        *before,
        hot,
        share,
        low_act,
        *own,
        low,
        gain,
    )


def low_rank_shards(
    query_emb,
    passage_emb,
    row_lse,
    positive,
    token_lengths,
    destination,
    mlp_act,
    resid,
    w_down,
    gain,
):
    wide_count = lax.axis_size("wide")
    blk, wide = lax.axis_index("blk"), lax.axis_index("wide")
    tok_count, width = resid.shape
    features = w_down.shape[1]
    pairs = row_lse.shape[0]
    slot_count = 3 * tok_count // (2 * wide_count)
    rows = wide_count * slot_count

    first_term = project((blk ^ 3)[None], mlp_act, w_down, width)
    arrived = [swap(first_term, 3)]
    _, query_emb, passage_emb = lax.optimization_barrier((first_term, query_emb, passage_emb))
    both = payload(query_emb, passage_emb, gain)
    parts = [both] + [swap(both, k) for k in (1, 2, 3)]
    second_term = project((blk ^ 1)[None], mlp_act, w_down, width)
    arrived.append(swap(second_term, 1))
    _, arrived[0], *parts = lax.optimization_barrier((second_term, arrived[0], *parts))
    query_grad, low_own = group_part(
        parts, row_lse, positive, token_lengths, destination, features, blk
    )
    _, mlp_act = lax.optimization_barrier((low_own, mlp_act))
    arrived.append(swap(project((blk ^ 2)[None], mlp_act, w_down, width), 2))
    own_term = project(blk[None], mlp_act, w_down, width, resid)

    low = lax.all_gather(low_own, "wide", axis=0, tiled=True)
    packed = pack(wide, destination, own_term, arrived, wide_count, slot_count)
    routed = [packed[k] if k == 0 else swap(packed[k], k, "wide") for k in range(wide_count)]
    low_act = low_activations(low, features, w_down, 0, 2)
    hot, share = slot_passages(wide, low, features, wide_count, slot_count, rows)
    low_act, hot, share, *routed = lax.optimization_barrier((low_act, hot, share, *routed))
    left, right = assemble(wide, routed)

    left_1, left_2 = swap(left, 1), swap(left, 2)
    right_1, right_2 = swap(right, 1), swap(right, 2)
    low_act = low_activations(low, features, w_down, 1, 2, [low_act])
    low_act, left_1, left_2 = lax.optimization_barrier((low_act, left_1, left_2))
    left_3 = swap(left_1, 2)

    def places(*pieces):
        return [(blk ^ k) * 2 + side for k, side in pieces]

    totals = back(
        jnp.stack(places((0, 0), (0, 1), (1, 0), (2, 0))),
        [left, right, left_1, left_2],
        w_down,
        low,
    )
    *totals, right_1, right_2 = lax.optimization_barrier((*totals, right_1, right_2))
    right_3 = swap(right_2, 1)
    totals = back(jnp.stack(places((1, 1), (2, 1))), [right_1, right_2], w_down, low, totals)
    act_grad, resid_grad, normed_out = finish(
        jnp.stack([*places((3, 0), (3, 1)), blk]),
        [left_3, right_3],
        w_down,
        low,
        totals,
        hot,
        share,
        low_act,
        [left, right],
        gain[None],
    )
    return (query_grad, resid_grad, act_grad, normed_out)


def coefficients(scores, lse_part, pos_part):
    columns = lax.broadcasted_iota(jnp.int32, scores.shape, 1)
    target = (pos_part[:, None] == columns).astype(jnp.float32)
    return (jnp.exp(scores - lse_part[:, None]) - target).astype(jnp.bfloat16)


def place_rows(destination, wide_count, slot_count):
    tok_count = destination.shape[0]
    dest_hot = (destination == lax.broadcasted_iota(jnp.int32, (tok_count, wide_count), 1)).astype(
        bf16
    )
    token = lax.iota(jnp.int32, tok_count)
    earlier = (token[None, :] < token[:, None]).astype(bf16)
    rank_of = jnp.dot(earlier, dest_hot, preferred_element_type=f32)
    slot_of = jnp.sum(rank_of * dest_hot.astype(f32), axis=1).astype(jnp.int32)
    slot_of = slot_of + destination[:, 0] * slot_count
    return (
        lax.broadcasted_iota(jnp.int32, (wide_count * slot_count, tok_count), 0) == slot_of[None, :]
    ).astype(bf16)


def row_shards(
    query_emb,
    passage_emb,
    row_lse,
    positive,
    token_lengths,
    destination,
    mlp_act,
    resid,
    w_down,
    gain,
):
    pair_rows = query_emb.shape[0]
    tok_count, feat_width = resid.shape
    features = w_down.shape[1]
    blk_index = lax.axis_index("blk")
    wide_count = lax.axis_size("wide")
    slot_count = 3 * tok_count // (2 * wide_count)
    offset = blk_index * feat_width
    query_all = lax.all_gather(query_emb, "blk", axis=0, tiled=True)
    passage_all = lax.all_gather(passage_emb, "blk", axis=0, tiled=True)
    scores = logit_scale * jnp.dot(query_all, passage_all.T, preferred_element_type=f32)
    coef_full = coefficients(scores, row_lse, positive)
    own_coef = lax.dynamic_slice_in_dim(coef_full, blk_index * pair_rows, pair_rows, 0)
    query_grad = (
        logit_scale * jnp.dot(own_coef, passage_all, preferred_element_type=f32)
    ).astype(bf16)
    query_cols = lax.dynamic_slice_in_dim(query_all, offset, feat_width, 1)
    grad_cols = logit_scale * lax.dot_general(
        query_cols, coef_full, (((0,), (0,)), ((), ())), preferred_element_type=f32
    )
    lengths_row = token_lengths[0]
    starts = jnp.cumsum(lengths_row) - lengths_row
    positions = lax.broadcasted_iota(jnp.int32, (tok_count, lengths_row.shape[0]), 0)
    member = (positions >= starts[None, :]) & (positions < (starts + lengths_row)[None, :])
    weights = member.astype(f32) * (1.0 / lengths_row.astype(f32))[None, :]
    tok_grad = lax.dot_general(
        weights,
        grad_cols,
        (((1,), (1,)), ((), ())),
        precision=lax.Precision.HIGHEST,
        preferred_element_type=f32,
    ).astype(bf16)
    terms = jnp.dot(mlp_act, w_down, preferred_element_type=f32)
    own = lax.dynamic_slice_in_dim(terms, offset, feat_width, 1) + resid.astype(f32)
    terms = lax.dynamic_update_slice_in_dim(terms, own, offset, 1)
    hidden = lax.psum_scatter(terms.astype(bf16), "blk", scatter_dimension=1, tiled=True)
    placer = place_rows(destination, wide_count, slot_count)
    payload = jnp.concatenate([hidden, tok_grad], axis=1)
    packed = jnp.dot(placer, payload, preferred_element_type=f32).astype(bf16)
    packed = packed.reshape(wide_count, slot_count, 2 * feat_width)
    rows = lax.all_to_all(packed, "wide", split_axis=0, concat_axis=0, tiled=True).reshape(
        wide_count * slot_count, 2 * feat_width
    )
    hidden = rows[:, :feat_width].astype(f32)
    gained = gain[None, :] * rows[:, feat_width:].astype(f32)
    squares, inner_sum = lax.psum(
        (jnp.sum(hidden * hidden, axis=1), jnp.sum(gained * hidden, axis=1)), "blk"
    )
    inv_rms = lax.rsqrt(squares / features + norm_eps)[:, None]
    normed = (gain[None, :] * hidden * inv_rms).astype(bf16)
    resid_back = (
        inv_rms * gained - hidden * (inv_rms * inv_rms * inv_rms) * inner_sum[:, None] / features
    ).astype(bf16)
    act_back = dot_t(lax.all_gather(resid_back, "blk", axis=1, tiled=True), w_down)
    return (query_grad, resid_back, act_back.astype(bf16), normed)


def solution(mesh):
    blk_count, wide_count = mesh.shape["blk"], mesh.shape["wide"]

    def shards(*operands):
        pairs, tok_count = operands[2].shape[0], operands[7].shape[0]
        low_rank = 2 * wide_count * pairs <= 3 * tok_count
        per_pair = tok_count // pairs
        aligned = operands[9].shape[0] % (lane * operands[0].shape[0]) == 0
        if low_rank and blk_count == 4 and aligned and per_pair * pairs == tok_count and wide_count & (wide_count - 1) == 0:
            return low_rank_shards(*operands)
        return row_shards(*operands)

    return jax.shard_map(
        shards,
        mesh=mesh,
        in_specs=(
            P(("wide", "blk"), None),
            P(("wide", "blk"), None),
            P("wide"),
            P("wide"),
            P("wide", None),
            P("wide", None),
            P("wide", "blk"),
            P("wide", "blk"),
            P("blk", None),
            P("blk"),
        ),
        out_specs=(P(("wide", "blk"), None), P("wide", "blk"), P("wide", "blk"), P("wide", "blk")),
        check_vma=False,
    )
```

```python
import jax
import jax.numpy as jnp
from jax import lax
from jax.experimental import pallas as pl
from jax.experimental.pallas import tpu as pltpu
from jax.sharding import PartitionSpec as P

logit_scale = 24.0
norm_eps = 1e-06
f32 = jnp.float32
bf16 = jnp.bfloat16
i32 = jnp.int32
lane = 128
kernel_vmem = 46 * 1024 * 1024
whole_vmem = 60 * 1024 * 1024


def params(vmem=kernel_vmem):
    return pltpu.CompilerParams(vmem_limit_bytes=vmem)


def cost(flops, nbytes):
    return pl.CostEstimate(flops=flops, bytes_accessed=nbytes, transcendentals=0)


def tile_of(extent, most):
    tile = most
    while extent % tile:
        tile //= 2
    return tile


def iota(shape, dim):
    return lax.broadcasted_iota(i32, shape, dim)


def dot(left, right):
    return jnp.dot(left, right, preferred_element_type=f32)


def dot_t(left, right):
    return lax.dot_general(left, right, (((1,), (1,)), ((), ())), preferred_element_type=f32)


def swap(rows, k, axis="blk"):
    return lax.ppermute(rows, axis, [(i, i ^ k) for i in range(lax.axis_size(axis))])


def after(first, *later):
    return lax.optimization_barrier((first, *later))


def project_body(has_resid, group_ref, act_hbm, w_hbm, *refs):
    out_ref, act, weights, act_sem, sems = refs[has_resid:]
    width = out_ref.shape[1]
    count, _, tile = weights.shape
    first = group_ref[0] * width

    def weight_copy(i):
        columns = pl.ds(pl.multiple_of(first + i * tile, lane), tile)
        return pltpu.make_async_copy(w_hbm.at[:, columns], weights.at[i], sems.at[i])

    act_copy = pltpu.make_async_copy(act_hbm, act, act_sem)
    act_copy.start()
    for i in range(count):
        weight_copy(i).start()
    act_copy.wait()

    @pl.loop(0, count)
    def _(i):
        weight_copy(i).wait()
        columns = pl.ds(pl.multiple_of(i * tile, lane), tile)
        term = dot(act[...], weights[i])
        if has_resid:
            term = term + refs[0][:, columns].astype(f32)
        out_ref[:, columns] = term.astype(out_ref.dtype)


def project(group, act, w_down, width, resid=None):
    rows, depth = act.shape
    tile = tile_of(width, 256)
    count = width // tile
    own = [] if resid is None else [resid]
    return pl.pallas_call(
        lambda *refs: project_body(len(own), *refs),
        in_specs=[pl.BlockSpec(memory_space=pltpu.SMEM)]
        + [pl.BlockSpec(memory_space=pl.ANY)] * 2
        + [pl.BlockSpec(memory_space=pltpu.VMEM)] * len(own),
        out_specs=pl.BlockSpec(memory_space=pltpu.VMEM),
        out_shape=jax.ShapeDtypeStruct((rows, width), f32 if own else bf16),
        scratch_shapes=[
            pltpu.VMEM((rows, depth), bf16),
            pltpu.VMEM((count, depth, tile), bf16),
            pltpu.SemaphoreType.DMA,
            pltpu.SemaphoreType.DMA((count,)),
        ],
        compiler_params=params(),
        cost_estimate=cost(2 * rows * depth * width, 2 * depth * width + 2 * rows * depth),
    )(group, act, w_down, *own)


def payload_body(query_ref, passage_ref, gain_ref, out_ref, gains):
    own, features = query_ref.shape
    piece = gains.shape[1]
    for row in range(own):
        gains[row : row + 1] = gain_ref[:, row * piece : (row + 1) * piece]
    gain = gains[...]
    high = gain.astype(bf16)
    out_ref[:, :features] = query_ref[...]
    out_ref[:, features : 2 * features] = passage_ref[...]
    out_ref[:, 2 * features : 2 * features + piece] = high
    out_ref[:, 2 * features + piece :] = (gain - high.astype(f32)).astype(bf16)


def payload(query_emb, passage_emb, gain):
    own, features = query_emb.shape
    piece = gain.shape[0] // own
    return pl.pallas_call(
        payload_body,
        out_shape=jax.ShapeDtypeStruct((own, 2 * features + 2 * piece), bf16),
        scratch_shapes=[pltpu.VMEM((own, piece), f32)],
        compiler_params=params(whole_vmem),
        cost_estimate=cost(own * features, 8 * own * features),
    )(query_emb, passage_emb, gain[None])


def group_body(count, blk_ref, *refs):
    parts, refs = refs[:count], refs[count:]
    lse_ref, pos_ref, dest_ref, len_ref = refs[:4]
    query_grad_ref, low_ref, query_all, passage_all, gain_all = refs[4:]
    own, features = query_grad_ref.shape
    pairs = own * count
    piece = features // pairs
    blk = blk_ref[0]
    for k in range(count):
        query_all[k * own : (k + 1) * own] = parts[k][:, :features].astype(f32)
        passage_all[k * own : (k + 1) * own] = parts[k][:, features : 2 * features].astype(f32)
        gains = parts[k][:, 2 * features : 2 * features + piece].astype(f32)
        gains = gains + parts[k][:, 2 * features + piece :].astype(f32)
        for row in range(own):
            first = pl.multiple_of(((blk ^ k) * own + row) * piece, lane)
            gain_all[:, pl.ds(first, piece)] = gains[row : row + 1]
    queries = query_all[...].astype(bf16)
    passages = passage_all[...].astype(bf16)

    def named(dim):
        place = iota((pairs, pairs), dim)
        return (blk ^ (place // own)) * own + place % own

    here_rows, here_cols = named(0), named(1)
    at_rows = here_rows == iota((pairs, pairs), 1)
    at_cols = here_cols == iota((pairs, pairs), 0)
    lse = jnp.sum(jnp.where(at_rows, lse_ref[...], 0.0), axis=1, keepdims=True)
    pos = jnp.sum(jnp.where(at_rows, pos_ref[...], 0), axis=1, keepdims=True)
    hit = (pos == here_cols).astype(f32)
    coef = (jnp.exp(logit_scale * dot_t(queries, passages) - lse) - hit).astype(bf16)
    query_grad_ref[...] = (logit_scale * dot(coef, passages))[:own].astype(bf16)
    same = iota((pairs, pairs), 0) == iota((pairs, pairs), 1)
    lse = jnp.sum(jnp.where(same, lse, 0.0), axis=0, keepdims=True)
    pos = jnp.sum(jnp.where(same, pos, 0), axis=0, keepdims=True)
    hit = (pos == here_rows).astype(f32)
    turned = (jnp.exp(logit_scale * dot_t(passages, queries) - lse) - hit).astype(bf16)
    turned = dot(at_cols.astype(f32).astype(bf16), turned).astype(bf16)
    pass_grad = logit_scale * dot(turned, queries)
    low_ref[:, :features] = (gain_all[...] * pass_grad).astype(bf16)
    row = iota((pairs, lane), 0)
    tokens = dest_ref.shape[1]
    table = jnp.zeros((pairs, lane), f32)
    for n in range(-(-tokens // lane)):
        some = dest_ref[:, n * lane : min(tokens, (n + 1) * lane)].astype(f32)
        table = jnp.where(row == n, widen(some), table)
    table = jnp.where(row == -(-tokens // lane), widen(len_ref[...].astype(f32)), table)
    low_ref[:, features:] = table.astype(bf16)


def widen(row):
    short = lane - row.shape[1]
    return jnp.concatenate([row, jnp.zeros((1, short), f32)], axis=1) if short else row


def group_part(parts, row_lse, positive, token_lengths, destination, features, blk):
    own = parts[0].shape[0]
    pairs = row_lse.shape[0]
    return pl.pallas_call(
        lambda *refs: group_body(pairs // own, *refs),
        in_specs=[pl.BlockSpec(memory_space=pltpu.SMEM)]
        + [pl.BlockSpec(memory_space=pltpu.VMEM)] * (len(parts) + 4),
        out_specs=[pl.BlockSpec(memory_space=pltpu.VMEM)] * 2,
        out_shape=[
            jax.ShapeDtypeStruct((own, features), bf16),
            jax.ShapeDtypeStruct((pairs, features + lane), bf16),
        ],
        scratch_shapes=[
            pltpu.VMEM((pairs, features), f32),
            pltpu.VMEM((pairs, features), f32),
            pltpu.VMEM((1, features), f32),
        ],
        compiler_params=params(),
        cost_estimate=cost(8 * pairs * pairs * features, 8 * pairs * features),
    )(
        blk[None],
        *parts,
        row_lse[None],
        positive[None],
        destination.reshape(1, -1),
        token_lengths,
    )


def earlier_of(tokens):
    return (iota((tokens, tokens), 0) < iota((tokens, tokens), 1)).astype(bf16)


def pack_body(terms, wide_ref, dest_ref, own_ref, *rest):
    outs = rest[terms:]
    groups, slots = len(outs), outs[0].shape[0]
    tokens = dest_ref.shape[1]
    stride = -(-slots // 16) * 16
    hidden = own_ref[...]
    for term in rest[:terms]:
        hidden = hidden + term[...].astype(f32)
    partner = dest_ref[...] ^ wide_ref[0]
    hit = (partner == iota((groups, tokens), 0)).astype(f32)
    rank = dot(hit.astype(bf16), earlier_of(tokens))
    rank = jnp.sum(rank * hit, axis=0, keepdims=True).astype(i32)
    place = iota((groups * stride, tokens), 0) == partner * stride + rank
    packed = dot(place.astype(f32).astype(bf16), hidden.astype(bf16)).astype(bf16)
    for k in range(groups):
        outs[k][...] = packed[k * stride : k * stride + slots]


def pack(wide, destination, own, terms, groups, slots):
    tokens, width = own.shape
    tile = tile_of(width, 512)
    column_spec = pl.BlockSpec((tokens, tile), lambda j, g: (0, j))
    return pl.pallas_call(
        lambda *refs: pack_body(len(terms), *refs),
        grid_spec=pltpu.PrefetchScalarGridSpec(
            num_scalar_prefetch=1,
            grid=(width // tile,),
            in_specs=[pl.BlockSpec((1, tokens), lambda j, g: (0, 0))]
            + [column_spec] * (1 + len(terms)),
            out_specs=[pl.BlockSpec((slots, tile), lambda j, g: (0, j))] * groups,
        ),
        out_shape=[jax.ShapeDtypeStruct((slots, width), bf16)] * groups,
        compiler_params=params(),
        cost_estimate=cost(4 * groups * slots * tokens * width, 10 * tokens * width),
    )(wide[None], destination.reshape(1, tokens), own, *terms)


def assemble_body(wide_ref, *refs):
    parts, out_ref = refs[:-1], refs[-1]
    slots = parts[0].shape[0]
    rows = out_ref.shape[0]
    row, column = iota((rows, slots), 0), iota((rows, slots), 1)
    total = 0.0
    for k, part in enumerate(parts):
        group = wide_ref[0] ^ k
        place = (row == group * slots + column).astype(f32).astype(bf16)
        total = total + dot(place, part[...])
    out_ref[...] = total.astype(bf16)


def assemble(wide, parts):
    slots, width = parts[0].shape
    rows = slots * len(parts)
    return pl.pallas_call(
        assemble_body,
        in_specs=[pl.BlockSpec(memory_space=pltpu.SMEM)]
        + [pl.BlockSpec(memory_space=pltpu.VMEM)] * len(parts),
        out_specs=pl.BlockSpec(memory_space=pltpu.VMEM),
        out_shape=jax.ShapeDtypeStruct((rows, width), bf16),
        compiler_params=params(),
        cost_estimate=cost(2 * rows * rows * width, 4 * rows * width),
    )(wide[None], *parts)


def slots_body(groups, slots, wide_ref, table_ref, hot_ref, share_ref):
    rows, columns = hot_ref.shape
    pairs = columns // groups
    blocks = -(-slots * groups * 2 // 3 // lane)
    table = table_ref[...]

    def tables(n):
        at = iota((groups, columns), 1) == iota((groups, columns), 0) * pairs + n
        return dot(at.astype(f32).astype(bf16), table)

    spread = (iota((rows, groups), 0) // slots == iota((rows, groups), 1)).astype(f32).astype(bf16)
    lengths = tables(blocks)
    upto = (iota((lane, lane), 0) <= iota((lane, lane), 1)).astype(f32).astype(bf16)
    ends = dot(lengths.astype(bf16), upto)
    slot = iota((rows, lane), 0) % slots
    before = jnp.zeros((groups, 1), f32)
    taken = jnp.zeros((rows, 1), f32)
    for n in range(blocks):
        token = iota((groups, lane), 1) + n * lane
        hit = (tables(n).astype(i32) == wide_ref[0]) & (token < slots * groups * 2 // 3)
        count = hit.astype(f32)
        rank = before + dot(count.astype(bf16), earlier_of(lane))
        before = before + jnp.sum(count, axis=1, keepdims=True)
        passage = jnp.ones((groups, lane), f32)
        for pair in range(pairs):
            passage = passage + (token.astype(f32) >= ends[:, pair : pair + 1]).astype(f32)
        code = jnp.where(hit, passage, 0.0)
        rank_rows = dot(spread, rank.astype(bf16)).astype(i32)
        code_rows = dot(spread, code.astype(bf16))
        taken = taken + jnp.sum(
            jnp.where(rank_rows == slot, code_rows, 0.0), axis=1, keepdims=True
        )
    taken = taken.astype(i32)
    column = iota((rows, columns), 1)
    first = iota((rows, columns), 0) // slots * pairs
    hot = (taken > 0) & (column == first + taken - 1)
    hot_ref[...] = hot.astype(f32).astype(bf16)
    length_rows = dot(spread, lengths.astype(bf16))
    length = jnp.where(iota((rows, lane), 1) == taken - 1, length_rows, 0.0)
    length = jnp.sum(length, axis=1, keepdims=True)
    share_ref[...] = jnp.where(taken > 0, 1.0 / jnp.maximum(length, 1.0), 0.0)


def slot_passages(wide, low, features, groups, slots, rows):
    columns = low.shape[0]
    return pl.pallas_call(
        lambda *refs: slots_body(groups, slots, *refs),
        grid=(1,),
        in_specs=[
            pl.BlockSpec(memory_space=pltpu.SMEM),
            pl.BlockSpec((columns, lane), lambda j: (0, features // lane)),
        ],
        out_specs=[
            pl.BlockSpec((rows, columns), lambda j: (0, 0)),
            pl.BlockSpec((rows, 1), lambda j: (0, 0)),
        ],
        out_shape=[
            jax.ShapeDtypeStruct((rows, columns), bf16),
            jax.ShapeDtypeStruct((rows, 1), f32),
        ],
        compiler_params=params(),
        cost_estimate=cost(4 * rows * groups * lane, 2 * rows * columns),
    )(wide[None], low)


def low_act_body(part, low_ref, w_hbm, *refs):
    out_ref, weights, sems = refs[-3:]
    count, tile, _ = weights.shape

    def weight_copy(t):
        rows = pl.ds(pl.multiple_of((part * count + t) * tile, tile), tile)
        return pltpu.make_async_copy(w_hbm.at[rows], weights.at[t], sems.at[t])

    for t in range(count):
        weight_copy(t).start()

    @pl.loop(0, count)
    def _(t):
        weight_copy(t).wait()
        rows = pl.ds(pl.multiple_of(t * tile, tile), tile)
        out_ref[rows] = dot_t(weights[t], low_ref[...]).astype(bf16)


def low_activations(low, features, w_down, part, parts, filled=()):
    pairs = low.shape[0]
    depth = w_down.shape[0]
    some = depth // parts
    tile = tile_of(some, 512)
    count = some // tile
    anywhere = pl.BlockSpec(memory_space=pl.ANY)
    return pl.pallas_call(
        lambda *refs: low_act_body(part, *refs),
        grid=(1,),
        in_specs=[pl.BlockSpec((pairs, features), lambda j: (0, 0)), anywhere]
        + [anywhere] * len(filled),
        out_specs=pl.BlockSpec((some, pairs), lambda j: (part, 0)),
        out_shape=jax.ShapeDtypeStruct((depth, pairs), bf16),
        scratch_shapes=[
            pltpu.VMEM((count, tile, features), bf16),
            pltpu.SemaphoreType.DMA((count,)),
        ],
        input_output_aliases={2: 0} if filled else {},
        compiler_params=params(),
        cost_estimate=cost(2 * pairs * some * features, 2 * some * features),
    )(low, w_down, *filled)


def statistics(hids, lows):
    squares, cross = 0.0, 0.0
    for hid_ref, low_ref in zip(hids, lows):
        hid = hid_ref[...].astype(f32)
        squares = squares + jnp.sum(hid * hid, axis=1, keepdims=True)
        cross = cross + dot_t(hid_ref[...], low_ref[...])
    return squares, cross


def product(hids, weights):
    total = 0.0
    for hid_ref, w_ref in zip(hids, weights):
        total = total + dot_t(hid_ref[...], w_ref[...])
    return total


def weight_specs(count, tile, width):
    return [
        pl.BlockSpec((tile // 2, width), lambda j, g, n=n, side=side: (2 * j + side, g[n]))
        for n in range(count)
        for side in range(2)
    ]


def low_specs(count, pairs, width):
    return [pl.BlockSpec((pairs, width), lambda j, g, n=n: (0, g[n])) for n in range(count)]


def back_body(count, carried, places_ref, *refs):
    hids, weights, refs = refs[:count], refs[count : 3 * count], refs[3 * count :]
    lows, before, (acc_ref, squares_ref, cross_ref) = refs[:count], refs[count:-3], refs[-3:]

    @pl.when(pl.program_id(0) == 0)
    def _():
        squares, cross = statistics(hids, lows)
        if carried:
            squares, cross = before[1][...] + squares, before[2][...] + cross
        squares_ref[...], cross_ref[...] = squares, cross

    half = acc_ref.shape[1] // 2
    for side in range(2):
        at = slice(side * half, (side + 1) * half)
        total = product(hids, weights[side::2])
        acc_ref[:, at] = before[0][:, at] + total if carried else total


def carried_specs(rows, pairs, tile):
    return [
        pl.BlockSpec((rows, tile), lambda j, g: (0, j)),
        pl.BlockSpec((rows, 1), lambda j, g: (0, 0)),
        pl.BlockSpec((rows, pairs), lambda j, g: (0, 0)),
    ]


def back(places, pieces, w_down, low, before=()):
    count = len(pieces)
    rows, width = pieces[0].shape
    depth = w_down.shape[0]
    pairs = low.shape[0]
    tile = tile_of(depth, 512)
    totals = carried_specs(rows, pairs, tile)
    return pl.pallas_call(
        lambda *refs: back_body(count, len(before), *refs),
        grid_spec=pltpu.PrefetchScalarGridSpec(
            num_scalar_prefetch=1,
            grid=(depth // tile,),
            in_specs=[pl.BlockSpec((rows, width), lambda j, g: (0, 0))] * count
            + weight_specs(count, tile, width)
            + low_specs(count, pairs, width)
            + totals[: len(before)],
            out_specs=totals,
        ),
        out_shape=[
            jax.ShapeDtypeStruct((rows, depth), f32),
            jax.ShapeDtypeStruct((rows, 1), f32),
            jax.ShapeDtypeStruct((rows, pairs), f32),
        ],
        compiler_params=params(),
        cost_estimate=cost(2 * rows * depth * width * count, 2 * depth * width * count),
    )(places, *pieces, *[w_down] * 2 * count, *[low] * count, *before)


def finish_body(features, count, places_ref, *refs):
    hids, weights, refs = refs[:count], refs[count : count + 2], refs[count + 2 :]
    low_ref, acc_ref, squares_ref, cross_ref, hot_ref, share_ref, low_act_ref = refs[:7]
    own_ref, own_low_ref, gain_ref, act_out, resid_out, normed_out = refs[7:13]
    hid, lead, pull, scale = refs[13:]
    part = hids[0].shape[0]
    step = own_ref.shape[0]

    @pl.when(pl.program_id(0) == 0)
    def _():
        for n in range(count):
            hid[n * part : (n + 1) * part] = hids[n][...]
        squares, cross = statistics([hid], [low_ref])
        hot = hot_ref[...].astype(f32)
        inner = jnp.sum((cross_ref[...] + cross) * hot, axis=1, keepdims=True) * share_ref[...]
        inv_rms = lax.rsqrt((squares_ref[...] + squares) / features + norm_eps)
        scale[...] = inv_rms
        lead[...] = inv_rms * share_ref[...]
        pull[...] = inv_rms * inv_rms * inv_rms * inner / features

    half = act_out.shape[1] // 2
    for side in range(2):
        at = slice(side * half, (side + 1) * half)
        low_act = dot_t(hot_ref[...], low_act_ref[at])
        hid_act = acc_ref[:, at] + product([hid], weights[side : side + 1])
        act_out[:, at] = (lead[...] * low_act - pull[...] * hid_act).astype(bf16)
    rows = pl.ds(pl.multiple_of(pl.program_id(0) * step, step), step)
    own = own_ref[...].astype(f32)
    own_low = dot(hot_ref[rows], own_low_ref[...])
    resid_out[...] = (lead[rows] * own_low - own * pull[rows]).astype(bf16)
    normed_out[...] = (gain_ref[...] * own * scale[rows]).astype(bf16)


def finish(places, pieces, w_down, low, before, hot, share, low_act, own, gain):
    count = len(pieces)
    rows, width = own.shape
    depth, features = w_down.shape
    pairs = hot.shape[1]
    tile = tile_of(depth, 512)
    steps = depth // tile
    step = rows // steps

    def whole(shape):
        return pl.BlockSpec(shape, lambda j, g: (0, 0))

    row_spec = pl.BlockSpec((step, width), lambda j, g: (j, 0))
    return pl.pallas_call(
        lambda *refs: finish_body(features, count, *refs),
        grid_spec=pltpu.PrefetchScalarGridSpec(
            num_scalar_prefetch=1,
            grid=(steps,),
            in_specs=[whole((rows // count, width))] * count
            + weight_specs(1, tile, width)
            + low_specs(1, pairs, width)
            + carried_specs(rows, pairs, tile)
            + [
                whole((rows, pairs)),
                whole((rows, 1)),
                pl.BlockSpec((tile, pairs), lambda j, g: (j, 0)),
                row_spec,
                pl.BlockSpec((pairs, width), lambda j, g: (0, g[1])),
                whole((1, width)),
            ],
            out_specs=[pl.BlockSpec((rows, tile), lambda j, g: (0, j)), row_spec, row_spec],
            scratch_shapes=[pltpu.VMEM((rows, width), bf16)] + [pltpu.VMEM((rows, 1), f32)] * 3,
        ),
        out_shape=[
            jax.ShapeDtypeStruct((rows, depth), bf16),
            jax.ShapeDtypeStruct((rows, width), bf16),
            jax.ShapeDtypeStruct((rows, width), bf16),
        ],
        compiler_params=params(),
        cost_estimate=cost(2 * rows * depth * width, 2 * depth * width + 6 * rows * depth),
    )(
        places,
        *pieces,
        *[w_down] * 2,
        low,
        *before,
        hot,
        share,
        low_act,
        own,
        low,
        gain,
    )


def low_rank_shards(
    query_emb,
    passage_emb,
    row_lse,
    positive,
    token_lengths,
    destination,
    mlp_act,
    resid,
    w_down,
    gain,
):
    wide_count = lax.axis_size("wide")
    blk, wide = lax.axis_index("blk"), lax.axis_index("wide")
    tok_count, width = resid.shape
    features = w_down.shape[1]
    pairs = row_lse.shape[0]
    slot_count = 3 * tok_count // (2 * wide_count)
    rows = wide_count * slot_count

    both = payload(query_emb, passage_emb, gain)
    parts = [both] + [swap(both, k) for k in (1, 2, 3)]
    first_term = project((blk ^ 3)[None], mlp_act, w_down, width)
    arrived = [swap(first_term, 3)]
    parts = after(first_term, *parts)[1:]
    query_grad, low_own = group_part(
        parts, row_lse, positive, token_lengths, destination, features, blk
    )
    mlp_act = after(low_own, mlp_act)[1]
    for k in (1, 2):
        arrived.append(swap(project((blk ^ k)[None], mlp_act, w_down, width), k))
    own_term = project(blk[None], mlp_act, w_down, width, resid)

    low = lax.all_gather(low_own, "wide", axis=0, tiled=True)
    packed = pack(wide, destination, own_term, arrived, wide_count, slot_count)
    routed = [packed[k] if k == 0 else swap(packed[k], k, "wide") for k in range(wide_count)]
    low_act = low_activations(low, features, w_down, 0, 2)
    hot, share = slot_passages(wide, low, features, wide_count, slot_count, rows)
    low_act, hot, share, *routed = lax.optimization_barrier((low_act, hot, share, *routed))
    own = assemble(wide, routed)

    beside, above = swap(own, 1), swap(own, 2)
    totals = back(blk[None], [own], w_down, low)
    low_act = low_activations(low, features, w_down, 1, 2, [low_act])
    low_act, *totals, beside, above = lax.optimization_barrier((low_act, *totals, beside, above))
    top = swap(beside[: rows // 2], 2)
    bottom = swap(above[rows // 2 :], 1)
    totals = back(jnp.stack([blk ^ 1, blk ^ 2]), [beside, above], w_down, low, totals)
    act_grad, resid_grad, normed_out = finish(
        jnp.stack([blk ^ 3, blk]),
        [top, bottom],
        w_down,
        low,
        totals,
        hot,
        share,
        low_act,
        own,
        gain[None],
    )
    return (query_grad, resid_grad, act_grad, normed_out)


def coefficients(scores, lse_part, pos_part):
    columns = lax.broadcasted_iota(jnp.int32, scores.shape, 1)
    target = (pos_part[:, None] == columns).astype(jnp.float32)
    return (jnp.exp(scores - lse_part[:, None]) - target).astype(jnp.bfloat16)


def place_rows(destination, wide_count, slot_count):
    tok_count = destination.shape[0]
    dest_hot = (destination == lax.broadcasted_iota(jnp.int32, (tok_count, wide_count), 1)).astype(
        bf16
    )
    token = lax.iota(jnp.int32, tok_count)
    earlier = (token[None, :] < token[:, None]).astype(bf16)
    rank_of = jnp.dot(earlier, dest_hot, preferred_element_type=f32)
    slot_of = jnp.sum(rank_of * dest_hot.astype(f32), axis=1).astype(jnp.int32)
    slot_of = slot_of + destination[:, 0] * slot_count
    return (
        lax.broadcasted_iota(jnp.int32, (wide_count * slot_count, tok_count), 0) == slot_of[None, :]
    ).astype(bf16)


def row_shards(
    query_emb,
    passage_emb,
    row_lse,
    positive,
    token_lengths,
    destination,
    mlp_act,
    resid,
    w_down,
    gain,
):
    pair_rows = query_emb.shape[0]
    tok_count, feat_width = resid.shape
    features = w_down.shape[1]
    blk_index = lax.axis_index("blk")
    wide_count = lax.axis_size("wide")
    slot_count = 3 * tok_count // (2 * wide_count)
    offset = blk_index * feat_width
    query_all = lax.all_gather(query_emb, "blk", axis=0, tiled=True)
    passage_all = lax.all_gather(passage_emb, "blk", axis=0, tiled=True)
    scores = logit_scale * jnp.dot(query_all, passage_all.T, preferred_element_type=f32)
    coef_full = coefficients(scores, row_lse, positive)
    own_coef = lax.dynamic_slice_in_dim(coef_full, blk_index * pair_rows, pair_rows, 0)
    query_grad = (
        logit_scale * jnp.dot(own_coef, passage_all, preferred_element_type=f32)
    ).astype(bf16)
    query_cols = lax.dynamic_slice_in_dim(query_all, offset, feat_width, 1)
    grad_cols = logit_scale * lax.dot_general(
        query_cols, coef_full, (((0,), (0,)), ((), ())), preferred_element_type=f32
    )
    lengths_row = token_lengths[0]
    starts = jnp.cumsum(lengths_row) - lengths_row
    positions = lax.broadcasted_iota(jnp.int32, (tok_count, lengths_row.shape[0]), 0)
    member = (positions >= starts[None, :]) & (positions < (starts + lengths_row)[None, :])
    weights = member.astype(f32) * (1.0 / lengths_row.astype(f32))[None, :]
    tok_grad = lax.dot_general(
        weights,
        grad_cols,
        (((1,), (1,)), ((), ())),
        precision=lax.Precision.HIGHEST,
        preferred_element_type=f32,
    ).astype(bf16)
    terms = jnp.dot(mlp_act, w_down, preferred_element_type=f32)
    own = lax.dynamic_slice_in_dim(terms, offset, feat_width, 1) + resid.astype(f32)
    terms = lax.dynamic_update_slice_in_dim(terms, own, offset, 1)
    hidden = lax.psum_scatter(terms.astype(bf16), "blk", scatter_dimension=1, tiled=True)
    placer = place_rows(destination, wide_count, slot_count)
    payload = jnp.concatenate([hidden, tok_grad], axis=1)
    packed = jnp.dot(placer, payload, preferred_element_type=f32).astype(bf16)
    packed = packed.reshape(wide_count, slot_count, 2 * feat_width)
    rows = lax.all_to_all(packed, "wide", split_axis=0, concat_axis=0, tiled=True).reshape(
        wide_count * slot_count, 2 * feat_width
    )
    hidden = rows[:, :feat_width].astype(f32)
    gained = gain[None, :] * rows[:, feat_width:].astype(f32)
    squares, inner_sum = lax.psum(
        (jnp.sum(hidden * hidden, axis=1), jnp.sum(gained * hidden, axis=1)), "blk"
    )
    inv_rms = lax.rsqrt(squares / features + norm_eps)[:, None]
    normed = (gain[None, :] * hidden * inv_rms).astype(bf16)
    resid_back = (
        inv_rms * gained - hidden * (inv_rms * inv_rms * inv_rms) * inner_sum[:, None] / features
    ).astype(bf16)
    act_back = dot_t(lax.all_gather(resid_back, "blk", axis=1, tiled=True), w_down)
    return (query_grad, resid_back, act_back.astype(bf16), normed)


def solution(mesh):
    blk_count, wide_count = mesh.shape["blk"], mesh.shape["wide"]

    def shards(*operands):
        pairs, tok_count = operands[2].shape[0], operands[7].shape[0]
        low_rank = 2 * wide_count * pairs <= 3 * tok_count
        per_pair = tok_count // pairs
        aligned = operands[9].shape[0] % (lane * operands[0].shape[0]) == 0 and wide_count <= lane
        if low_rank and blk_count == 4 and aligned and per_pair * pairs == tok_count and wide_count & (wide_count - 1) == 0:
            return low_rank_shards(*operands)
        return row_shards(*operands)

    return jax.shard_map(
        shards,
        mesh=mesh,
        in_specs=(
            P(("wide", "blk"), None),
            P(("wide", "blk"), None),
            P("wide"),
            P("wide"),
            P("wide", None),
            P("wide", None),
            P("wide", "blk"),
            P("wide", "blk"),
            P("blk", None),
            P("blk"),
        ),
        out_specs=(P(("wide", "blk"), None), P("wide", "blk"), P("wide", "blk"), P("wide", "blk")),
        check_vma=False,
    )
```

```python
import jax
import jax.numpy as jnp
from jax import lax
from jax.experimental import pallas as pl
from jax.experimental.pallas import tpu as pltpu
from jax.sharding import PartitionSpec as P

logit_scale = 24.0
norm_eps = 1e-06
f32 = jnp.float32
bf16 = jnp.bfloat16
i32 = jnp.int32
lane = 128
kernel_vmem = 46 * 1024 * 1024
whole_vmem = 60 * 1024 * 1024


def params(vmem=kernel_vmem):
    return pltpu.CompilerParams(vmem_limit_bytes=vmem)


def cost(flops, nbytes):
    return pl.CostEstimate(flops=flops, bytes_accessed=nbytes, transcendentals=0)


def tile_of(extent, most):
    tile = most
    while extent % tile:
        tile //= 2
    return tile


def iota(shape, dim):
    return lax.broadcasted_iota(i32, shape, dim)


def dot(left, right):
    return jnp.dot(left, right, preferred_element_type=f32)


def dot_t(left, right):
    return lax.dot_general(left, right, (((1,), (1,)), ((), ())), preferred_element_type=f32)


def swap(rows, k, axis="blk"):
    return lax.ppermute(rows, axis, [(i, i ^ k) for i in range(lax.axis_size(axis))])


def after(first, *later):
    return lax.optimization_barrier((first, *later))


def project_body(tiles_each, has_resid, starts_ref, act_hbm, w_hbm, *refs):
    outs, (act, weights, act_sem, sems) = refs[has_resid:-4], refs[-4:]
    count, _, tile = weights.shape

    def weight_copy(i):
        columns = pl.ds(pl.multiple_of(starts_ref[i] * tile, lane), tile)
        return pltpu.make_async_copy(w_hbm.at[:, columns], weights.at[i], sems.at[i])

    act_copy = pltpu.make_async_copy(act_hbm, act, act_sem)
    act_copy.start()
    for i in range(count):
        weight_copy(i).start()
    act_copy.wait()
    for n, out_ref in enumerate(outs):

        @pl.loop(0, tiles_each)
        def _(i):
            weight_copy(n * tiles_each + i).wait()
            columns = pl.ds(pl.multiple_of(i * tile, lane), tile)
            term = dot(act[...], weights[n * tiles_each + i])
            if has_resid:
                term = term + refs[0][:, columns].astype(f32)
            out_ref[:, columns] = term.astype(out_ref.dtype)


def project(pieces, act, w_down, width, resid=None):
    rows, depth = act.shape
    tile = tile_of(width, 256)
    each = width // tile
    count = each * len(pieces)
    starts = jnp.stack([piece * each + i for piece in pieces for i in range(each)])
    own = [] if resid is None else [resid]
    return pl.pallas_call(
        lambda *refs: project_body(each, len(own), *refs),
        in_specs=[pl.BlockSpec(memory_space=pltpu.SMEM)]
        + [pl.BlockSpec(memory_space=pl.ANY)] * 2
        + [pl.BlockSpec(memory_space=pltpu.VMEM)] * len(own),
        out_specs=[pl.BlockSpec(memory_space=pltpu.VMEM)] * len(pieces),
        out_shape=[jax.ShapeDtypeStruct((rows, width), f32 if own else bf16)] * len(pieces),
        scratch_shapes=[
            pltpu.VMEM((rows, depth), bf16),
            pltpu.VMEM((count, depth, tile), bf16),
            pltpu.SemaphoreType.DMA,
            pltpu.SemaphoreType.DMA((count,)),
        ],
        compiler_params=params(),
        cost_estimate=cost(2 * rows * depth * tile * count, 2 * depth * (tile * count + rows)),
    )(starts, act, w_down, *own)


def payload_body(query_ref, passage_ref, gain_ref, out_ref, gains):
    own, features = query_ref.shape
    piece = gains.shape[1]
    for row in range(own):
        gains[row : row + 1] = gain_ref[:, row * piece : (row + 1) * piece]
    gain = gains[...]
    high = gain.astype(bf16)
    out_ref[:, :features] = query_ref[...]
    out_ref[:, features : 2 * features] = passage_ref[...]
    out_ref[:, 2 * features : 2 * features + piece] = high
    out_ref[:, 2 * features + piece :] = (gain - high.astype(f32)).astype(bf16)


def payload(query_emb, passage_emb, gain):
    own, features = query_emb.shape
    piece = gain.shape[0] // own
    return pl.pallas_call(
        payload_body,
        out_shape=jax.ShapeDtypeStruct((own, 2 * features + 2 * piece), bf16),
        scratch_shapes=[pltpu.VMEM((own, piece), f32)],
        compiler_params=params(whole_vmem),
        cost_estimate=cost(own * features, 8 * own * features),
    )(query_emb, passage_emb, gain[None])


def group_body(count, blk_ref, *refs):
    parts, refs = refs[:count], refs[count:]
    lse_ref, pos_ref, dest_ref, len_ref = refs[:4]
    query_grad_ref, low_ref, query_all, passage_all, gain_all = refs[4:]
    own, features = query_grad_ref.shape
    pairs = own * count
    piece = features // pairs
    blk = blk_ref[0]
    for k in range(count):
        query_all[k * own : (k + 1) * own] = parts[k][:, :features].astype(f32)
        passage_all[k * own : (k + 1) * own] = parts[k][:, features : 2 * features].astype(f32)
        gains = parts[k][:, 2 * features : 2 * features + piece].astype(f32)
        gains = gains + parts[k][:, 2 * features + piece :].astype(f32)
        for row in range(own):
            first = pl.multiple_of(((blk ^ k) * own + row) * piece, lane)
            gain_all[:, pl.ds(first, piece)] = gains[row : row + 1]
    queries = query_all[...].astype(bf16)
    passages = passage_all[...].astype(bf16)

    def named(dim):
        place = iota((pairs, pairs), dim)
        return (blk ^ (place // own)) * own + place % own

    here_rows, here_cols = named(0), named(1)
    at_rows = here_rows == iota((pairs, pairs), 1)
    at_cols = here_cols == iota((pairs, pairs), 0)
    lse = jnp.sum(jnp.where(at_rows, lse_ref[...], 0.0), axis=1, keepdims=True)
    pos = jnp.sum(jnp.where(at_rows, pos_ref[...], 0), axis=1, keepdims=True)
    hit = (pos == here_cols).astype(f32)
    coef = (jnp.exp(logit_scale * dot_t(queries, passages) - lse) - hit).astype(bf16)
    query_grad_ref[...] = (logit_scale * dot(coef, passages))[:own].astype(bf16)
    same = iota((pairs, pairs), 0) == iota((pairs, pairs), 1)
    lse = jnp.sum(jnp.where(same, lse, 0.0), axis=0, keepdims=True)
    pos = jnp.sum(jnp.where(same, pos, 0), axis=0, keepdims=True)
    hit = (pos == here_rows).astype(f32)
    turned = (jnp.exp(logit_scale * dot_t(passages, queries) - lse) - hit).astype(bf16)
    turned = dot(at_cols.astype(f32).astype(bf16), turned).astype(bf16)
    pass_grad = logit_scale * dot(turned, queries)
    low_ref[:, :features] = (gain_all[...] * pass_grad).astype(bf16)
    row = iota((pairs, lane), 0)
    tokens = dest_ref.shape[1]
    table = jnp.zeros((pairs, lane), f32)
    for n in range(-(-tokens // lane)):
        some = dest_ref[:, n * lane : min(tokens, (n + 1) * lane)].astype(f32)
        table = jnp.where(row == n, widen(some), table)
    table = jnp.where(row == -(-tokens // lane), widen(len_ref[...].astype(f32)), table)
    low_ref[:, features:] = table.astype(bf16)


def widen(row):
    short = lane - row.shape[1]
    return jnp.concatenate([row, jnp.zeros((1, short), f32)], axis=1) if short else row


def group_part(parts, row_lse, positive, token_lengths, destination, features, blk):
    own = parts[0].shape[0]
    pairs = row_lse.shape[0]
    return pl.pallas_call(
        lambda *refs: group_body(pairs // own, *refs),
        in_specs=[pl.BlockSpec(memory_space=pltpu.SMEM)]
        + [pl.BlockSpec(memory_space=pltpu.VMEM)] * (len(parts) + 4),
        out_specs=[pl.BlockSpec(memory_space=pltpu.VMEM)] * 2,
        out_shape=[
            jax.ShapeDtypeStruct((own, features), bf16),
            jax.ShapeDtypeStruct((pairs, features + lane), bf16),
        ],
        scratch_shapes=[
            pltpu.VMEM((pairs, features), f32),
            pltpu.VMEM((pairs, features), f32),
            pltpu.VMEM((1, features), f32),
        ],
        compiler_params=params(),
        cost_estimate=cost(8 * pairs * pairs * features, 8 * pairs * features),
    )(
        blk[None],
        *parts,
        row_lse[None],
        positive[None],
        destination.reshape(1, -1),
        token_lengths,
    )


def earlier_of(tokens):
    return (iota((tokens, tokens), 0) < iota((tokens, tokens), 1)).astype(bf16)


def pack_body(wide_ref, dest_ref, own_ref, far_ref, *rest):
    halves, outs = rest[:4], rest[4:]
    groups, slots = len(outs), outs[0].shape[0]
    tokens = dest_ref.shape[1]
    stride = -(-slots // 16) * 16
    hidden = own_ref[...] + far_ref[...].astype(f32)
    for left, right in (halves[:2], halves[2:]):
        hidden = hidden + jnp.where(
            pl.program_id(0) == 0, left[...].astype(f32), right[...].astype(f32)
        )
    partner = dest_ref[...] ^ wide_ref[0]
    hit = (partner == iota((groups, tokens), 0)).astype(f32)
    rank = dot(hit.astype(bf16), earlier_of(tokens))
    rank = jnp.sum(rank * hit, axis=0, keepdims=True).astype(i32)
    place = iota((groups * stride, tokens), 0) == partner * stride + rank
    packed = dot(place.astype(f32).astype(bf16), hidden.astype(bf16)).astype(bf16)
    for k in range(groups):
        outs[k][...] = packed[k * stride : k * stride + slots]


def pack(wide, destination, own, far, halves, groups, slots):
    tokens, width = own.shape
    tile = width // 2
    column_spec = pl.BlockSpec((tokens, tile), lambda j, g: (0, j))
    return pl.pallas_call(
        pack_body,
        grid_spec=pltpu.PrefetchScalarGridSpec(
            num_scalar_prefetch=1,
            grid=(width // tile,),
            in_specs=[pl.BlockSpec((1, tokens), lambda j, g: (0, 0))]
            + [column_spec] * 2
            + [pl.BlockSpec((tokens, tile), lambda j, g: (0, 0))] * len(halves),
            out_specs=[pl.BlockSpec((slots, tile), lambda j, g: (0, j))] * groups,
        ),
        out_shape=[jax.ShapeDtypeStruct((slots, width), bf16)] * groups,
        compiler_params=params(),
        cost_estimate=cost(4 * groups * slots * tokens * width, 10 * tokens * width),
    )(wide[None], destination.reshape(1, tokens), own, far, *halves)


def assemble_body(wide_ref, *refs):
    parts, out_ref = refs[:-1], refs[-1]
    slots = parts[0].shape[0]
    rows = out_ref.shape[0]
    row, column = iota((rows, slots), 0), iota((rows, slots), 1)
    total = 0.0
    for n, part in enumerate(parts):
        group = wide_ref[0] ^ (len(parts) - 1 - n)
        place = (row == group * slots + column).astype(f32).astype(bf16)
        total = total + dot(place, part[...])
    out_ref[...] = total.astype(bf16)


def assemble(wide, parts):
    slots, width = parts[0].shape
    rows = slots * len(parts)
    return pl.pallas_call(
        assemble_body,
        in_specs=[pl.BlockSpec(memory_space=pltpu.SMEM)]
        + [pl.BlockSpec(memory_space=pltpu.VMEM)] * len(parts),
        out_specs=pl.BlockSpec(memory_space=pltpu.VMEM),
        out_shape=jax.ShapeDtypeStruct((rows, width), bf16),
        compiler_params=params(),
        cost_estimate=cost(2 * rows * rows * width, 4 * rows * width),
    )(wide[None], *parts)


def slots_body(groups, slots, wide_ref, table_ref, hot_ref, share_ref):
    rows, columns = hot_ref.shape
    pairs = columns // groups
    blocks = -(-slots * groups * 2 // 3 // lane)
    table = table_ref[...]

    def tables(n):
        at = iota((groups, columns), 1) == iota((groups, columns), 0) * pairs + n
        return dot(at.astype(f32).astype(bf16), table)

    spread = (iota((rows, groups), 0) // slots == iota((rows, groups), 1)).astype(f32).astype(bf16)
    lengths = tables(blocks)
    upto = (iota((lane, lane), 0) <= iota((lane, lane), 1)).astype(f32).astype(bf16)
    ends = dot(lengths.astype(bf16), upto)
    slot = iota((rows, lane), 0) % slots
    before = jnp.zeros((groups, 1), f32)
    taken = jnp.zeros((rows, 1), f32)
    for n in range(blocks):
        token = iota((groups, lane), 1) + n * lane
        hit = (tables(n).astype(i32) == wide_ref[0]) & (token < slots * groups * 2 // 3)
        count = hit.astype(f32)
        rank = before + dot(count.astype(bf16), earlier_of(lane))
        before = before + jnp.sum(count, axis=1, keepdims=True)
        passage = jnp.ones((groups, lane), f32)
        for pair in range(pairs):
            passage = passage + (token.astype(f32) >= ends[:, pair : pair + 1]).astype(f32)
        code = jnp.where(hit, passage, 0.0)
        rank_rows = dot(spread, rank.astype(bf16)).astype(i32)
        code_rows = dot(spread, code.astype(bf16))
        taken = taken + jnp.sum(
            jnp.where(rank_rows == slot, code_rows, 0.0), axis=1, keepdims=True
        )
    taken = taken.astype(i32)
    column = iota((rows, columns), 1)
    first = iota((rows, columns), 0) // slots * pairs
    hot = (taken > 0) & (column == first + taken - 1)
    hot_ref[...] = hot.astype(f32).astype(bf16)
    length_rows = dot(spread, lengths.astype(bf16))
    length = jnp.where(iota((rows, lane), 1) == taken - 1, length_rows, 0.0)
    length = jnp.sum(length, axis=1, keepdims=True)
    share_ref[...] = jnp.where(taken > 0, 1.0 / jnp.maximum(length, 1.0), 0.0)


def slot_passages(wide, low, features, groups, slots, rows):
    columns = low.shape[0]
    return pl.pallas_call(
        lambda *refs: slots_body(groups, slots, *refs),
        grid=(1,),
        in_specs=[
            pl.BlockSpec(memory_space=pltpu.SMEM),
            pl.BlockSpec((columns, lane), lambda j: (0, features // lane)),
        ],
        out_specs=[
            pl.BlockSpec((rows, columns), lambda j: (0, 0)),
            pl.BlockSpec((rows, 1), lambda j: (0, 0)),
        ],
        out_shape=[
            jax.ShapeDtypeStruct((rows, columns), bf16),
            jax.ShapeDtypeStruct((rows, 1), f32),
        ],
        compiler_params=params(),
        cost_estimate=cost(4 * rows * groups * lane, 2 * rows * columns),
    )(wide[None], low)


def statistics(hids, lows):
    squares, cross = 0.0, 0.0
    for hid_ref, low_ref in zip(hids, lows):
        hid = hid_ref[...].astype(f32)
        squares = squares + jnp.sum(hid * hid, axis=1, keepdims=True)
        cross = cross + dot_t(hid_ref[...], low_ref[...])
    return squares, cross


def weight_specs(count, tile, width):
    return [
        pl.BlockSpec((tile // 2, width), lambda j, g, n=n, side=side: (2 * j + side, g[n]))
        for n in range(count)
        for side in range(2)
    ]


def low_specs(count, pairs, width):
    return [pl.BlockSpec((pairs, width), lambda j, g, n=n: (0, g[n])) for n in range(count)]


def back_body(count, carried, places_ref, *refs):
    hids, weights, refs = refs[:count], refs[count : 3 * count], refs[3 * count :]
    lows, before = refs[:count], refs[count:-4]
    acc_ref, squares_ref, cross_ref, stack = refs[-4:]
    rows = hids[0].shape[0]

    @pl.when(pl.program_id(0) == 0)
    def _():
        for n in range(count):
            stack[n, :rows] = hids[n][...]
            stack[n, rows:] = lows[n][...]
        squares, cross = statistics(hids, lows)
        if carried:
            squares, cross = before[1][...] + squares, before[2][...] + cross
        squares_ref[...], cross_ref[...] = squares, cross

    half = acc_ref.shape[1] // 2
    for side in range(2):
        at = slice(side * half, (side + 1) * half)
        total = dot_t(stack[0], weights[side][...])
        for n in range(1, count):
            total = total + dot_t(stack[n], weights[2 * n + side][...])
        acc_ref[:, at] = before[0][:, at] + total if carried else total


def carried_specs(rows, pairs, tile):
    return [
        pl.BlockSpec((rows + pairs, tile), lambda j, g: (0, j)),
        pl.BlockSpec((rows, 1), lambda j, g: (0, 0)),
        pl.BlockSpec((rows, pairs), lambda j, g: (0, 0)),
    ]


def back(places, pieces, w_down, low, before=()):
    count = len(pieces)
    rows, width = pieces[0].shape
    depth = w_down.shape[0]
    pairs = low.shape[0]
    tile = tile_of(depth, 512)
    totals = carried_specs(rows, pairs, tile)
    return pl.pallas_call(
        lambda *refs: back_body(count, len(before), *refs),
        grid_spec=pltpu.PrefetchScalarGridSpec(
            num_scalar_prefetch=1,
            grid=(depth // tile,),
            in_specs=[pl.BlockSpec((rows, width), lambda j, g: (0, 0))] * count
            + weight_specs(count, tile, width)
            + low_specs(count, pairs, width)
            + totals[: len(before)],
            out_specs=totals,
            scratch_shapes=[pltpu.VMEM((count, rows + pairs, width), bf16)],
        ),
        out_shape=[
            jax.ShapeDtypeStruct((rows + pairs, depth), f32),
            jax.ShapeDtypeStruct((rows, 1), f32),
            jax.ShapeDtypeStruct((rows, pairs), f32),
        ],
        compiler_params=params(),
        cost_estimate=cost(2 * rows * depth * width * count, 2 * depth * width * count),
    )(places, *pieces, *[w_down] * 2 * count, *[low] * count, *before)


def finish_body(features, count, places_ref, *refs):
    hids, weights, refs = refs[:count], refs[count : count + 2], refs[count + 2 :]
    low_ref, acc_ref, squares_ref, cross_ref, hot_ref, share_ref = refs[:6]
    own_ref, own_low_ref, gain_ref, act_out, resid_out, normed_out = refs[6:12]
    stack, lead, pull, scale = refs[12:]
    count_rows = hot_ref.shape[0]
    part = hids[0].shape[0]
    step = own_ref.shape[0]

    @pl.when(pl.program_id(0) == 0)
    def _():
        for n in range(count):
            stack[n * part : (n + 1) * part] = hids[n][...]
        stack[count_rows:] = low_ref[...]
        squares, cross = statistics([stack.at[:count_rows]], [low_ref])
        hot = hot_ref[...].astype(f32)
        inner = jnp.sum((cross_ref[...] + cross) * hot, axis=1, keepdims=True) * share_ref[...]
        inv_rms = lax.rsqrt((squares_ref[...] + squares) / features + norm_eps)
        scale[...] = inv_rms
        lead[...] = inv_rms * share_ref[...]
        pull[...] = inv_rms * inv_rms * inv_rms * inner / features

    half = act_out.shape[1] // 2
    for side in range(2):
        at = slice(side * half, (side + 1) * half)
        total = acc_ref[:, at] + dot_t(stack[...], weights[side][...])
        low_act = dot(hot_ref[...], total[count_rows:].astype(bf16))
        act_out[:, at] = (lead[...] * low_act - pull[...] * total[:count_rows]).astype(bf16)
    rows = pl.ds(pl.multiple_of(pl.program_id(0) * step, step), step)
    own = own_ref[...].astype(f32)
    own_low = dot(hot_ref[rows], own_low_ref[...])
    resid_out[...] = (lead[rows] * own_low - own * pull[rows]).astype(bf16)
    normed_out[...] = (gain_ref[...] * own * scale[rows]).astype(bf16)


def finish(places, pieces, w_down, low, before, hot, share, own, gain):
    count = len(pieces)
    rows, width = own.shape
    depth, features = w_down.shape
    pairs = hot.shape[1]
    tile = tile_of(depth, 512)
    steps = depth // tile
    step = rows // steps

    def whole(shape):
        return pl.BlockSpec(shape, lambda j, g: (0, 0))

    row_spec = pl.BlockSpec((step, width), lambda j, g: (j, 0))
    return pl.pallas_call(
        lambda *refs: finish_body(features, count, *refs),
        grid_spec=pltpu.PrefetchScalarGridSpec(
            num_scalar_prefetch=1,
            grid=(steps,),
            in_specs=[whole((rows // count, width))] * count
            + weight_specs(1, tile, width)
            + low_specs(1, pairs, width)
            + carried_specs(rows, pairs, tile)
            + [
                whole((rows, pairs)),
                whole((rows, 1)),
                row_spec,
                pl.BlockSpec((pairs, width), lambda j, g: (0, g[1])),
                whole((1, width)),
            ],
            out_specs=[pl.BlockSpec((rows, tile), lambda j, g: (0, j)), row_spec, row_spec],
            scratch_shapes=[pltpu.VMEM((rows + pairs, width), bf16)]
            + [pltpu.VMEM((rows, 1), f32)] * 3,
        ),
        out_shape=[
            jax.ShapeDtypeStruct((rows, depth), bf16),
            jax.ShapeDtypeStruct((rows, width), bf16),
            jax.ShapeDtypeStruct((rows, width), bf16),
        ],
        compiler_params=params(),
        cost_estimate=cost(2 * rows * depth * width, 2 * depth * width + 6 * rows * depth),
    )(
        places,
        *pieces,
        *[w_down] * 2,
        low,
        *before,
        hot,
        share,
        own,
        low,
        gain,
    )


def low_rank_shards(
    query_emb,
    passage_emb,
    row_lse,
    positive,
    token_lengths,
    destination,
    mlp_act,
    resid,
    w_down,
    gain,
):
    wide_count = lax.axis_size("wide")
    blk, wide = lax.axis_index("blk"), lax.axis_index("wide")
    tok_count, width = resid.shape
    features = w_down.shape[1]
    pairs = row_lse.shape[0]
    slot_count = 3 * tok_count // (2 * wide_count)
    rows = wide_count * slot_count

    both = payload(query_emb, passage_emb, gain)
    parts = [both] + [swap(both, k) for k in (1, 2, 3)]
    (first_term,) = project([blk ^ 3], mlp_act, w_down, width)
    far = swap(first_term, 3)
    _, *parts = lax.optimization_barrier((first_term, *parts))
    query_grad, low_own = group_part(
        parts, row_lse, positive, token_lengths, destination, features, blk
    )
    _, mlp_act = lax.optimization_barrier((low_own, mlp_act))
    halves = []
    for side in range(2):
        places = [(blk ^ k) * 2 + side for k in (1, 2)]
        terms = project(places, mlp_act, w_down, width // 2)
        halves += [swap(terms[0], 1), swap(terms[1], 2)]
    (own_term,) = project([blk], mlp_act, w_down, width, resid)

    low = lax.all_gather(low_own, "wide", axis=0, tiled=True)
    packed = pack(wide, destination, own_term, far, halves[::2] + halves[1::2], wide_count, slot_count)
    routed = [swap(packed[k], k, "wide") for k in range(wide_count - 1, 0, -1)] + [packed[0]]

    hot, share = slot_passages(wide, low, features, wide_count, slot_count, rows)
    hot, share, *routed = lax.optimization_barrier((hot, share, *routed))
    own = assemble(wide, routed)

    beside, above = swap(own, 1), swap(own, 2)
    totals = back(blk[None], [own], w_down, low)
    *totals, beside, above = lax.optimization_barrier((*totals, beside, above))
    top = swap(beside[: rows // 2], 2)
    bottom = swap(above[rows // 2 :], 1)
    totals = back(jnp.stack([blk ^ 1, blk ^ 2]), [beside, above], w_down, low, totals)
    act_grad, resid_grad, normed_out = finish(
        jnp.stack([blk ^ 3, blk]),
        [top, bottom],
        w_down,
        low,
        totals,
        hot,
        share,
        own,
        gain[None],
    )
    return (query_grad, resid_grad, act_grad, normed_out)


def coefficients(scores, lse_part, pos_part):
    columns = lax.broadcasted_iota(jnp.int32, scores.shape, 1)
    target = (pos_part[:, None] == columns).astype(jnp.float32)
    return (jnp.exp(scores - lse_part[:, None]) - target).astype(jnp.bfloat16)


def place_rows(destination, wide_count, slot_count):
    tok_count = destination.shape[0]
    dest_hot = (destination == lax.broadcasted_iota(jnp.int32, (tok_count, wide_count), 1)).astype(
        bf16
    )
    token = lax.iota(jnp.int32, tok_count)
    earlier = (token[None, :] < token[:, None]).astype(bf16)
    rank_of = jnp.dot(earlier, dest_hot, preferred_element_type=f32)
    slot_of = jnp.sum(rank_of * dest_hot.astype(f32), axis=1).astype(jnp.int32)
    slot_of = slot_of + destination[:, 0] * slot_count
    return (
        lax.broadcasted_iota(jnp.int32, (wide_count * slot_count, tok_count), 0) == slot_of[None, :]
    ).astype(bf16)


def row_shards(
    query_emb,
    passage_emb,
    row_lse,
    positive,
    token_lengths,
    destination,
    mlp_act,
    resid,
    w_down,
    gain,
):
    pair_rows = query_emb.shape[0]
    tok_count, feat_width = resid.shape
    features = w_down.shape[1]
    blk_index = lax.axis_index("blk")
    wide_count = lax.axis_size("wide")
    slot_count = 3 * tok_count // (2 * wide_count)
    offset = blk_index * feat_width
    query_all = lax.all_gather(query_emb, "blk", axis=0, tiled=True)
    passage_all = lax.all_gather(passage_emb, "blk", axis=0, tiled=True)
    scores = logit_scale * jnp.dot(query_all, passage_all.T, preferred_element_type=f32)
    coef_full = coefficients(scores, row_lse, positive)
    own_coef = lax.dynamic_slice_in_dim(coef_full, blk_index * pair_rows, pair_rows, 0)
    query_grad = (
        logit_scale * jnp.dot(own_coef, passage_all, preferred_element_type=f32)
    ).astype(bf16)
    query_cols = lax.dynamic_slice_in_dim(query_all, offset, feat_width, 1)
    grad_cols = logit_scale * lax.dot_general(
        query_cols, coef_full, (((0,), (0,)), ((), ())), preferred_element_type=f32
    )
    lengths_row = token_lengths[0]
    starts = jnp.cumsum(lengths_row) - lengths_row
    positions = lax.broadcasted_iota(jnp.int32, (tok_count, lengths_row.shape[0]), 0)
    member = (positions >= starts[None, :]) & (positions < (starts + lengths_row)[None, :])
    weights = member.astype(f32) * (1.0 / lengths_row.astype(f32))[None, :]
    tok_grad = lax.dot_general(
        weights,
        grad_cols,
        (((1,), (1,)), ((), ())),
        precision=lax.Precision.HIGHEST,
        preferred_element_type=f32,
    ).astype(bf16)
    terms = jnp.dot(mlp_act, w_down, preferred_element_type=f32)
    own = lax.dynamic_slice_in_dim(terms, offset, feat_width, 1) + resid.astype(f32)
    terms = lax.dynamic_update_slice_in_dim(terms, own, offset, 1)
    hidden = lax.psum_scatter(terms.astype(bf16), "blk", scatter_dimension=1, tiled=True)
    placer = place_rows(destination, wide_count, slot_count)
    payload = jnp.concatenate([hidden, tok_grad], axis=1)
    packed = jnp.dot(placer, payload, preferred_element_type=f32).astype(bf16)
    packed = packed.reshape(wide_count, slot_count, 2 * feat_width)
    rows = lax.all_to_all(packed, "wide", split_axis=0, concat_axis=0, tiled=True).reshape(
        wide_count * slot_count, 2 * feat_width
    )
    hidden = rows[:, :feat_width].astype(f32)
    gained = gain[None, :] * rows[:, feat_width:].astype(f32)
    squares, inner_sum = lax.psum(
        (jnp.sum(hidden * hidden, axis=1), jnp.sum(gained * hidden, axis=1)), "blk"
    )
    inv_rms = lax.rsqrt(squares / features + norm_eps)[:, None]
    normed = (gain[None, :] * hidden * inv_rms).astype(bf16)
    resid_back = (
        inv_rms * gained - hidden * (inv_rms * inv_rms * inv_rms) * inner_sum[:, None] / features
    ).astype(bf16)
    act_back = dot_t(lax.all_gather(resid_back, "blk", axis=1, tiled=True), w_down)
    return (query_grad, resid_back, act_back.astype(bf16), normed)


def solution(mesh):
    blk_count, wide_count = mesh.shape["blk"], mesh.shape["wide"]

    def shards(*operands):
        pairs, tok_count = operands[2].shape[0], operands[7].shape[0]
        low_rank = 2 * wide_count * pairs <= 3 * tok_count
        per_pair = tok_count // pairs
        aligned = operands[9].shape[0] % (lane * operands[0].shape[0]) == 0 and wide_count <= lane
        if low_rank and blk_count == 4 and aligned and per_pair * pairs == tok_count and wide_count & (wide_count - 1) == 0:
            return low_rank_shards(*operands)
        return row_shards(*operands)

    return jax.shard_map(
        shards,
        mesh=mesh,
        in_specs=(
            P(("wide", "blk"), None),
            P(("wide", "blk"), None),
            P("wide"),
            P("wide"),
            P("wide", None),
            P("wide", None),
            P("wide", "blk"),
            P("wide", "blk"),
            P("blk", None),
            P("blk"),
        ),
        out_specs=(P(("wide", "blk"), None), P("wide", "blk"), P("wide", "blk"), P("wide", "blk")),
        check_vma=False,
    )
```

```python
import jax
import jax.numpy as jnp
from jax import lax
from jax.experimental import pallas as pl
from jax.experimental.pallas import tpu as pltpu
from jax.sharding import PartitionSpec as P

logit_scale = 24.0
norm_eps = 1e-06
f32 = jnp.float32
bf16 = jnp.bfloat16
i32 = jnp.int32
lane = 128
kernel_vmem = 46 * 1024 * 1024
whole_vmem = 60 * 1024 * 1024


def params(vmem=kernel_vmem):
    return pltpu.CompilerParams(vmem_limit_bytes=vmem)


def cost(flops, nbytes):
    return pl.CostEstimate(flops=flops, bytes_accessed=nbytes, transcendentals=0)


def tile_of(extent, most):
    tile = most
    while extent % tile:
        tile //= 2
    return tile


def iota(shape, dim):
    return lax.broadcasted_iota(i32, shape, dim)


def dot(left, right):
    return jnp.dot(left, right, preferred_element_type=f32)


def dot_t(left, right):
    return lax.dot_general(left, right, (((1,), (1,)), ((), ())), preferred_element_type=f32)


def swap(rows, k, axis="blk"):
    return lax.ppermute(rows, axis, [(i, i ^ k) for i in range(lax.axis_size(axis))])


def after(first, *later):
    return lax.optimization_barrier((first, *later))


def project_body(has_resid, group_ref, act_hbm, w_hbm, *refs):
    out_ref, act, weights, act_sem, sems = refs[has_resid:]
    width = out_ref.shape[1]
    count, _, tile = weights.shape
    first = group_ref[0] * width

    def weight_copy(i):
        columns = pl.ds(pl.multiple_of(first + i * tile, lane), tile)
        return pltpu.make_async_copy(w_hbm.at[:, columns], weights.at[i], sems.at[i])

    act_copy = pltpu.make_async_copy(act_hbm, act, act_sem)
    act_copy.start()
    for i in range(count):
        weight_copy(i).start()
    act_copy.wait()

    @pl.loop(0, count)
    def _(i):
        weight_copy(i).wait()
        columns = pl.ds(pl.multiple_of(i * tile, lane), tile)
        term = dot(act[...], weights[i])
        if has_resid:
            term = term + refs[0][:, columns].astype(f32)
        out_ref[:, columns] = term.astype(out_ref.dtype)


def project(group, act, w_down, width, resid=None):
    rows, depth = act.shape
    tile = tile_of(width, 256)
    count = width // tile
    own = [] if resid is None else [resid]
    return pl.pallas_call(
        lambda *refs: project_body(len(own), *refs),
        in_specs=[pl.BlockSpec(memory_space=pltpu.SMEM)]
        + [pl.BlockSpec(memory_space=pl.ANY)] * 2
        + [pl.BlockSpec(memory_space=pltpu.VMEM)] * len(own),
        out_specs=pl.BlockSpec(memory_space=pltpu.VMEM),
        out_shape=jax.ShapeDtypeStruct((rows, width), f32 if own else bf16),
        scratch_shapes=[
            pltpu.VMEM((rows, depth), bf16),
            pltpu.VMEM((count, depth, tile), bf16),
            pltpu.SemaphoreType.DMA,
            pltpu.SemaphoreType.DMA((count,)),
        ],
        compiler_params=params(),
        cost_estimate=cost(2 * rows * depth * width, 2 * depth * width + 2 * rows * depth),
    )(group, act, w_down, *own)


def payload_body(query_ref, passage_ref, gain_ref, out_ref, gains):
    own, features = query_ref.shape
    piece = gains.shape[1]
    for row in range(own):
        gains[row : row + 1] = gain_ref[:, row * piece : (row + 1) * piece]
    gain = gains[...]
    high = gain.astype(bf16)
    out_ref[:, :features] = query_ref[...]
    out_ref[:, features : 2 * features] = passage_ref[...]
    out_ref[:, 2 * features : 2 * features + piece] = high
    out_ref[:, 2 * features + piece :] = (gain - high.astype(f32)).astype(bf16)


def payload(query_emb, passage_emb, gain):
    own, features = query_emb.shape
    piece = gain.shape[0] // own
    return pl.pallas_call(
        payload_body,
        out_shape=jax.ShapeDtypeStruct((own, 2 * features + 2 * piece), bf16),
        scratch_shapes=[pltpu.VMEM((own, piece), f32)],
        compiler_params=params(whole_vmem),
        cost_estimate=cost(own * features, 8 * own * features),
    )(query_emb, passage_emb, gain[None])


def group_body(count, blk_ref, *refs):
    parts, refs = refs[:count], refs[count:]
    lse_ref, pos_ref, dest_ref, len_ref = refs[:4]
    query_grad_ref, low_ref, query_all, passage_all, gain_all = refs[4:]
    own, features = query_grad_ref.shape
    pairs = own * count
    piece = features // pairs
    blk = blk_ref[0]
    for k in range(count):
        query_all[k * own : (k + 1) * own] = parts[k][:, :features].astype(f32)
        passage_all[k * own : (k + 1) * own] = parts[k][:, features : 2 * features].astype(f32)
        gains = parts[k][:, 2 * features : 2 * features + piece].astype(f32)
        gains = gains + parts[k][:, 2 * features + piece :].astype(f32)
        for row in range(own):
            first = pl.multiple_of(((blk ^ k) * own + row) * piece, lane)
            gain_all[:, pl.ds(first, piece)] = gains[row : row + 1]
    queries = query_all[...].astype(bf16)
    passages = passage_all[...].astype(bf16)

    def named(dim):
        place = iota((pairs, pairs), dim)
        return (blk ^ (place // own)) * own + place % own

    here_rows, here_cols = named(0), named(1)
    at_rows = here_rows == iota((pairs, pairs), 1)
    at_cols = here_cols == iota((pairs, pairs), 0)
    lse = jnp.sum(jnp.where(at_rows, lse_ref[...], 0.0), axis=1, keepdims=True)
    pos = jnp.sum(jnp.where(at_rows, pos_ref[...], 0), axis=1, keepdims=True)
    hit = (pos == here_cols).astype(f32)
    coef = (jnp.exp(logit_scale * dot_t(queries, passages) - lse) - hit).astype(bf16)
    query_grad_ref[...] = (logit_scale * dot(coef, passages))[:own].astype(bf16)
    same = iota((pairs, pairs), 0) == iota((pairs, pairs), 1)
    lse = jnp.sum(jnp.where(same, lse, 0.0), axis=0, keepdims=True)
    pos = jnp.sum(jnp.where(same, pos, 0), axis=0, keepdims=True)
    hit = (pos == here_rows).astype(f32)
    turned = (jnp.exp(logit_scale * dot_t(passages, queries) - lse) - hit).astype(bf16)
    turned = dot(at_cols.astype(f32).astype(bf16), turned).astype(bf16)
    pass_grad = logit_scale * dot(turned, queries)
    low_ref[:, :features] = (gain_all[...] * pass_grad).astype(bf16)
    row = iota((pairs, lane), 0)
    tokens = dest_ref.shape[1]
    table = jnp.zeros((pairs, lane), f32)
    for n in range(-(-tokens // lane)):
        some = dest_ref[:, n * lane : min(tokens, (n + 1) * lane)].astype(f32)
        table = jnp.where(row == n, widen(some), table)
    table = jnp.where(row == -(-tokens // lane), widen(len_ref[...].astype(f32)), table)
    low_ref[:, features:] = table.astype(bf16)


def widen(row):
    short = lane - row.shape[1]
    return jnp.concatenate([row, jnp.zeros((1, short), f32)], axis=1) if short else row


def group_part(parts, row_lse, positive, token_lengths, destination, features, blk):
    own = parts[0].shape[0]
    pairs = row_lse.shape[0]
    return pl.pallas_call(
        lambda *refs: group_body(pairs // own, *refs),
        in_specs=[pl.BlockSpec(memory_space=pltpu.SMEM)]
        + [pl.BlockSpec(memory_space=pltpu.VMEM)] * (len(parts) + 4),
        out_specs=[pl.BlockSpec(memory_space=pltpu.VMEM)] * 2,
        out_shape=[
            jax.ShapeDtypeStruct((own, features), bf16),
            jax.ShapeDtypeStruct((pairs, features + lane), bf16),
        ],
        scratch_shapes=[
            pltpu.VMEM((pairs, features), f32),
            pltpu.VMEM((pairs, features), f32),
            pltpu.VMEM((1, features), f32),
        ],
        compiler_params=params(),
        cost_estimate=cost(8 * pairs * pairs * features, 8 * pairs * features),
    )(
        blk[None],
        *parts,
        row_lse[None],
        positive[None],
        destination.reshape(1, -1),
        token_lengths,
    )


def earlier_of(tokens):
    return (iota((tokens, tokens), 0) < iota((tokens, tokens), 1)).astype(bf16)


def pack_body(terms, wide_ref, dest_ref, own_ref, *rest):
    outs = rest[terms:]
    groups, slots = len(outs), outs[0].shape[0]
    tokens = dest_ref.shape[1]
    stride = -(-slots // 16) * 16
    hidden = own_ref[...]
    for term in rest[:terms]:
        hidden = hidden + term[...].astype(f32)
    partner = dest_ref[...] ^ wide_ref[0]
    hit = (partner == iota((groups, tokens), 0)).astype(f32)
    rank = dot(hit.astype(bf16), earlier_of(tokens))
    rank = jnp.sum(rank * hit, axis=0, keepdims=True).astype(i32)
    place = iota((groups * stride, tokens), 0) == partner * stride + rank
    packed = dot(place.astype(f32).astype(bf16), hidden.astype(bf16)).astype(bf16)
    for k in range(groups):
        outs[k][...] = packed[k * stride : k * stride + slots]


def pack(wide, destination, own, terms, groups, slots):
    tokens, width = own.shape
    tile = tile_of(width, 512)
    column_spec = pl.BlockSpec((tokens, tile), lambda j, g: (0, j))
    return pl.pallas_call(
        lambda *refs: pack_body(len(terms), *refs),
        grid_spec=pltpu.PrefetchScalarGridSpec(
            num_scalar_prefetch=1,
            grid=(width // tile,),
            in_specs=[pl.BlockSpec((1, tokens), lambda j, g: (0, 0))]
            + [column_spec] * (1 + len(terms)),
            out_specs=[pl.BlockSpec((slots, tile), lambda j, g: (0, j))] * groups,
        ),
        out_shape=[jax.ShapeDtypeStruct((slots, width), bf16)] * groups,
        compiler_params=params(),
        cost_estimate=cost(4 * groups * slots * tokens * width, 10 * tokens * width),
    )(wide[None], destination.reshape(1, tokens), own, *terms)


def assemble_body(wide_ref, *refs):
    parts, out_ref = refs[:-1], refs[-1]
    slots = parts[0].shape[0]
    rows = out_ref.shape[0]
    row, column = iota((rows, slots), 0), iota((rows, slots), 1)
    total = 0.0
    for k, part in enumerate(parts):
        group = wide_ref[0] ^ k
        place = (row == group * slots + column).astype(f32).astype(bf16)
        total = total + dot(place, part[...])
    out_ref[...] = total.astype(bf16)


def assemble(wide, parts):
    slots, width = parts[0].shape
    rows = slots * len(parts)
    return pl.pallas_call(
        assemble_body,
        in_specs=[pl.BlockSpec(memory_space=pltpu.SMEM)]
        + [pl.BlockSpec(memory_space=pltpu.VMEM)] * len(parts),
        out_specs=pl.BlockSpec(memory_space=pltpu.VMEM),
        out_shape=jax.ShapeDtypeStruct((rows, width), bf16),
        compiler_params=params(),
        cost_estimate=cost(2 * rows * rows * width, 4 * rows * width),
    )(wide[None], *parts)


def slots_body(groups, slots, wide_ref, table_ref, hot_ref, share_ref):
    rows, columns = hot_ref.shape
    pairs = columns // groups
    blocks = -(-slots * groups * 2 // 3 // lane)
    table = table_ref[...]

    def tables(n):
        at = iota((groups, columns), 1) == iota((groups, columns), 0) * pairs + n
        return dot(at.astype(f32).astype(bf16), table)

    spread = (iota((rows, groups), 0) // slots == iota((rows, groups), 1)).astype(f32).astype(bf16)
    lengths = tables(blocks)
    upto = (iota((lane, lane), 0) <= iota((lane, lane), 1)).astype(f32).astype(bf16)
    ends = dot(lengths.astype(bf16), upto)
    slot = iota((rows, lane), 0) % slots
    before = jnp.zeros((groups, 1), f32)
    taken = jnp.zeros((rows, 1), f32)
    for n in range(blocks):
        token = iota((groups, lane), 1) + n * lane
        hit = (tables(n).astype(i32) == wide_ref[0]) & (token < slots * groups * 2 // 3)
        count = hit.astype(f32)
        rank = before + dot(count.astype(bf16), earlier_of(lane))
        before = before + jnp.sum(count, axis=1, keepdims=True)
        passage = jnp.ones((groups, lane), f32)
        for pair in range(pairs):
            passage = passage + (token.astype(f32) >= ends[:, pair : pair + 1]).astype(f32)
        code = jnp.where(hit, passage, 0.0)
        rank_rows = dot(spread, rank.astype(bf16)).astype(i32)
        code_rows = dot(spread, code.astype(bf16))
        taken = taken + jnp.sum(
            jnp.where(rank_rows == slot, code_rows, 0.0), axis=1, keepdims=True
        )
    taken = taken.astype(i32)
    column = iota((rows, columns), 1)
    first = iota((rows, columns), 0) // slots * pairs
    hot = (taken > 0) & (column == first + taken - 1)
    hot_ref[...] = hot.astype(f32).astype(bf16)
    length_rows = dot(spread, lengths.astype(bf16))
    length = jnp.where(iota((rows, lane), 1) == taken - 1, length_rows, 0.0)
    length = jnp.sum(length, axis=1, keepdims=True)
    share_ref[...] = jnp.where(taken > 0, 1.0 / jnp.maximum(length, 1.0), 0.0)


def slot_passages(wide, low, features, groups, slots, rows):
    columns = low.shape[0]
    return pl.pallas_call(
        lambda *refs: slots_body(groups, slots, *refs),
        grid=(1,),
        in_specs=[
            pl.BlockSpec(memory_space=pltpu.SMEM),
            pl.BlockSpec((columns, lane), lambda j: (0, features // lane)),
        ],
        out_specs=[
            pl.BlockSpec((rows, columns), lambda j: (0, 0)),
            pl.BlockSpec((rows, 1), lambda j: (0, 0)),
        ],
        out_shape=[
            jax.ShapeDtypeStruct((rows, columns), bf16),
            jax.ShapeDtypeStruct((rows, 1), f32),
        ],
        compiler_params=params(),
        cost_estimate=cost(4 * rows * groups * lane, 2 * rows * columns),
    )(wide[None], low)


def low_act_body(part, low_ref, w_hbm, *refs):
    out_ref, weights, sems = refs[-3:]
    count, tile, _ = weights.shape

    def weight_copy(t):
        rows = pl.ds(pl.multiple_of((part * count + t) * tile, tile), tile)
        return pltpu.make_async_copy(w_hbm.at[rows], weights.at[t], sems.at[t])

    for t in range(count):
        weight_copy(t).start()

    @pl.loop(0, count)
    def _(t):
        weight_copy(t).wait()
        rows = pl.ds(pl.multiple_of(t * tile, tile), tile)
        out_ref[rows] = dot_t(weights[t], low_ref[...]).astype(bf16)


def low_activations(low, features, w_down, part, parts, filled=()):
    pairs = low.shape[0]
    depth = w_down.shape[0]
    some = depth // parts
    tile = tile_of(some, 512)
    count = some // tile
    anywhere = pl.BlockSpec(memory_space=pl.ANY)
    return pl.pallas_call(
        lambda *refs: low_act_body(part, *refs),
        grid=(1,),
        in_specs=[pl.BlockSpec((pairs, features), lambda j: (0, 0)), anywhere]
        + [anywhere] * len(filled),
        out_specs=pl.BlockSpec((some, pairs), lambda j: (part, 0)),
        out_shape=jax.ShapeDtypeStruct((depth, pairs), bf16),
        scratch_shapes=[
            pltpu.VMEM((count, tile, features), bf16),
            pltpu.SemaphoreType.DMA((count,)),
        ],
        input_output_aliases={2: 0} if filled else {},
        compiler_params=params(),
        cost_estimate=cost(2 * pairs * some * features, 2 * some * features),
    )(low, w_down, *filled)


def statistics(hids, lows):
    squares, cross = 0.0, 0.0
    for hid_ref, low_ref in zip(hids, lows):
        hid = hid_ref[...].astype(f32)
        squares = squares + jnp.sum(hid * hid, axis=1, keepdims=True)
        cross = cross + dot_t(hid_ref[...], low_ref[...])
    return squares, cross


def product(hids, weights):
    total = 0.0
    for hid_ref, w_ref in zip(hids, weights):
        total = total + dot_t(hid_ref[...], w_ref[...])
    return total


def weight_specs(count, tile, width):
    return [
        pl.BlockSpec((tile // 2, width), lambda j, g, n=n, side=side: (2 * j + side, g[n]))
        for n in range(count)
        for side in range(2)
    ]


def low_specs(count, pairs, width):
    return [pl.BlockSpec((pairs, width), lambda j, g, n=n: (0, g[n])) for n in range(count)]


def back_body(count, carried, places_ref, *refs):
    hids, weights, refs = refs[:count], refs[count : 3 * count], refs[3 * count :]
    lows, before, (acc_ref, squares_ref, cross_ref) = refs[:count], refs[count:-3], refs[-3:]

    @pl.when(pl.program_id(0) == 0)
    def _():
        squares, cross = statistics(hids, lows)
        if carried:
            squares, cross = before[1][...] + squares, before[2][...] + cross
        squares_ref[...], cross_ref[...] = squares, cross

    half = acc_ref.shape[1] // 2
    for side in range(2):
        at = slice(side * half, (side + 1) * half)
        total = product(hids, weights[side::2])
        if carried:
            total = total + before[0][:, at].astype(f32)
        acc_ref[:, at] = total.astype(bf16)


def carried_specs(rows, pairs, tile):
    return [
        pl.BlockSpec((rows, tile), lambda j, g: (0, j)),
        pl.BlockSpec((rows, 1), lambda j, g: (0, 0)),
        pl.BlockSpec((rows, pairs), lambda j, g: (0, 0)),
    ]


def back(places, pieces, w_down, low, before=()):
    count = len(pieces)
    rows, width = pieces[0].shape
    depth = w_down.shape[0]
    pairs = low.shape[0]
    tile = tile_of(depth, 512)
    totals = carried_specs(rows, pairs, tile)
    return pl.pallas_call(
        lambda *refs: back_body(count, len(before), *refs),
        grid_spec=pltpu.PrefetchScalarGridSpec(
            num_scalar_prefetch=1,
            grid=(depth // tile,),
            in_specs=[pl.BlockSpec((rows, width), lambda j, g: (0, 0))] * count
            + weight_specs(count, tile, width)
            + low_specs(count, pairs, width)
            + totals[: len(before)],
            out_specs=totals,
        ),
        out_shape=[
            jax.ShapeDtypeStruct((rows, depth), bf16),
            jax.ShapeDtypeStruct((rows, 1), f32),
            jax.ShapeDtypeStruct((rows, pairs), f32),
        ],
        compiler_params=params(),
        cost_estimate=cost(2 * rows * depth * width * count, 2 * depth * width * count),
    )(places, *pieces, *[w_down] * 2 * count, *[low] * count, *before)


def finish_body(features, count, places_ref, *refs):
    hids, weights, refs = refs[:count], refs[count : count + 2], refs[count + 2 :]
    low_ref, acc_ref, squares_ref, cross_ref, hot_ref, share_ref, low_act_ref = refs[:7]
    own_ref, own_low_ref, gain_ref, act_out, resid_out, normed_out = refs[7:13]
    hid, lead, pull, scale = refs[13:]
    part = hids[0].shape[0]
    step = own_ref.shape[0]

    @pl.when(pl.program_id(0) == 0)
    def _():
        for n in range(count):
            hid[n * part : (n + 1) * part] = hids[n][...]
        squares, cross = statistics([hid], [low_ref])
        hot = hot_ref[...].astype(f32)
        inner = jnp.sum((cross_ref[...] + cross) * hot, axis=1, keepdims=True) * share_ref[...]
        inv_rms = lax.rsqrt((squares_ref[...] + squares) / features + norm_eps)
        scale[...] = inv_rms
        lead[...] = inv_rms * share_ref[...]
        pull[...] = inv_rms * inv_rms * inv_rms * inner / features

    half = act_out.shape[1] // 2
    for side in range(2):
        at = slice(side * half, (side + 1) * half)
        low_act = dot_t(hot_ref[...], low_act_ref[at])
        hid_act = acc_ref[:, at].astype(f32) + product([hid], weights[side : side + 1])
        act_out[:, at] = (lead[...] * low_act - pull[...] * hid_act).astype(bf16)
    rows = pl.ds(pl.multiple_of(pl.program_id(0) * step, step), step)
    own = own_ref[...].astype(f32)
    own_low = dot(hot_ref[rows], own_low_ref[...])
    resid_out[...] = (lead[rows] * own_low - own * pull[rows]).astype(bf16)
    normed_out[...] = (gain_ref[...] * own * scale[rows]).astype(bf16)


def finish(places, pieces, w_down, low, before, hot, share, low_act, own, gain):
    count = len(pieces)
    rows, width = own.shape
    depth, features = w_down.shape
    pairs = hot.shape[1]
    tile = tile_of(depth, 512)
    steps = depth // tile
    step = rows // steps

    def whole(shape):
        return pl.BlockSpec(shape, lambda j, g: (0, 0))

    row_spec = pl.BlockSpec((step, width), lambda j, g: (j, 0))
    return pl.pallas_call(
        lambda *refs: finish_body(features, count, *refs),
        grid_spec=pltpu.PrefetchScalarGridSpec(
            num_scalar_prefetch=1,
            grid=(steps,),
            in_specs=[whole((rows // count, width))] * count
            + weight_specs(1, tile, width)
            + low_specs(1, pairs, width)
            + carried_specs(rows, pairs, tile)
            + [
                whole((rows, pairs)),
                whole((rows, 1)),
                pl.BlockSpec((tile, pairs), lambda j, g: (j, 0)),
                row_spec,
                pl.BlockSpec((pairs, width), lambda j, g: (0, g[1])),
                whole((1, width)),
            ],
            out_specs=[pl.BlockSpec((rows, tile), lambda j, g: (0, j)), row_spec, row_spec],
            scratch_shapes=[pltpu.VMEM((rows, width), bf16)] + [pltpu.VMEM((rows, 1), f32)] * 3,
        ),
        out_shape=[
            jax.ShapeDtypeStruct((rows, depth), bf16),
            jax.ShapeDtypeStruct((rows, width), bf16),
            jax.ShapeDtypeStruct((rows, width), bf16),
        ],
        compiler_params=params(),
        cost_estimate=cost(2 * rows * depth * width, 2 * depth * width + 6 * rows * depth),
    )(
        places,
        *pieces,
        *[w_down] * 2,
        low,
        *before,
        hot,
        share,
        low_act,
        own,
        low,
        gain,
    )


def low_rank_shards(
    query_emb,
    passage_emb,
    row_lse,
    positive,
    token_lengths,
    destination,
    mlp_act,
    resid,
    w_down,
    gain,
):
    wide_count = lax.axis_size("wide")
    blk, wide = lax.axis_index("blk"), lax.axis_index("wide")
    tok_count, width = resid.shape
    features = w_down.shape[1]
    pairs = row_lse.shape[0]
    slot_count = 3 * tok_count // (2 * wide_count)
    rows = wide_count * slot_count

    both = payload(query_emb, passage_emb, gain)
    parts = [both] + [swap(both, k) for k in (1, 2, 3)]
    first_term = project((blk ^ 3)[None], mlp_act, w_down, width)
    arrived = [swap(first_term, 3)]
    parts = after(first_term, *parts)[1:]
    query_grad, low_own = group_part(
        parts, row_lse, positive, token_lengths, destination, features, blk
    )
    mlp_act = after(low_own, mlp_act)[1]
    for k in (1, 2):
        arrived.append(swap(project((blk ^ k)[None], mlp_act, w_down, width), k))
    own_term = project(blk[None], mlp_act, w_down, width, resid)

    low = lax.all_gather(low_own, "wide", axis=0, tiled=True)
    packed = pack(wide, destination, own_term, arrived, wide_count, slot_count)
    routed = [packed[k] if k == 0 else swap(packed[k], k, "wide") for k in range(wide_count)]
    low_act = low_activations(low, features, w_down, 0, 2)
    hot, share = slot_passages(wide, low, features, wide_count, slot_count, rows)
    low_act, hot, share, *routed = lax.optimization_barrier((low_act, hot, share, *routed))
    own = assemble(wide, routed)

    beside, above = swap(own, 1), swap(own, 2)
    totals = back(blk[None], [own], w_down, low)
    low_act = low_activations(low, features, w_down, 1, 2, [low_act])
    low_act, *totals, beside, above = lax.optimization_barrier((low_act, *totals, beside, above))
    top = swap(beside[: rows // 2], 2)
    bottom = swap(above[rows // 2 :], 1)
    totals = back(jnp.stack([blk ^ 1, blk ^ 2]), [beside, above], w_down, low, totals)
    act_grad, resid_grad, normed_out = finish(
        jnp.stack([blk ^ 3, blk]),
        [top, bottom],
        w_down,
        low,
        totals,
        hot,
        share,
        low_act,
        own,
        gain[None],
    )
    return (query_grad, resid_grad, act_grad, normed_out)


def coefficients(scores, lse_part, pos_part):
    columns = lax.broadcasted_iota(jnp.int32, scores.shape, 1)
    target = (pos_part[:, None] == columns).astype(jnp.float32)
    return (jnp.exp(scores - lse_part[:, None]) - target).astype(jnp.bfloat16)


def place_rows(destination, wide_count, slot_count):
    tok_count = destination.shape[0]
    dest_hot = (destination == lax.broadcasted_iota(jnp.int32, (tok_count, wide_count), 1)).astype(
        bf16
    )
    token = lax.iota(jnp.int32, tok_count)
    earlier = (token[None, :] < token[:, None]).astype(bf16)
    rank_of = jnp.dot(earlier, dest_hot, preferred_element_type=f32)
    slot_of = jnp.sum(rank_of * dest_hot.astype(f32), axis=1).astype(jnp.int32)
    slot_of = slot_of + destination[:, 0] * slot_count
    return (
        lax.broadcasted_iota(jnp.int32, (wide_count * slot_count, tok_count), 0) == slot_of[None, :]
    ).astype(bf16)


def row_shards(
    query_emb,
    passage_emb,
    row_lse,
    positive,
    token_lengths,
    destination,
    mlp_act,
    resid,
    w_down,
    gain,
):
    pair_rows = query_emb.shape[0]
    tok_count, feat_width = resid.shape
    features = w_down.shape[1]
    blk_index = lax.axis_index("blk")
    wide_count = lax.axis_size("wide")
    slot_count = 3 * tok_count // (2 * wide_count)
    offset = blk_index * feat_width
    query_all = lax.all_gather(query_emb, "blk", axis=0, tiled=True)
    passage_all = lax.all_gather(passage_emb, "blk", axis=0, tiled=True)
    scores = logit_scale * jnp.dot(query_all, passage_all.T, preferred_element_type=f32)
    coef_full = coefficients(scores, row_lse, positive)
    own_coef = lax.dynamic_slice_in_dim(coef_full, blk_index * pair_rows, pair_rows, 0)
    query_grad = (
        logit_scale * jnp.dot(own_coef, passage_all, preferred_element_type=f32)
    ).astype(bf16)
    query_cols = lax.dynamic_slice_in_dim(query_all, offset, feat_width, 1)
    grad_cols = logit_scale * lax.dot_general(
        query_cols, coef_full, (((0,), (0,)), ((), ())), preferred_element_type=f32
    )
    lengths_row = token_lengths[0]
    starts = jnp.cumsum(lengths_row) - lengths_row
    positions = lax.broadcasted_iota(jnp.int32, (tok_count, lengths_row.shape[0]), 0)
    member = (positions >= starts[None, :]) & (positions < (starts + lengths_row)[None, :])
    weights = member.astype(f32) * (1.0 / lengths_row.astype(f32))[None, :]
    tok_grad = lax.dot_general(
        weights,
        grad_cols,
        (((1,), (1,)), ((), ())),
        precision=lax.Precision.HIGHEST,
        preferred_element_type=f32,
    ).astype(bf16)
    terms = jnp.dot(mlp_act, w_down, preferred_element_type=f32)
    own = lax.dynamic_slice_in_dim(terms, offset, feat_width, 1) + resid.astype(f32)
    terms = lax.dynamic_update_slice_in_dim(terms, own, offset, 1)
    hidden = lax.psum_scatter(terms.astype(bf16), "blk", scatter_dimension=1, tiled=True)
    placer = place_rows(destination, wide_count, slot_count)
    payload = jnp.concatenate([hidden, tok_grad], axis=1)
    packed = jnp.dot(placer, payload, preferred_element_type=f32).astype(bf16)
    packed = packed.reshape(wide_count, slot_count, 2 * feat_width)
    rows = lax.all_to_all(packed, "wide", split_axis=0, concat_axis=0, tiled=True).reshape(
        wide_count * slot_count, 2 * feat_width
    )
    hidden = rows[:, :feat_width].astype(f32)
    gained = gain[None, :] * rows[:, feat_width:].astype(f32)
    squares, inner_sum = lax.psum(
        (jnp.sum(hidden * hidden, axis=1), jnp.sum(gained * hidden, axis=1)), "blk"
    )
    inv_rms = lax.rsqrt(squares / features + norm_eps)[:, None]
    normed = (gain[None, :] * hidden * inv_rms).astype(bf16)
    resid_back = (
        inv_rms * gained - hidden * (inv_rms * inv_rms * inv_rms) * inner_sum[:, None] / features
    ).astype(bf16)
    act_back = dot_t(lax.all_gather(resid_back, "blk", axis=1, tiled=True), w_down)
    return (query_grad, resid_back, act_back.astype(bf16), normed)


def solution(mesh):
    blk_count, wide_count = mesh.shape["blk"], mesh.shape["wide"]

    def shards(*operands):
        pairs, tok_count = operands[2].shape[0], operands[7].shape[0]
        low_rank = 2 * wide_count * pairs <= 3 * tok_count
        per_pair = tok_count // pairs
        aligned = operands[9].shape[0] % (lane * operands[0].shape[0]) == 0 and wide_count <= lane
        if low_rank and blk_count == 4 and aligned and per_pair * pairs == tok_count and wide_count & (wide_count - 1) == 0:
            return low_rank_shards(*operands)
        return row_shards(*operands)

    return jax.shard_map(
        shards,
        mesh=mesh,
        in_specs=(
            P(("wide", "blk"), None),
            P(("wide", "blk"), None),
            P("wide"),
            P("wide"),
            P("wide", None),
            P("wide", None),
            P("wide", "blk"),
            P("wide", "blk"),
            P("blk", None),
            P("blk"),
        ),
        out_specs=(P(("wide", "blk"), None), P("wide", "blk"), P("wide", "blk"), P("wide", "blk")),
        check_vma=False,
    )
```

```python
import jax
import jax.numpy as jnp
from jax import lax
from jax.experimental import pallas as pl
from jax.experimental.pallas import tpu as pltpu
from jax.sharding import PartitionSpec as P

logit_scale = 24.0
norm_eps = 1e-06
f32 = jnp.float32
bf16 = jnp.bfloat16
i32 = jnp.int32
lane = 128
kernel_vmem = 46 * 1024 * 1024
whole_vmem = 60 * 1024 * 1024


def params(vmem=kernel_vmem):
    return pltpu.CompilerParams(vmem_limit_bytes=vmem)


def cost(flops, nbytes):
    return pl.CostEstimate(flops=flops, bytes_accessed=nbytes, transcendentals=0)


def tile_of(extent, most):
    tile = most
    while extent % tile:
        tile //= 2
    return tile


def iota(shape, dim):
    return lax.broadcasted_iota(i32, shape, dim)


def dot(left, right):
    return jnp.dot(left, right, preferred_element_type=f32)


def dot_t(left, right):
    return lax.dot_general(left, right, (((1,), (1,)), ((), ())), preferred_element_type=f32)


def swap(rows, k, axis="blk"):
    return lax.ppermute(rows, axis, [(i, i ^ k) for i in range(lax.axis_size(axis))])


def after(first, *later):
    return lax.optimization_barrier((first, *later))


def project_body(has_resid, group_ref, act_hbm, w_hbm, *refs):
    out_ref, act, weights, act_sem, sems = refs[has_resid:]
    width = out_ref.shape[1]
    count, _, tile = weights.shape
    first = group_ref[0] * width

    def weight_copy(i):
        columns = pl.ds(pl.multiple_of(first + i * tile, lane), tile)
        return pltpu.make_async_copy(w_hbm.at[:, columns], weights.at[i], sems.at[i])

    act_copy = pltpu.make_async_copy(act_hbm, act, act_sem)
    act_copy.start()
    for i in range(count):
        weight_copy(i).start()
    act_copy.wait()

    @pl.loop(0, count)
    def _(i):
        weight_copy(i).wait()
        columns = pl.ds(pl.multiple_of(i * tile, lane), tile)
        term = dot(act[...], weights[i])
        if has_resid:
            term = term + refs[0][:, columns].astype(f32)
        out_ref[:, columns] = term.astype(out_ref.dtype)


def project(group, act, w_down, width, resid=None):
    rows, depth = act.shape
    tile = tile_of(width, 256)
    count = width // tile
    own = [] if resid is None else [resid]
    return pl.pallas_call(
        lambda *refs: project_body(len(own), *refs),
        in_specs=[pl.BlockSpec(memory_space=pltpu.SMEM)]
        + [pl.BlockSpec(memory_space=pl.ANY)] * 2
        + [pl.BlockSpec(memory_space=pltpu.VMEM)] * len(own),
        out_specs=pl.BlockSpec(memory_space=pltpu.VMEM),
        out_shape=jax.ShapeDtypeStruct((rows, width), f32 if own else bf16),
        scratch_shapes=[
            pltpu.VMEM((rows, depth), bf16),
            pltpu.VMEM((count, depth, tile), bf16),
            pltpu.SemaphoreType.DMA,
            pltpu.SemaphoreType.DMA((count,)),
        ],
        compiler_params=params(),
        cost_estimate=cost(2 * rows * depth * width, 2 * depth * width + 2 * rows * depth),
    )(group, act, w_down, *own)


def payload_body(query_ref, passage_ref, gain_ref, out_ref, gains):
    own, features = query_ref.shape
    piece = gains.shape[1]
    for row in range(own):
        gains[row : row + 1] = gain_ref[:, row * piece : (row + 1) * piece]
    gain = gains[...]
    high = gain.astype(bf16)
    out_ref[:, :features] = query_ref[...]
    out_ref[:, features : 2 * features] = passage_ref[...]
    out_ref[:, 2 * features : 2 * features + piece] = high
    out_ref[:, 2 * features + piece :] = (gain - high.astype(f32)).astype(bf16)


def payload(query_emb, passage_emb, gain):
    own, features = query_emb.shape
    piece = gain.shape[0] // own
    return pl.pallas_call(
        payload_body,
        out_shape=jax.ShapeDtypeStruct((own, 2 * features + 2 * piece), bf16),
        scratch_shapes=[pltpu.VMEM((own, piece), f32)],
        compiler_params=params(whole_vmem),
        cost_estimate=cost(own * features, 8 * own * features),
    )(query_emb, passage_emb, gain[None])


def group_body(count, blk_ref, *refs):
    parts, refs = refs[:count], refs[count:]
    lse_ref, pos_ref, dest_ref, len_ref = refs[:4]
    query_grad_ref, low_ref, query_all, passage_all, gain_all = refs[4:]
    own, features = query_grad_ref.shape
    pairs = own * count
    piece = features // pairs
    blk = blk_ref[0]
    for k in range(count):
        query_all[k * own : (k + 1) * own] = parts[k][:, :features].astype(f32)
        passage_all[k * own : (k + 1) * own] = parts[k][:, features : 2 * features].astype(f32)
        gains = parts[k][:, 2 * features : 2 * features + piece].astype(f32)
        gains = gains + parts[k][:, 2 * features + piece :].astype(f32)
        for row in range(own):
            first = pl.multiple_of(((blk ^ k) * own + row) * piece, lane)
            gain_all[:, pl.ds(first, piece)] = gains[row : row + 1]
    queries = query_all[...].astype(bf16)
    passages = passage_all[...].astype(bf16)

    def named(dim):
        place = iota((pairs, pairs), dim)
        return (blk ^ (place // own)) * own + place % own

    here_rows, here_cols = named(0), named(1)
    at_rows = here_rows == iota((pairs, pairs), 1)
    at_cols = here_cols == iota((pairs, pairs), 0)
    lse = jnp.sum(jnp.where(at_rows, lse_ref[...], 0.0), axis=1, keepdims=True)
    pos = jnp.sum(jnp.where(at_rows, pos_ref[...], 0), axis=1, keepdims=True)
    hit = (pos == here_cols).astype(f32)
    coef = (jnp.exp(logit_scale * dot_t(queries, passages) - lse) - hit).astype(bf16)
    query_grad_ref[...] = (logit_scale * dot(coef, passages))[:own].astype(bf16)
    same = iota((pairs, pairs), 0) == iota((pairs, pairs), 1)
    lse = jnp.sum(jnp.where(same, lse, 0.0), axis=0, keepdims=True)
    pos = jnp.sum(jnp.where(same, pos, 0), axis=0, keepdims=True)
    hit = (pos == here_rows).astype(f32)
    turned = (jnp.exp(logit_scale * dot_t(passages, queries) - lse) - hit).astype(bf16)
    turned = dot(at_cols.astype(f32).astype(bf16), turned).astype(bf16)
    pass_grad = logit_scale * dot(turned, queries)
    low_ref[:, :features] = (gain_all[...] * pass_grad).astype(bf16)
    row = iota((pairs, lane), 0)
    tokens = dest_ref.shape[1]
    table = jnp.zeros((pairs, lane), f32)
    for n in range(-(-tokens // lane)):
        some = dest_ref[:, n * lane : min(tokens, (n + 1) * lane)].astype(f32)
        table = jnp.where(row == n, widen(some), table)
    table = jnp.where(row == -(-tokens // lane), widen(len_ref[...].astype(f32)), table)
    low_ref[:, features:] = table.astype(bf16)


def widen(row):
    short = lane - row.shape[1]
    return jnp.concatenate([row, jnp.zeros((1, short), f32)], axis=1) if short else row


def group_part(parts, row_lse, positive, token_lengths, destination, features, blk):
    own = parts[0].shape[0]
    pairs = row_lse.shape[0]
    return pl.pallas_call(
        lambda *refs: group_body(pairs // own, *refs),
        in_specs=[pl.BlockSpec(memory_space=pltpu.SMEM)]
        + [pl.BlockSpec(memory_space=pltpu.VMEM)] * (len(parts) + 4),
        out_specs=[pl.BlockSpec(memory_space=pltpu.VMEM)] * 2,
        out_shape=[
            jax.ShapeDtypeStruct((own, features), bf16),
            jax.ShapeDtypeStruct((pairs, features + lane), bf16),
        ],
        scratch_shapes=[
            pltpu.VMEM((pairs, features), f32),
            pltpu.VMEM((pairs, features), f32),
            pltpu.VMEM((1, features), f32),
        ],
        compiler_params=params(),
        cost_estimate=cost(8 * pairs * pairs * features, 8 * pairs * features),
    )(
        blk[None],
        *parts,
        row_lse[None],
        positive[None],
        destination.reshape(1, -1),
        token_lengths,
    )


def earlier_of(tokens):
    return (iota((tokens, tokens), 0) < iota((tokens, tokens), 1)).astype(bf16)


def pack_body(terms, wide_ref, dest_ref, own_ref, *rest):
    outs = rest[terms:]
    groups, slots = len(outs), outs[0].shape[0]
    tokens = dest_ref.shape[1]
    stride = -(-slots // 16) * 16
    hidden = own_ref[...]
    for term in rest[:terms]:
        hidden = hidden + term[...].astype(f32)
    partner = dest_ref[...] ^ wide_ref[0]
    hit = (partner == iota((groups, tokens), 0)).astype(f32)
    rank = dot(hit.astype(bf16), earlier_of(tokens))
    rank = jnp.sum(rank * hit, axis=0, keepdims=True).astype(i32)
    place = iota((groups * stride, tokens), 0) == partner * stride + rank
    packed = dot(place.astype(f32).astype(bf16), hidden.astype(bf16)).astype(bf16)
    for k in range(groups):
        outs[k][...] = packed[k * stride : k * stride + slots]


def pack(wide, destination, own, terms, groups, slots):
    tokens, width = own.shape
    tile = tile_of(width, 512)
    column_spec = pl.BlockSpec((tokens, tile), lambda j, g: (0, j))
    return pl.pallas_call(
        lambda *refs: pack_body(len(terms), *refs),
        grid_spec=pltpu.PrefetchScalarGridSpec(
            num_scalar_prefetch=1,
            grid=(width // tile,),
            in_specs=[pl.BlockSpec((1, tokens), lambda j, g: (0, 0))]
            + [column_spec] * (1 + len(terms)),
            out_specs=[pl.BlockSpec((slots, tile), lambda j, g: (0, j))] * groups,
        ),
        out_shape=[jax.ShapeDtypeStruct((slots, width), bf16)] * groups,
        compiler_params=params(),
        cost_estimate=cost(4 * groups * slots * tokens * width, 10 * tokens * width),
    )(wide[None], destination.reshape(1, tokens), own, *terms)


def assemble_body(wide_ref, *refs):
    parts, out_ref = refs[:-1], refs[-1]
    slots = parts[0].shape[0]
    rows = out_ref.shape[0]
    row, column = iota((rows, slots), 0), iota((rows, slots), 1)
    total = 0.0
    for k, part in enumerate(parts):
        group = wide_ref[0] ^ k
        place = (row == group * slots + column).astype(f32).astype(bf16)
        total = total + dot(place, part[...])
    out_ref[...] = total.astype(bf16)


def assemble(wide, parts):
    slots, width = parts[0].shape
    rows = slots * len(parts)
    return pl.pallas_call(
        assemble_body,
        in_specs=[pl.BlockSpec(memory_space=pltpu.SMEM)]
        + [pl.BlockSpec(memory_space=pltpu.VMEM)] * len(parts),
        out_specs=pl.BlockSpec(memory_space=pltpu.VMEM),
        out_shape=jax.ShapeDtypeStruct((rows, width), bf16),
        compiler_params=params(),
        cost_estimate=cost(2 * rows * rows * width, 4 * rows * width),
    )(wide[None], *parts)


def slots_body(groups, slots, wide_ref, table_ref, hot_ref, share_ref):
    rows, columns = hot_ref.shape
    pairs = columns // groups
    blocks = -(-slots * groups * 2 // 3 // lane)
    table = table_ref[...]

    def tables(n):
        at = iota((groups, columns), 1) == iota((groups, columns), 0) * pairs + n
        return dot(at.astype(f32).astype(bf16), table)

    spread = (iota((rows, groups), 0) // slots == iota((rows, groups), 1)).astype(f32).astype(bf16)
    lengths = tables(blocks)
    upto = (iota((lane, lane), 0) <= iota((lane, lane), 1)).astype(f32).astype(bf16)
    ends = dot(lengths.astype(bf16), upto)
    slot = iota((rows, lane), 0) % slots
    before = jnp.zeros((groups, 1), f32)
    taken = jnp.zeros((rows, 1), f32)
    for n in range(blocks):
        token = iota((groups, lane), 1) + n * lane
        hit = (tables(n).astype(i32) == wide_ref[0]) & (token < slots * groups * 2 // 3)
        count = hit.astype(f32)
        rank = before + dot(count.astype(bf16), earlier_of(lane))
        before = before + jnp.sum(count, axis=1, keepdims=True)
        passage = jnp.ones((groups, lane), f32)
        for pair in range(pairs):
            passage = passage + (token.astype(f32) >= ends[:, pair : pair + 1]).astype(f32)
        code = jnp.where(hit, passage, 0.0)
        rank_rows = dot(spread, rank.astype(bf16)).astype(i32)
        code_rows = dot(spread, code.astype(bf16))
        taken = taken + jnp.sum(
            jnp.where(rank_rows == slot, code_rows, 0.0), axis=1, keepdims=True
        )
    taken = taken.astype(i32)
    column = iota((rows, columns), 1)
    first = iota((rows, columns), 0) // slots * pairs
    hot = (taken > 0) & (column == first + taken - 1)
    hot_ref[...] = hot.astype(f32).astype(bf16)
    length_rows = dot(spread, lengths.astype(bf16))
    length = jnp.where(iota((rows, lane), 1) == taken - 1, length_rows, 0.0)
    length = jnp.sum(length, axis=1, keepdims=True)
    share_ref[...] = jnp.where(taken > 0, 1.0 / jnp.maximum(length, 1.0), 0.0)


def slot_passages(wide, low, features, groups, slots, rows):
    columns = low.shape[0]
    return pl.pallas_call(
        lambda *refs: slots_body(groups, slots, *refs),
        grid=(1,),
        in_specs=[
            pl.BlockSpec(memory_space=pltpu.SMEM),
            pl.BlockSpec((columns, lane), lambda j: (0, features // lane)),
        ],
        out_specs=[
            pl.BlockSpec((rows, columns), lambda j: (0, 0)),
            pl.BlockSpec((rows, 1), lambda j: (0, 0)),
        ],
        out_shape=[
            jax.ShapeDtypeStruct((rows, columns), bf16),
            jax.ShapeDtypeStruct((rows, 1), f32),
        ],
        compiler_params=params(),
        cost_estimate=cost(4 * rows * groups * lane, 2 * rows * columns),
    )(wide[None], low)


def low_act_body(part, low_ref, w_hbm, *refs):
    out_ref, weights, sems = refs[-3:]
    count, tile, _ = weights.shape

    def weight_copy(t):
        rows = pl.ds(pl.multiple_of((part * count + t) * tile, tile), tile)
        return pltpu.make_async_copy(w_hbm.at[rows], weights.at[t], sems.at[t])

    for t in range(count):
        weight_copy(t).start()

    @pl.loop(0, count)
    def _(t):
        weight_copy(t).wait()
        rows = pl.ds(pl.multiple_of(t * tile, tile), tile)
        out_ref[rows] = dot_t(weights[t], low_ref[...]).astype(bf16)


def low_activations(low, features, w_down, part, parts, filled=()):
    pairs = low.shape[0]
    depth = w_down.shape[0]
    some = depth // parts
    tile = tile_of(some, 512)
    count = some // tile
    anywhere = pl.BlockSpec(memory_space=pl.ANY)
    return pl.pallas_call(
        lambda *refs: low_act_body(part, *refs),
        grid=(1,),
        in_specs=[pl.BlockSpec((pairs, features), lambda j: (0, 0)), anywhere]
        + [anywhere] * len(filled),
        out_specs=pl.BlockSpec((some, pairs), lambda j: (part, 0)),
        out_shape=jax.ShapeDtypeStruct((depth, pairs), bf16),
        scratch_shapes=[
            pltpu.VMEM((count, tile, features), bf16),
            pltpu.SemaphoreType.DMA((count,)),
        ],
        input_output_aliases={2: 0} if filled else {},
        compiler_params=params(),
        cost_estimate=cost(2 * pairs * some * features, 2 * some * features),
    )(low, w_down, *filled)


def statistics(hids, lows):
    squares, cross = 0.0, 0.0
    for hid_ref, low_ref in zip(hids, lows):
        hid = hid_ref[...].astype(f32)
        squares = squares + jnp.sum(hid * hid, axis=1, keepdims=True)
        cross = cross + dot_t(hid_ref[...], low_ref[...])
    return squares, cross


def product(hids, weights):
    total = 0.0
    for hid_ref, w_ref in zip(hids, weights):
        total = total + dot_t(hid_ref[...], w_ref[...])
    return total


def weight_specs(count, tile, width):
    return [
        pl.BlockSpec((tile // 2, width), lambda j, g, n=n, side=side: (2 * j + side, g[n]))
        for n in range(count)
        for side in range(2)
    ]


def low_specs(count, pairs, width):
    return [pl.BlockSpec((pairs, width), lambda j, g, n=n: (0, g[n])) for n in range(count)]


def back_body(count, carried, places_ref, *refs):
    hids, weights, refs = refs[:count], refs[count : 3 * count], refs[3 * count :]
    lows, before, (acc_ref, squares_ref, cross_ref) = refs[:count], refs[count:-3], refs[-3:]

    @pl.when(pl.program_id(0) == 0)
    def _():
        squares, cross = statistics(hids, lows)
        if carried:
            squares, cross = before[1][...] + squares, before[2][...] + cross
        squares_ref[...], cross_ref[...] = squares, cross

    half = acc_ref.shape[1] // 2
    for side in range(2):
        at = slice(side * half, (side + 1) * half)
        total = product(hids, weights[side::2])
        if carried:
            total = total + before[0][:, at].astype(f32)
        acc_ref[:, at] = total.astype(bf16)


def carried_specs(rows, pairs, tile):
    return [
        pl.BlockSpec((rows, tile), lambda j, g: (0, j)),
        pl.BlockSpec((rows, 1), lambda j, g: (0, 0)),
        pl.BlockSpec((rows, pairs), lambda j, g: (0, 0)),
    ]


def back(places, pieces, w_down, low, before=()):
    count = len(pieces)
    rows, width = pieces[0].shape
    depth = w_down.shape[0]
    pairs = low.shape[0]
    tile = tile_of(depth, 512)
    totals = carried_specs(rows, pairs, tile)
    return pl.pallas_call(
        lambda *refs: back_body(count, len(before), *refs),
        grid_spec=pltpu.PrefetchScalarGridSpec(
            num_scalar_prefetch=1,
            grid=(depth // tile,),
            in_specs=[pl.BlockSpec((rows, width), lambda j, g: (0, 0))] * count
            + weight_specs(count, tile, width)
            + low_specs(count, pairs, width)
            + totals[: len(before)],
            out_specs=totals,
        ),
        out_shape=[
            jax.ShapeDtypeStruct((rows, depth), bf16),
            jax.ShapeDtypeStruct((rows, 1), f32),
            jax.ShapeDtypeStruct((rows, pairs), f32),
        ],
        compiler_params=params(),
        cost_estimate=cost(2 * rows * depth * width * count, 2 * depth * width * count),
    )(places, *pieces, *[w_down] * 2 * count, *[low] * count, *before)


def finish_body(features, count, places_ref, *refs):
    hids, weights, refs = refs[:count], refs[count : count + 2], refs[count + 2 :]
    low_ref, acc_ref, squares_ref, cross_ref, hot_ref, share_ref, low_act_ref = refs[:7]
    own_ref, own_low_ref, gain_ref, act_out, resid_out, normed_out = refs[7:13]
    hid, lead, pull, scale = refs[13:]
    part = hids[0].shape[0]
    step = own_ref.shape[0]

    @pl.when(pl.program_id(0) == 0)
    def _():
        for n in range(count):
            hid[n * part : (n + 1) * part] = hids[n][...]
        squares, cross = statistics([hid], [low_ref])
        hot = hot_ref[...].astype(f32)
        inner = jnp.sum((cross_ref[...] + cross) * hot, axis=1, keepdims=True) * share_ref[...]
        inv_rms = lax.rsqrt((squares_ref[...] + squares) / features + norm_eps)
        scale[...] = inv_rms
        lead[...] = inv_rms * share_ref[...]
        pull[...] = inv_rms * inv_rms * inv_rms * inner / features

    half = act_out.shape[1] // 2
    for side in range(2):
        at = slice(side * half, (side + 1) * half)
        low_act = dot_t(hot_ref[...], low_act_ref[at])
        hid_act = acc_ref[:, at].astype(f32) + product([hid], weights[side : side + 1])
        act_out[:, at] = (lead[...] * low_act - pull[...] * hid_act).astype(bf16)
    rows = pl.ds(pl.multiple_of(pl.program_id(0) * step, step), step)
    own = own_ref[...].astype(f32)
    own_low = dot(hot_ref[rows], own_low_ref[...])
    resid_out[...] = (lead[rows] * own_low - own * pull[rows]).astype(bf16)
    normed_out[...] = (gain_ref[...] * own * scale[rows]).astype(bf16)


def finish(places, pieces, w_down, low, before, hot, share, low_act, own, gain):
    count = len(pieces)
    rows, width = own.shape
    depth, features = w_down.shape
    pairs = hot.shape[1]
    tile = tile_of(depth, 1024)
    steps = depth // tile
    step = rows // steps

    def whole(shape):
        return pl.BlockSpec(shape, lambda j, g: (0, 0))

    row_spec = pl.BlockSpec((step, width), lambda j, g: (j, 0))
    return pl.pallas_call(
        lambda *refs: finish_body(features, count, *refs),
        grid_spec=pltpu.PrefetchScalarGridSpec(
            num_scalar_prefetch=1,
            grid=(steps,),
            in_specs=[whole((rows // count, width))] * count
            + weight_specs(1, tile, width)
            + low_specs(1, pairs, width)
            + carried_specs(rows, pairs, tile)
            + [
                whole((rows, pairs)),
                whole((rows, 1)),
                pl.BlockSpec((tile, pairs), lambda j, g: (j, 0)),
                row_spec,
                pl.BlockSpec((pairs, width), lambda j, g: (0, g[1])),
                whole((1, width)),
            ],
            out_specs=[pl.BlockSpec((rows, tile), lambda j, g: (0, j)), row_spec, row_spec],
            scratch_shapes=[pltpu.VMEM((rows, width), bf16)] + [pltpu.VMEM((rows, 1), f32)] * 3,
        ),
        out_shape=[
            jax.ShapeDtypeStruct((rows, depth), bf16),
            jax.ShapeDtypeStruct((rows, width), bf16),
            jax.ShapeDtypeStruct((rows, width), bf16),
        ],
        compiler_params=params(),
        cost_estimate=cost(2 * rows * depth * width, 2 * depth * width + 6 * rows * depth),
    )(
        places,
        *pieces,
        *[w_down] * 2,
        low,
        *before,
        hot,
        share,
        low_act,
        own,
        low,
        gain,
    )


def low_rank_shards(
    query_emb,
    passage_emb,
    row_lse,
    positive,
    token_lengths,
    destination,
    mlp_act,
    resid,
    w_down,
    gain,
):
    wide_count = lax.axis_size("wide")
    blk, wide = lax.axis_index("blk"), lax.axis_index("wide")
    tok_count, width = resid.shape
    features = w_down.shape[1]
    pairs = row_lse.shape[0]
    slot_count = 3 * tok_count // (2 * wide_count)
    rows = wide_count * slot_count

    both = payload(query_emb, passage_emb, gain)
    parts = [both] + [swap(both, k) for k in (1, 2, 3)]
    first_term = project((blk ^ 3)[None], mlp_act, w_down, width)
    arrived = [swap(first_term, 3)]
    parts = after(first_term, *parts)[1:]
    query_grad, low_own = group_part(
        parts, row_lse, positive, token_lengths, destination, features, blk
    )
    mlp_act = after(low_own, mlp_act)[1]
    for k in (1, 2):
        arrived.append(swap(project((blk ^ k)[None], mlp_act, w_down, width), k))
    own_term = project(blk[None], mlp_act, w_down, width, resid)

    low = lax.all_gather(low_own, "wide", axis=0, tiled=True)
    packed = pack(wide, destination, own_term, arrived, wide_count, slot_count)
    routed = [packed[k] if k == 0 else swap(packed[k], k, "wide") for k in range(wide_count)]
    low_act = low_activations(low, features, w_down, 0, 2)
    hot, share = slot_passages(wide, low, features, wide_count, slot_count, rows)
    low_act, hot, share, *routed = lax.optimization_barrier((low_act, hot, share, *routed))
    own = assemble(wide, routed)

    beside, above = swap(own, 1), swap(own, 2)
    totals = back(blk[None], [own], w_down, low)
    low_act = low_activations(low, features, w_down, 1, 2, [low_act])
    low_act, *totals, beside, above = lax.optimization_barrier((low_act, *totals, beside, above))
    top = swap(beside[: rows // 2], 2)
    bottom = swap(above[rows // 2 :], 1)
    totals = back(jnp.stack([blk ^ 1, blk ^ 2]), [beside, above], w_down, low, totals)
    act_grad, resid_grad, normed_out = finish(
        jnp.stack([blk ^ 3, blk]),
        [top, bottom],
        w_down,
        low,
        totals,
        hot,
        share,
        low_act,
        own,
        gain[None],
    )
    return (query_grad, resid_grad, act_grad, normed_out)


def coefficients(scores, lse_part, pos_part):
    columns = lax.broadcasted_iota(jnp.int32, scores.shape, 1)
    target = (pos_part[:, None] == columns).astype(jnp.float32)
    return (jnp.exp(scores - lse_part[:, None]) - target).astype(jnp.bfloat16)


def place_rows(destination, wide_count, slot_count):
    tok_count = destination.shape[0]
    dest_hot = (destination == lax.broadcasted_iota(jnp.int32, (tok_count, wide_count), 1)).astype(
        bf16
    )
    token = lax.iota(jnp.int32, tok_count)
    earlier = (token[None, :] < token[:, None]).astype(bf16)
    rank_of = jnp.dot(earlier, dest_hot, preferred_element_type=f32)
    slot_of = jnp.sum(rank_of * dest_hot.astype(f32), axis=1).astype(jnp.int32)
    slot_of = slot_of + destination[:, 0] * slot_count
    return (
        lax.broadcasted_iota(jnp.int32, (wide_count * slot_count, tok_count), 0) == slot_of[None, :]
    ).astype(bf16)


def row_shards(
    query_emb,
    passage_emb,
    row_lse,
    positive,
    token_lengths,
    destination,
    mlp_act,
    resid,
    w_down,
    gain,
):
    pair_rows = query_emb.shape[0]
    tok_count, feat_width = resid.shape
    features = w_down.shape[1]
    blk_index = lax.axis_index("blk")
    wide_count = lax.axis_size("wide")
    slot_count = 3 * tok_count // (2 * wide_count)
    offset = blk_index * feat_width
    query_all = lax.all_gather(query_emb, "blk", axis=0, tiled=True)
    passage_all = lax.all_gather(passage_emb, "blk", axis=0, tiled=True)
    scores = logit_scale * jnp.dot(query_all, passage_all.T, preferred_element_type=f32)
    coef_full = coefficients(scores, row_lse, positive)
    own_coef = lax.dynamic_slice_in_dim(coef_full, blk_index * pair_rows, pair_rows, 0)
    query_grad = (
        logit_scale * jnp.dot(own_coef, passage_all, preferred_element_type=f32)
    ).astype(bf16)
    query_cols = lax.dynamic_slice_in_dim(query_all, offset, feat_width, 1)
    grad_cols = logit_scale * lax.dot_general(
        query_cols, coef_full, (((0,), (0,)), ((), ())), preferred_element_type=f32
    )
    lengths_row = token_lengths[0]
    starts = jnp.cumsum(lengths_row) - lengths_row
    positions = lax.broadcasted_iota(jnp.int32, (tok_count, lengths_row.shape[0]), 0)
    member = (positions >= starts[None, :]) & (positions < (starts + lengths_row)[None, :])
    weights = member.astype(f32) * (1.0 / lengths_row.astype(f32))[None, :]
    tok_grad = lax.dot_general(
        weights,
        grad_cols,
        (((1,), (1,)), ((), ())),
        precision=lax.Precision.HIGHEST,
        preferred_element_type=f32,
    ).astype(bf16)
    terms = jnp.dot(mlp_act, w_down, preferred_element_type=f32)
    own = lax.dynamic_slice_in_dim(terms, offset, feat_width, 1) + resid.astype(f32)
    terms = lax.dynamic_update_slice_in_dim(terms, own, offset, 1)
    hidden = lax.psum_scatter(terms.astype(bf16), "blk", scatter_dimension=1, tiled=True)
    placer = place_rows(destination, wide_count, slot_count)
    payload = jnp.concatenate([hidden, tok_grad], axis=1)
    packed = jnp.dot(placer, payload, preferred_element_type=f32).astype(bf16)
    packed = packed.reshape(wide_count, slot_count, 2 * feat_width)
    rows = lax.all_to_all(packed, "wide", split_axis=0, concat_axis=0, tiled=True).reshape(
        wide_count * slot_count, 2 * feat_width
    )
    hidden = rows[:, :feat_width].astype(f32)
    gained = gain[None, :] * rows[:, feat_width:].astype(f32)
    squares, inner_sum = lax.psum(
        (jnp.sum(hidden * hidden, axis=1), jnp.sum(gained * hidden, axis=1)), "blk"
    )
    inv_rms = lax.rsqrt(squares / features + norm_eps)[:, None]
    normed = (gain[None, :] * hidden * inv_rms).astype(bf16)
    resid_back = (
        inv_rms * gained - hidden * (inv_rms * inv_rms * inv_rms) * inner_sum[:, None] / features
    ).astype(bf16)
    act_back = dot_t(lax.all_gather(resid_back, "blk", axis=1, tiled=True), w_down)
    return (query_grad, resid_back, act_back.astype(bf16), normed)


def solution(mesh):
    blk_count, wide_count = mesh.shape["blk"], mesh.shape["wide"]

    def shards(*operands):
        pairs, tok_count = operands[2].shape[0], operands[7].shape[0]
        low_rank = 2 * wide_count * pairs <= 3 * tok_count
        per_pair = tok_count // pairs
        aligned = operands[9].shape[0] % (lane * operands[0].shape[0]) == 0 and wide_count <= lane
        if low_rank and blk_count == 4 and aligned and per_pair * pairs == tok_count and wide_count & (wide_count - 1) == 0:
            return low_rank_shards(*operands)
        return row_shards(*operands)

    return jax.shard_map(
        shards,
        mesh=mesh,
        in_specs=(
            P(("wide", "blk"), None),
            P(("wide", "blk"), None),
            P("wide"),
            P("wide"),
            P("wide", None),
            P("wide", None),
            P("wide", "blk"),
            P("wide", "blk"),
            P("blk", None),
            P("blk"),
        ),
        out_specs=(P(("wide", "blk"), None), P("wide", "blk"), P("wide", "blk"), P("wide", "blk")),
        check_vma=False,
    )
```

```python
import jax
import jax.numpy as jnp
from jax import lax
from jax.experimental import pallas as pl
from jax.experimental.pallas import tpu as pltpu
from jax.sharding import PartitionSpec as P

logit_scale = 24.0
norm_eps = 1e-06
f32 = jnp.float32
bf16 = jnp.bfloat16
i32 = jnp.int32
lane = 128
kernel_vmem = 46 * 1024 * 1024
whole_vmem = 60 * 1024 * 1024


def params(vmem=kernel_vmem):
    return pltpu.CompilerParams(vmem_limit_bytes=vmem)


def cost(flops, nbytes):
    return pl.CostEstimate(flops=flops, bytes_accessed=nbytes, transcendentals=0)


def tile_of(extent, most):
    tile = most
    while extent % tile:
        tile //= 2
    return tile


def iota(shape, dim):
    return lax.broadcasted_iota(i32, shape, dim)


def dot(left, right):
    return jnp.dot(left, right, preferred_element_type=f32)


def dot_t(left, right):
    return lax.dot_general(left, right, (((1,), (1,)), ((), ())), preferred_element_type=f32)


def swap(rows, k, axis="blk"):
    return lax.ppermute(rows, axis, [(i, i ^ k) for i in range(lax.axis_size(axis))])


def after(first, *later):
    return lax.optimization_barrier((first, *later))


def project_body(has_resid, group_ref, act_hbm, w_hbm, *refs):
    out_ref, act, weights, act_sem, sems = refs[has_resid:]
    width = out_ref.shape[1]
    count, _, tile = weights.shape
    first = group_ref[0] * width

    def weight_copy(i):
        columns = pl.ds(pl.multiple_of(first + i * tile, lane), tile)
        return pltpu.make_async_copy(w_hbm.at[:, columns], weights.at[i], sems.at[i])

    act_copy = pltpu.make_async_copy(act_hbm, act, act_sem)
    act_copy.start()
    for i in range(count):
        weight_copy(i).start()
    act_copy.wait()

    @pl.loop(0, count)
    def _(i):
        weight_copy(i).wait()
        columns = pl.ds(pl.multiple_of(i * tile, lane), tile)
        term = dot(act[...], weights[i])
        if has_resid:
            term = term + refs[0][:, columns].astype(f32)
        out_ref[:, columns] = term.astype(out_ref.dtype)


def project(group, act, w_down, width, resid=None):
    rows, depth = act.shape
    tile = tile_of(width, 256)
    count = width // tile
    own = [] if resid is None else [resid]
    return pl.pallas_call(
        lambda *refs: project_body(len(own), *refs),
        in_specs=[pl.BlockSpec(memory_space=pltpu.SMEM)]
        + [pl.BlockSpec(memory_space=pl.ANY)] * 2
        + [pl.BlockSpec(memory_space=pltpu.VMEM)] * len(own),
        out_specs=pl.BlockSpec(memory_space=pltpu.VMEM),
        out_shape=jax.ShapeDtypeStruct((rows, width), f32 if own else bf16),
        scratch_shapes=[
            pltpu.VMEM((rows, depth), bf16),
            pltpu.VMEM((count, depth, tile), bf16),
            pltpu.SemaphoreType.DMA,
            pltpu.SemaphoreType.DMA((count,)),
        ],
        compiler_params=params(),
        cost_estimate=cost(2 * rows * depth * width, 2 * depth * width + 2 * rows * depth),
    )(group, act, w_down, *own)


def payload_body(query_ref, passage_ref, gain_ref, out_ref, gains):
    own, features = query_ref.shape
    piece = gains.shape[1]
    for row in range(own):
        gains[row : row + 1] = gain_ref[:, row * piece : (row + 1) * piece]
    gain = gains[...]
    high = gain.astype(bf16)
    out_ref[:, :features] = query_ref[...]
    out_ref[:, features : 2 * features] = passage_ref[...]
    out_ref[:, 2 * features : 2 * features + piece] = high
    out_ref[:, 2 * features + piece :] = (gain - high.astype(f32)).astype(bf16)


def payload(query_emb, passage_emb, gain):
    own, features = query_emb.shape
    piece = gain.shape[0] // own
    return pl.pallas_call(
        payload_body,
        out_shape=jax.ShapeDtypeStruct((own, 2 * features + 2 * piece), bf16),
        scratch_shapes=[pltpu.VMEM((own, piece), f32)],
        compiler_params=params(whole_vmem),
        cost_estimate=cost(own * features, 8 * own * features),
    )(query_emb, passage_emb, gain[None])


def group_body(count, blk_ref, *refs):
    parts, refs = refs[:count], refs[count:]
    lse_ref, pos_ref, dest_ref, len_ref = refs[:4]
    query_grad_ref, low_ref, query_all, passage_all, gain_all = refs[4:]
    own, features = query_grad_ref.shape
    pairs = own * count
    piece = features // pairs
    blk = blk_ref[0]
    for k in range(count):
        query_all[k * own : (k + 1) * own] = parts[k][:, :features].astype(f32)
        passage_all[k * own : (k + 1) * own] = parts[k][:, features : 2 * features].astype(f32)
        gains = parts[k][:, 2 * features : 2 * features + piece].astype(f32)
        gains = gains + parts[k][:, 2 * features + piece :].astype(f32)
        for row in range(own):
            first = pl.multiple_of(((blk ^ k) * own + row) * piece, lane)
            gain_all[:, pl.ds(first, piece)] = gains[row : row + 1]
    queries = query_all[...].astype(bf16)
    passages = passage_all[...].astype(bf16)

    def named(dim):
        place = iota((pairs, pairs), dim)
        return (blk ^ (place // own)) * own + place % own

    here_rows, here_cols = named(0), named(1)
    at_rows = here_rows == iota((pairs, pairs), 1)
    at_cols = here_cols == iota((pairs, pairs), 0)
    lse = jnp.sum(jnp.where(at_rows, lse_ref[...], 0.0), axis=1, keepdims=True)
    pos = jnp.sum(jnp.where(at_rows, pos_ref[...], 0), axis=1, keepdims=True)
    hit = (pos == here_cols).astype(f32)
    coef = (jnp.exp(logit_scale * dot_t(queries, passages) - lse) - hit).astype(bf16)
    query_grad_ref[...] = (logit_scale * dot(coef, passages))[:own].astype(bf16)
    same = iota((pairs, pairs), 0) == iota((pairs, pairs), 1)
    lse = jnp.sum(jnp.where(same, lse, 0.0), axis=0, keepdims=True)
    pos = jnp.sum(jnp.where(same, pos, 0), axis=0, keepdims=True)
    hit = (pos == here_rows).astype(f32)
    turned = (jnp.exp(logit_scale * dot_t(passages, queries) - lse) - hit).astype(bf16)
    turned = dot(at_cols.astype(f32).astype(bf16), turned).astype(bf16)
    pass_grad = logit_scale * dot(turned, queries)
    low_ref[:, :features] = (gain_all[...] * pass_grad).astype(bf16)
    row = iota((pairs, lane), 0)
    tokens = dest_ref.shape[1]
    table = jnp.zeros((pairs, lane), f32)
    for n in range(-(-tokens // lane)):
        some = dest_ref[:, n * lane : min(tokens, (n + 1) * lane)].astype(f32)
        table = jnp.where(row == n, widen(some), table)
    table = jnp.where(row == -(-tokens // lane), widen(len_ref[...].astype(f32)), table)
    low_ref[:, features:] = table.astype(bf16)


def widen(row):
    short = lane - row.shape[1]
    return jnp.concatenate([row, jnp.zeros((1, short), f32)], axis=1) if short else row


def group_part(parts, row_lse, positive, token_lengths, destination, features, blk):
    own = parts[0].shape[0]
    pairs = row_lse.shape[0]
    return pl.pallas_call(
        lambda *refs: group_body(pairs // own, *refs),
        in_specs=[pl.BlockSpec(memory_space=pltpu.SMEM)]
        + [pl.BlockSpec(memory_space=pltpu.VMEM)] * (len(parts) + 4),
        out_specs=[pl.BlockSpec(memory_space=pltpu.VMEM)] * 2,
        out_shape=[
            jax.ShapeDtypeStruct((own, features), bf16),
            jax.ShapeDtypeStruct((pairs, features + lane), bf16),
        ],
        scratch_shapes=[
            pltpu.VMEM((pairs, features), f32),
            pltpu.VMEM((pairs, features), f32),
            pltpu.VMEM((1, features), f32),
        ],
        compiler_params=params(),
        cost_estimate=cost(8 * pairs * pairs * features, 8 * pairs * features),
    )(
        blk[None],
        *parts,
        row_lse[None],
        positive[None],
        destination.reshape(1, -1),
        token_lengths,
    )


def earlier_of(tokens):
    return (iota((tokens, tokens), 0) < iota((tokens, tokens), 1)).astype(bf16)


def pack_body(terms, wide_ref, dest_ref, own_ref, *rest):
    outs = rest[terms:]
    groups, slots = len(outs), outs[0].shape[0]
    tokens = dest_ref.shape[1]
    stride = -(-slots // 16) * 16
    hidden = own_ref[...]
    for term in rest[:terms]:
        hidden = hidden + term[...].astype(f32)
    partner = dest_ref[...] ^ wide_ref[0]
    hit = (partner == iota((groups, tokens), 0)).astype(f32)
    rank = dot(hit.astype(bf16), earlier_of(tokens))
    rank = jnp.sum(rank * hit, axis=0, keepdims=True).astype(i32)
    place = iota((groups * stride, tokens), 0) == partner * stride + rank
    packed = dot(place.astype(f32).astype(bf16), hidden.astype(bf16)).astype(bf16)
    for k in range(groups):
        outs[k][...] = packed[k * stride : k * stride + slots]


def pack(wide, destination, own, terms, groups, slots):
    tokens, width = own.shape
    tile = tile_of(width, 512)
    column_spec = pl.BlockSpec((tokens, tile), lambda j, g: (0, j))
    return pl.pallas_call(
        lambda *refs: pack_body(len(terms), *refs),
        grid_spec=pltpu.PrefetchScalarGridSpec(
            num_scalar_prefetch=1,
            grid=(width // tile,),
            in_specs=[pl.BlockSpec((1, tokens), lambda j, g: (0, 0))]
            + [column_spec] * (1 + len(terms)),
            out_specs=[pl.BlockSpec((slots, tile), lambda j, g: (0, j))] * groups,
        ),
        out_shape=[jax.ShapeDtypeStruct((slots, width), bf16)] * groups,
        compiler_params=params(),
        cost_estimate=cost(4 * groups * slots * tokens * width, 10 * tokens * width),
    )(wide[None], destination.reshape(1, tokens), own, *terms)


def assemble_body(wide_ref, *refs):
    parts, out_ref = refs[:-1], refs[-1]
    slots = parts[0].shape[0]
    rows = out_ref.shape[0]
    row, column = iota((rows, slots), 0), iota((rows, slots), 1)
    total = 0.0
    for k, part in enumerate(parts):
        group = wide_ref[0] ^ k
        place = (row == group * slots + column).astype(f32).astype(bf16)
        total = total + dot(place, part[...])
    out_ref[...] = total.astype(bf16)


def assemble(wide, parts):
    slots, width = parts[0].shape
    rows = slots * len(parts)
    return pl.pallas_call(
        assemble_body,
        in_specs=[pl.BlockSpec(memory_space=pltpu.SMEM)]
        + [pl.BlockSpec(memory_space=pltpu.VMEM)] * len(parts),
        out_specs=pl.BlockSpec(memory_space=pltpu.VMEM),
        out_shape=jax.ShapeDtypeStruct((rows, width), bf16),
        compiler_params=params(),
        cost_estimate=cost(2 * rows * rows * width, 4 * rows * width),
    )(wide[None], *parts)


def slots_body(groups, slots, wide_ref, table_ref, hot_ref, share_ref):
    rows, columns = hot_ref.shape
    pairs = columns // groups
    blocks = -(-slots * groups * 2 // 3 // lane)
    table = table_ref[...]

    def tables(n):
        at = iota((groups, columns), 1) == iota((groups, columns), 0) * pairs + n
        return dot(at.astype(f32).astype(bf16), table)

    spread = (iota((rows, groups), 0) // slots == iota((rows, groups), 1)).astype(f32).astype(bf16)
    lengths = tables(blocks)
    upto = (iota((lane, lane), 0) <= iota((lane, lane), 1)).astype(f32).astype(bf16)
    ends = dot(lengths.astype(bf16), upto)
    slot = iota((rows, lane), 0) % slots
    before = jnp.zeros((groups, 1), f32)
    taken = jnp.zeros((rows, 1), f32)
    for n in range(blocks):
        token = iota((groups, lane), 1) + n * lane
        hit = (tables(n).astype(i32) == wide_ref[0]) & (token < slots * groups * 2 // 3)
        count = hit.astype(f32)
        rank = before + dot(count.astype(bf16), earlier_of(lane))
        before = before + jnp.sum(count, axis=1, keepdims=True)
        passage = jnp.ones((groups, lane), f32)
        for pair in range(pairs):
            passage = passage + (token.astype(f32) >= ends[:, pair : pair + 1]).astype(f32)
        code = jnp.where(hit, passage, 0.0)
        rank_rows = dot(spread, rank.astype(bf16)).astype(i32)
        code_rows = dot(spread, code.astype(bf16))
        taken = taken + jnp.sum(
            jnp.where(rank_rows == slot, code_rows, 0.0), axis=1, keepdims=True
        )
    taken = taken.astype(i32)
    column = iota((rows, columns), 1)
    first = iota((rows, columns), 0) // slots * pairs
    hot = (taken > 0) & (column == first + taken - 1)
    hot_ref[...] = hot.astype(f32).astype(bf16)
    length_rows = dot(spread, lengths.astype(bf16))
    length = jnp.where(iota((rows, lane), 1) == taken - 1, length_rows, 0.0)
    length = jnp.sum(length, axis=1, keepdims=True)
    share_ref[...] = jnp.where(taken > 0, 1.0 / jnp.maximum(length, 1.0), 0.0)


def slot_passages(wide, low, features, groups, slots, rows):
    columns = low.shape[0]
    return pl.pallas_call(
        lambda *refs: slots_body(groups, slots, *refs),
        grid=(1,),
        in_specs=[
            pl.BlockSpec(memory_space=pltpu.SMEM),
            pl.BlockSpec((columns, lane), lambda j: (0, features // lane)),
        ],
        out_specs=[
            pl.BlockSpec((rows, columns), lambda j: (0, 0)),
            pl.BlockSpec((rows, 1), lambda j: (0, 0)),
        ],
        out_shape=[
            jax.ShapeDtypeStruct((rows, columns), bf16),
            jax.ShapeDtypeStruct((rows, 1), f32),
        ],
        compiler_params=params(),
        cost_estimate=cost(4 * rows * groups * lane, 2 * rows * columns),
    )(wide[None], low)


def low_act_body(part, low_ref, w_hbm, *refs):
    out_ref, weights, sems = refs[-3:]
    count, tile, _ = weights.shape

    def weight_copy(t):
        rows = pl.ds(pl.multiple_of((part * count + t) * tile, tile), tile)
        return pltpu.make_async_copy(w_hbm.at[rows], weights.at[t], sems.at[t])

    for t in range(count):
        weight_copy(t).start()

    @pl.loop(0, count)
    def _(t):
        weight_copy(t).wait()
        rows = pl.ds(pl.multiple_of(t * tile, tile), tile)
        out_ref[rows] = dot_t(weights[t], low_ref[...]).astype(bf16)


def low_activations(low, features, w_down, part, parts, filled=()):
    pairs = low.shape[0]
    depth = w_down.shape[0]
    some = depth // parts
    tile = tile_of(some, 512)
    count = some // tile
    anywhere = pl.BlockSpec(memory_space=pl.ANY)
    return pl.pallas_call(
        lambda *refs: low_act_body(part, *refs),
        grid=(1,),
        in_specs=[pl.BlockSpec((pairs, features), lambda j: (0, 0)), anywhere]
        + [anywhere] * len(filled),
        out_specs=pl.BlockSpec((some, pairs), lambda j: (part, 0)),
        out_shape=jax.ShapeDtypeStruct((depth, pairs), bf16),
        scratch_shapes=[
            pltpu.VMEM((count, tile, features), bf16),
            pltpu.SemaphoreType.DMA((count,)),
        ],
        input_output_aliases={2: 0} if filled else {},
        compiler_params=params(),
        cost_estimate=cost(2 * pairs * some * features, 2 * some * features),
    )(low, w_down, *filled)


def statistics(hids, lows):
    squares, cross = 0.0, 0.0
    for hid_ref, low_ref in zip(hids, lows):
        hid = hid_ref[...].astype(f32)
        squares = squares + jnp.sum(hid * hid, axis=1, keepdims=True)
        cross = cross + dot_t(hid_ref[...], low_ref[...])
    return squares, cross


def product(hids, weights):
    total = 0.0
    for hid_ref, w_ref in zip(hids, weights):
        total = total + dot_t(hid_ref[...], w_ref[...])
    return total


def weight_specs(count, tile, width):
    return [
        pl.BlockSpec((tile // 2, width), lambda j, g, n=n, side=side: (2 * j + side, g[n]))
        for n in range(count)
        for side in range(2)
    ]


def low_specs(count, pairs, width):
    return [pl.BlockSpec((pairs, width), lambda j, g, n=n: (0, g[n])) for n in range(count)]


def back_body(count, carried, places_ref, *refs):
    hids, weights, refs = refs[:count], refs[count : 3 * count], refs[3 * count :]
    lows, before, (acc_ref, squares_ref, cross_ref) = refs[:count], refs[count:-3], refs[-3:]

    @pl.when(pl.program_id(0) == 0)
    def _():
        squares, cross = statistics(hids, lows)
        if carried:
            squares, cross = before[1][...] + squares, before[2][...] + cross
        squares_ref[...], cross_ref[...] = squares, cross

    half = acc_ref.shape[1] // 2
    for side in range(2):
        at = slice(side * half, (side + 1) * half)
        total = product(hids, weights[side::2])
        if carried:
            total = total + before[0][:, at].astype(f32)
        acc_ref[:, at] = total.astype(bf16)


def carried_specs(rows, pairs, tile):
    return [
        pl.BlockSpec((rows, tile), lambda j, g: (0, j)),
        pl.BlockSpec((rows, 1), lambda j, g: (0, 0)),
        pl.BlockSpec((rows, pairs), lambda j, g: (0, 0)),
    ]


def back(places, pieces, w_down, low, before=()):
    count = len(pieces)
    rows, width = pieces[0].shape
    depth = w_down.shape[0]
    pairs = low.shape[0]
    tile = tile_of(depth, 1024)
    totals = carried_specs(rows, pairs, tile)
    return pl.pallas_call(
        lambda *refs: back_body(count, len(before), *refs),
        grid_spec=pltpu.PrefetchScalarGridSpec(
            num_scalar_prefetch=1,
            grid=(depth // tile,),
            in_specs=[pl.BlockSpec((rows, width), lambda j, g: (0, 0))] * count
            + weight_specs(count, tile, width)
            + low_specs(count, pairs, width)
            + totals[: len(before)],
            out_specs=totals,
        ),
        out_shape=[
            jax.ShapeDtypeStruct((rows, depth), bf16),
            jax.ShapeDtypeStruct((rows, 1), f32),
            jax.ShapeDtypeStruct((rows, pairs), f32),
        ],
        compiler_params=params(),
        cost_estimate=cost(2 * rows * depth * width * count, 2 * depth * width * count),
    )(places, *pieces, *[w_down] * 2 * count, *[low] * count, *before)


def finish_body(features, count, places_ref, *refs):
    hids, weights, refs = refs[:count], refs[count : count + 2], refs[count + 2 :]
    low_ref, acc_ref, squares_ref, cross_ref, hot_ref, share_ref, low_act_ref = refs[:7]
    own_ref, own_low_ref, gain_ref, act_out, resid_out, normed_out = refs[7:13]
    hid, lead, pull, scale = refs[13:]
    part = hids[0].shape[0]
    step = own_ref.shape[0]

    @pl.when(pl.program_id(0) == 0)
    def _():
        for n in range(count):
            hid[n * part : (n + 1) * part] = hids[n][...]
        squares, cross = statistics([hid], [low_ref])
        hot = hot_ref[...].astype(f32)
        inner = jnp.sum((cross_ref[...] + cross) * hot, axis=1, keepdims=True) * share_ref[...]
        inv_rms = lax.rsqrt((squares_ref[...] + squares) / features + norm_eps)
        scale[...] = inv_rms
        lead[...] = inv_rms * share_ref[...]
        pull[...] = inv_rms * inv_rms * inv_rms * inner / features

    half = act_out.shape[1] // 2
    for side in range(2):
        at = slice(side * half, (side + 1) * half)
        low_act = dot_t(hot_ref[...], low_act_ref[at])
        hid_act = acc_ref[:, at].astype(f32) + product([hid], weights[side : side + 1])
        act_out[:, at] = (lead[...] * low_act - pull[...] * hid_act).astype(bf16)
    rows = pl.ds(pl.multiple_of(pl.program_id(0) * step, step), step)
    own = own_ref[...].astype(f32)
    own_low = dot(hot_ref[rows], own_low_ref[...])
    resid_out[...] = (lead[rows] * own_low - own * pull[rows]).astype(bf16)
    normed_out[...] = (gain_ref[...] * own * scale[rows]).astype(bf16)


def finish(places, pieces, w_down, low, before, hot, share, low_act, own, gain):
    count = len(pieces)
    rows, width = own.shape
    depth, features = w_down.shape
    pairs = hot.shape[1]
    tile = tile_of(depth, 1024)
    steps = depth // tile
    step = rows // steps

    def whole(shape):
        return pl.BlockSpec(shape, lambda j, g: (0, 0))

    row_spec = pl.BlockSpec((step, width), lambda j, g: (j, 0))
    return pl.pallas_call(
        lambda *refs: finish_body(features, count, *refs),
        grid_spec=pltpu.PrefetchScalarGridSpec(
            num_scalar_prefetch=1,
            grid=(steps,),
            in_specs=[whole((rows // count, width))] * count
            + weight_specs(1, tile, width)
            + low_specs(1, pairs, width)
            + carried_specs(rows, pairs, tile)
            + [
                whole((rows, pairs)),
                whole((rows, 1)),
                pl.BlockSpec((tile, pairs), lambda j, g: (j, 0)),
                row_spec,
                pl.BlockSpec((pairs, width), lambda j, g: (0, g[1])),
                whole((1, width)),
            ],
            out_specs=[pl.BlockSpec((rows, tile), lambda j, g: (0, j)), row_spec, row_spec],
            scratch_shapes=[pltpu.VMEM((rows, width), bf16)] + [pltpu.VMEM((rows, 1), f32)] * 3,
        ),
        out_shape=[
            jax.ShapeDtypeStruct((rows, depth), bf16),
            jax.ShapeDtypeStruct((rows, width), bf16),
            jax.ShapeDtypeStruct((rows, width), bf16),
        ],
        compiler_params=params(),
        cost_estimate=cost(2 * rows * depth * width, 2 * depth * width + 6 * rows * depth),
    )(
        places,
        *pieces,
        *[w_down] * 2,
        low,
        *before,
        hot,
        share,
        low_act,
        own,
        low,
        gain,
    )


def low_rank_shards(
    query_emb,
    passage_emb,
    row_lse,
    positive,
    token_lengths,
    destination,
    mlp_act,
    resid,
    w_down,
    gain,
):
    wide_count = lax.axis_size("wide")
    blk, wide = lax.axis_index("blk"), lax.axis_index("wide")
    tok_count, width = resid.shape
    features = w_down.shape[1]
    pairs = row_lse.shape[0]
    slot_count = 3 * tok_count // (2 * wide_count)
    rows = wide_count * slot_count

    both = payload(query_emb, passage_emb, gain)
    parts = [both] + [swap(both, k) for k in (1, 2, 3)]
    first_term = project((blk ^ 3)[None], mlp_act, w_down, width)
    arrived = [swap(first_term, 3)]
    parts = after(first_term, *parts)[1:]
    query_grad, low_own = group_part(
        parts, row_lse, positive, token_lengths, destination, features, blk
    )
    mlp_act = after(low_own, mlp_act)[1]
    for k in (1, 2):
        arrived.append(swap(project((blk ^ k)[None], mlp_act, w_down, width), k))
    own_term = project(blk[None], mlp_act, w_down, width, resid)

    low = lax.all_gather(low_own, "wide", axis=0, tiled=True)
    packed = pack(wide, destination, own_term, arrived, wide_count, slot_count)
    routed = [packed[k] if k == 0 else swap(packed[k], k, "wide") for k in range(wide_count)]
    low_act = low_activations(low, features, w_down, 0, 2)
    hot, share = slot_passages(wide, low, features, wide_count, slot_count, rows)
    low_act, hot, share, *routed = lax.optimization_barrier((low_act, hot, share, *routed))
    own = assemble(wide, routed)

    beside, above = swap(own, 1), swap(own, 2)
    totals = back(blk[None], [own], w_down, low)
    low_act = low_activations(low, features, w_down, 1, 2, [low_act])
    low_act, *totals, beside, above = lax.optimization_barrier((low_act, *totals, beside, above))
    top = swap(beside[: rows // 2], 2)
    bottom = swap(above[rows // 2 :], 1)
    totals = back(jnp.stack([blk ^ 1, blk ^ 2]), [beside, above], w_down, low, totals)
    act_grad, resid_grad, normed_out = finish(
        jnp.stack([blk ^ 3, blk]),
        [top, bottom],
        w_down,
        low,
        totals,
        hot,
        share,
        low_act,
        own,
        gain[None],
    )
    return (query_grad, resid_grad, act_grad, normed_out)


def coefficients(scores, lse_part, pos_part):
    columns = lax.broadcasted_iota(jnp.int32, scores.shape, 1)
    target = (pos_part[:, None] == columns).astype(jnp.float32)
    return (jnp.exp(scores - lse_part[:, None]) - target).astype(jnp.bfloat16)


def place_rows(destination, wide_count, slot_count):
    tok_count = destination.shape[0]
    dest_hot = (destination == lax.broadcasted_iota(jnp.int32, (tok_count, wide_count), 1)).astype(
        bf16
    )
    token = lax.iota(jnp.int32, tok_count)
    earlier = (token[None, :] < token[:, None]).astype(bf16)
    rank_of = jnp.dot(earlier, dest_hot, preferred_element_type=f32)
    slot_of = jnp.sum(rank_of * dest_hot.astype(f32), axis=1).astype(jnp.int32)
    slot_of = slot_of + destination[:, 0] * slot_count
    return (
        lax.broadcasted_iota(jnp.int32, (wide_count * slot_count, tok_count), 0) == slot_of[None, :]
    ).astype(bf16)


def row_shards(
    query_emb,
    passage_emb,
    row_lse,
    positive,
    token_lengths,
    destination,
    mlp_act,
    resid,
    w_down,
    gain,
):
    pair_rows = query_emb.shape[0]
    tok_count, feat_width = resid.shape
    features = w_down.shape[1]
    blk_index = lax.axis_index("blk")
    wide_count = lax.axis_size("wide")
    slot_count = 3 * tok_count // (2 * wide_count)
    offset = blk_index * feat_width
    query_all = lax.all_gather(query_emb, "blk", axis=0, tiled=True)
    passage_all = lax.all_gather(passage_emb, "blk", axis=0, tiled=True)
    scores = logit_scale * jnp.dot(query_all, passage_all.T, preferred_element_type=f32)
    coef_full = coefficients(scores, row_lse, positive)
    own_coef = lax.dynamic_slice_in_dim(coef_full, blk_index * pair_rows, pair_rows, 0)
    query_grad = (
        logit_scale * jnp.dot(own_coef, passage_all, preferred_element_type=f32)
    ).astype(bf16)
    query_cols = lax.dynamic_slice_in_dim(query_all, offset, feat_width, 1)
    grad_cols = logit_scale * lax.dot_general(
        query_cols, coef_full, (((0,), (0,)), ((), ())), preferred_element_type=f32
    )
    lengths_row = token_lengths[0]
    starts = jnp.cumsum(lengths_row) - lengths_row
    positions = lax.broadcasted_iota(jnp.int32, (tok_count, lengths_row.shape[0]), 0)
    member = (positions >= starts[None, :]) & (positions < (starts + lengths_row)[None, :])
    weights = member.astype(f32) * (1.0 / lengths_row.astype(f32))[None, :]
    tok_grad = lax.dot_general(
        weights,
        grad_cols,
        (((1,), (1,)), ((), ())),
        precision=lax.Precision.HIGHEST,
        preferred_element_type=f32,
    ).astype(bf16)
    terms = jnp.dot(mlp_act, w_down, preferred_element_type=f32)
    own = lax.dynamic_slice_in_dim(terms, offset, feat_width, 1) + resid.astype(f32)
    terms = lax.dynamic_update_slice_in_dim(terms, own, offset, 1)
    hidden = lax.psum_scatter(terms.astype(bf16), "blk", scatter_dimension=1, tiled=True)
    placer = place_rows(destination, wide_count, slot_count)
    payload = jnp.concatenate([hidden, tok_grad], axis=1)
    packed = jnp.dot(placer, payload, preferred_element_type=f32).astype(bf16)
    packed = packed.reshape(wide_count, slot_count, 2 * feat_width)
    rows = lax.all_to_all(packed, "wide", split_axis=0, concat_axis=0, tiled=True).reshape(
        wide_count * slot_count, 2 * feat_width
    )
    hidden = rows[:, :feat_width].astype(f32)
    gained = gain[None, :] * rows[:, feat_width:].astype(f32)
    squares, inner_sum = lax.psum(
        (jnp.sum(hidden * hidden, axis=1), jnp.sum(gained * hidden, axis=1)), "blk"
    )
    inv_rms = lax.rsqrt(squares / features + norm_eps)[:, None]
    normed = (gain[None, :] * hidden * inv_rms).astype(bf16)
    resid_back = (
        inv_rms * gained - hidden * (inv_rms * inv_rms * inv_rms) * inner_sum[:, None] / features
    ).astype(bf16)
    act_back = dot_t(lax.all_gather(resid_back, "blk", axis=1, tiled=True), w_down)
    return (query_grad, resid_back, act_back.astype(bf16), normed)


def solution(mesh):
    blk_count, wide_count = mesh.shape["blk"], mesh.shape["wide"]

    def shards(*operands):
        pairs, tok_count = operands[2].shape[0], operands[7].shape[0]
        low_rank = 2 * wide_count * pairs <= 3 * tok_count
        per_pair = tok_count // pairs
        aligned = operands[9].shape[0] % (lane * operands[0].shape[0]) == 0 and wide_count <= lane
        if low_rank and blk_count == 4 and aligned and per_pair * pairs == tok_count and wide_count & (wide_count - 1) == 0:
            return low_rank_shards(*operands)
        return row_shards(*operands)

    return jax.shard_map(
        shards,
        mesh=mesh,
        in_specs=(
            P(("wide", "blk"), None),
            P(("wide", "blk"), None),
            P("wide"),
            P("wide"),
            P("wide", None),
            P("wide", None),
            P("wide", "blk"),
            P("wide", "blk"),
            P("blk", None),
            P("blk"),
        ),
        out_specs=(P(("wide", "blk"), None), P("wide", "blk"), P("wide", "blk"), P("wide", "blk")),
        check_vma=False,
    )
```
